32 devices in a mesh: row: 8 (over z, x), col: 2 (over core), rep: 2 (over y).
Axes of the slice: x: 2, y: 2, z: 4, core: 2. Of those that a mesh axis runs over, the one named last changes fastest.
Arguments:
- left_values: float32 [8, 2, 2, 3, 8, 2, 128, 128], P('row', 'rep', 'col'), may hold values from -0.5 to 0.5
- left_rows: int32 [8, 2, 2, 3, 8, 2], P('row', 'rep', 'col'), may hold values from 0 to 3, as said below
- right_values: float32 [2, 8, 2, 8, 4, 128, 128], P('rep', 'row', 'col'), may hold values from -1.5 to 1.5
- right_cols: int32 [2, 8, 2, 8, 4], P('rep', 'row', 'col'), may hold values from 0 to 7
- result_slots: int32 [8, 2, 24], P('row', 'col'), may hold values from 0 to 31, as said below
Outputs:
- result_blocks: float32 [8, 2, 24, 128, 128], P('row', 'col', 'rep')
The draws below stay inside these ranges and needn't reach their ends.
Inputs may be any that keep to these rules, and one draw needn't show every extreme that they name: `result_slots`: within one result tile the 24 slots are distinct; slot value p stands for the block at block row p // 8 and block column p % 8 of the tile. `left_rows`: the 2 block rows of one block column of a panel are distinct.
All inputs are finite; a program needn't handle non-finite values.
Results may differ from the reference program's by a relative error of at most 0.0003.
Values sent between devices are 32-bit elements; how exact they have to be, the bound alone decides.
No kernel may reach another device: no remote copies, remote signals or barrier semaphores. Data moves between devices by JAX's collectives and lax.ppermute only.
A program may use at most 64 MiB of HBM per device.

```python
import jax
import jax.numpy as jnp
from jax import lax

ROW_TILES = 8
COL_TILES = 2
LAYERS = 2
BS = 128
KB = 8
BPR = 4
LPB = 2
STEPS = 4
RB = 4
CB = 8
NC = 24
M_SLOTS = 3


def draw_result_slots(key, part):
    tile_keys = jax.random.split(key, ROW_TILES * COL_TILES)

    def pick_slots(tile_key):
        return jax.random.permutation(tile_key, RB * CB)[:NC].astype(jnp.int32)
    return jax.vmap(pick_slots)(tile_keys).reshape(ROW_TILES, COL_TILES, NC)


def draw_left_rows(key, part):
    count = ROW_TILES * LAYERS * COL_TILES * M_SLOTS * KB
    column_keys = jax.random.split(jax.random.fold_in(key, 7), count)

    def pick_rows(column_key):
        return jax.random.permutation(column_key, RB)[:LPB].astype(jnp.int32)
    return jax.vmap(pick_rows)(column_keys).reshape(ROW_TILES, LAYERS, COL_TILES, M_SLOTS, KB, LPB)


def set_ends(array, key, low, largest):
    shape = array.shape
    spot = [jax.random.randint(jax.random.fold_in(key, axis), (), 0, shape[axis]) for axis in range(len(shape))]
    array = array.at[tuple(spot)].set(low)
    longest = shape.index(max(shape))
    spot[longest] = (spot[longest] + 1) % shape[longest]
    return array.at[tuple(spot)].set(largest)


def steps_of(stream_key, extent, shards, smallest, largest):
    def one(dim, shards_of):
        draws = jax.random.uniform(jax.random.fold_in(jax.random.fold_in(stream_key, 6), dim), (shards_of,), jnp.float32, smallest / len(shards), largest / len(shards))
        return jnp.repeat(jnp.exp(draws), extent[dim] // shards_of).reshape((-1,) + (1,) * (len(extent) - dim - 1))

    gain = one(*shards[0])
    for cut in shards[1:]:
        gain = gain * one(*cut)
    return gain


def gaussian(key, dims, scale, bound, cuts=(), held_as=jnp.bfloat16):
    factor_of = steps_of(key, dims, cuts, -0.22, 0.18) if cuts else 1.0
    drawn = jax.random.normal(key, dims, jnp.float32) * scale * factor_of
    return jnp.minimum(jnp.maximum(drawn, -bound), bound).astype(held_as)


def setup_inputs(seed: int = 0) -> dict:
    keys = jax.random.split(jax.random.key(seed), 6)
    left_values = gaussian(keys[0], (ROW_TILES, LAYERS, COL_TILES, M_SLOTS, KB, LPB, BS, BS), BS ** -0.5, 0.5, ((0, 8), (1, 2), (2, 2)), jnp.float32)
    left_rows = draw_left_rows(jax.random.fold_in(keys[5], 71), 0)
    right_values = gaussian(keys[2], (LAYERS, ROW_TILES, COL_TILES, KB, BPR, BS, BS), (2 * STEPS * KB * LPB * BPR // (RB * CB)) ** -0.5, 1.5, ((0, 2), (1, 8), (2, 2)), jnp.float32)
    right_cols = set_ends(jax.random.randint(keys[3], (LAYERS, ROW_TILES, COL_TILES, KB, BPR), 0, CB), jax.random.fold_in(keys[3], 1), 0, CB - 1).astype(jnp.int32)
    result_slots = draw_result_slots(jax.random.fold_in(keys[5], 71), 0)
    return {"left_values": left_values, "left_rows": left_rows, "right_values": right_values, "right_cols": right_cols, "result_slots": result_slots}


highest = lax.Precision.HIGHEST


def turn_products(left_blocks, left_places, right_blocks, right_places, listed):
    products = jnp.einsum("kaxy,kbyz->kabxz", left_blocks, right_blocks, precision=highest)
    block_codes = left_places[:, :, None] * CB + right_places[:, None, :]
    onehot = (block_codes[:, :, :, None] == listed[None, None, None, :]).astype(jnp.float32)
    return jnp.einsum("kabc,kabxz->cxz", onehot, products, precision=highest)


def reference(left_values, left_rows, right_values, right_cols, result_slots):
    layer_ids = jnp.arange(LAYERS, dtype=jnp.int32)
    column_ids = jnp.arange(COL_TILES, dtype=jnp.int32)

    def one_tile(tile_row, layer_index, tile_col):
        totals = jnp.zeros((NC, BS, BS), jnp.float32)
        for turn_index in range(STEPS):
            source = (tile_col + turn_index) % COL_TILES
            slot_index = (tile_col + turn_index) // COL_TILES
            right_row = (tile_row + turn_index) % ROW_TILES
            totals = totals + turn_products(
                left_values[tile_row, layer_index, source, slot_index],
                left_rows[tile_row, layer_index, source, slot_index],
                right_values[layer_index, right_row, tile_col],
                right_cols[layer_index, right_row, tile_col],
                result_slots[tile_row, tile_col])
        return totals

    def one_row(tile_row):
        def per_layer(layer_index):
            def per_column(tile_col):
                return one_tile(tile_row, layer_index, tile_col)
            return jax.vmap(per_column)(column_ids)
        layered = jax.vmap(per_layer)(layer_ids)
        return jnp.sum(layered, axis=0)

    return lax.map(one_row, jnp.arange(ROW_TILES, dtype=jnp.int32))
```

```python
import functools

import jax
import jax.numpy as jnp
from jax import lax
from jax.experimental import pallas as pl
from jax.experimental.pallas import tpu as pltpu
from jax.sharding import PartitionSpec as P

STEPS = 4
CB = 8
QUARTERS = 4

bf16 = jnp.bfloat16
f32 = jnp.float32

Z_EVEN = ((1, 2, 0), (1, 2, 1), (1, 2, 2), (1, 2, 3), (1, 3, 0), (0, 0, 0), (0, 0, 0))
Z_ODD = ((1, 2, 1), (1, 2, 2), (1, 2, 3), (1, 3, 0), (1, 3, 1), (1, 3, 2), (1, 3, 3))
X_EVEN = ((1, 1, 0), (1, 1, 1), (1, 1, 2), (1, 1, 3), (1, 3, 1), (1, 3, 2), (1, 3, 3))
X_ODD = ((0, 0, 0), (0, 0, 0), (1, 1, 0), (1, 1, 1), (1, 1, 2), (1, 1, 3), (1, 2, 0))
OWN = tuple((1, 0, q) for q in range(QUARTERS))
STAGES = len(Z_EVEN)


def split_panels(left_refs, out_ref):
    for turn, left_ref in enumerate(left_refs):
        block = left_ref[0].reshape(-1, left_ref.shape[-1])
        high = block.astype(bf16)
        low = (block - high.astype(f32)).astype(bf16)
        out_ref[turn, 0] = jnp.concatenate([high, low], axis=1)


def split_left(panels):
    kb, lpb, bs, _ = panels[0].shape
    turns = len(panels)

    def body(*refs):
        split_panels(refs[:-1], refs[-1])

    return pl.pallas_call(
        body,
        grid=(kb,),
        in_specs=[pl.BlockSpec((1, lpb, bs, bs), lambda k: (k, 0, 0, 0))] * turns,
        out_specs=pl.BlockSpec((turns, 1, lpb * bs, 2 * bs), lambda k: (0, k, 0, 0)),
        out_shape=jax.ShapeDtypeStruct((turns, kb, lpb * bs, 2 * bs), bf16),
        cost_estimate=pl.CostEstimate(flops=4 * turns * kb * lpb * bs * bs, bytes_accessed=8 * turns * kb * lpb * bs * bs, transcendentals=0),
        name="split_left",
    )(*panels)


def accumulate(places, picks, table, left_cat, chunks, totals, kb):
    rows_all, cols_all, slots, where_at = places
    count = len(chunks)
    nc = slots.shape[0]
    turns, _, lrows, lcat = left_cat.shape
    bs = lcat // 2
    lpb = lrows // bs
    per = kb // QUARTERS
    bpr = chunks[0][0].shape[1]
    first = totals is None

    def kernel(table_ref, rows_ref, cols_ref, slots_ref, at_ref, *refs):
        left_refs = refs[:count]
        right_refs = refs[count:2 * count]
        out_ref, place_ref = refs[-2:]
        if first:
            out_ref[...] = jnp.zeros_like(out_ref)
        else:
            out_ref[...] = refs[2 * count][...]
        row, rows_n, col, cols_n, slots_m, rep = (at_ref[n] for n in range(6))
        for code in range(CB * CB):
            place_ref[code] = nc
        half = nc // 2
        for n in range(nc):
            local = lax.rem(n + nc - half * rep, nc)
            place_ref[slots_ref[n]] = local
        for c, (_, _, pick) in enumerate(chunks):
            counts = table_ref[3 * pick]
            turn = table_ref[3 * pick + 1]
            quarter = table_ref[3 * pick + 2]

            def do(c=c, turn=turn, quarter=quarter):
                c_at = lax.rem(col + turn, cols_n)
                m_at = lax.div(col + turn, cols_n)
                rows_base = ((c_at * slots_m + m_at) * kb + quarter * per) * lpb
                cols_base = (lax.rem(row + turn, rows_n) * kb + quarter * per) * bpr
                for k in range(per):
                    cat = left_refs[c][0, k]
                    left3 = jnp.concatenate([cat, cat[:, :bs]], axis=1)
                    right = jnp.concatenate([right_refs[c][k, b] for b in range(bpr)], axis=1)
                    high = right.astype(bf16)
                    low = (right - high.astype(f32)).astype(bf16)
                    right3 = jnp.concatenate([high, high, low], axis=0)
                    out = jnp.dot(left3, right3, preferred_element_type=f32)
                    for a in range(lpb):
                        left_place = rows_ref[rows_base + k * lpb + a] * CB
                        for b in range(bpr):
                            code = left_place + cols_ref[cols_base + k * bpr + b]
                            n = place_ref[code]
                            out_ref[n] += out[a * bs:(a + 1) * bs, b * bs:(b + 1) * bs]

            pl.when(counts > 0)(do)

    def left_spec(pick):
        return pl.BlockSpec((1, per, lrows, lcat), lambda g, tab, *_: (tab[3 * pick + 1], tab[3 * pick + 2], 0, 0))

    def right_spec(at):
        return pl.BlockSpec((per, bpr, bs, bs), lambda g, *_: (at, 0, 0, 0))

    total_spec = pl.BlockSpec((nc + 1, bs, bs), lambda g, *_: (0, 0, 0))
    operands = [left_cat] * count + [c[0] for c in chunks] + ([] if first else [totals])
    in_specs = [left_spec(c[2]) for c in chunks] + [right_spec(c[1]) for c in chunks] + ([] if first else [total_spec])
    flops = count * per * 2 * lrows * 3 * bs * bpr * bs
    moved = 4 * (count * per * bpr * bs * bs + 2 * (nc + 1) * bs * bs)
    return pl.pallas_call(
        kernel,
        grid_spec=pltpu.PrefetchScalarGridSpec(
            num_scalar_prefetch=5,
            grid=(1,),
            in_specs=in_specs,
            out_specs=total_spec,
            scratch_shapes=[pltpu.SMEM((CB * CB,), jnp.int32)],
        ),
        out_shape=jax.ShapeDtypeStruct((nc + 1, bs, bs), f32),
        input_output_aliases={} if first else {5 + 2 * count: 0},
        compiler_params=pltpu.CompilerParams(vmem_limit_bytes=32 * 1024 * 1024),
        cost_estimate=pl.CostEstimate(flops=flops, bytes_accessed=moved, transcendentals=0),
        name="accumulate",
    )(table, rows_all, cols_all, slots, where_at, *operands)


def after(x, *others):
    return lax.optimization_barrier((x,) + others)[0]


def shards(left_values, left_rows, right_values, right_cols, result_slots):
    rows_n, cols_n, reps = (lax.axis_size(a) for a in ("row", "col", "rep"))
    row, col, rep = (lax.axis_index(a) for a in ("row", "col", "rep"))
    panels = left_values[0, 0, 0]
    slots_m, kb = panels.shape[:2]
    right = right_values[0, 0, 0]
    slots = result_slots[0, 0]
    nc = slots.shape[0]
    per = kb // QUARTERS
    odd = row % 2 == 1

    z_pairs = [(r, (r - 2) % rows_n) for r in range(rows_n)]
    x_pairs = [(r, r ^ 1) for r in range(rows_n)]

    def along_z(even_chunk, odd_chunk):
        return lax.ppermute(jnp.where(odd, odd_chunk, even_chunk), "row", z_pairs)

    def along_x(even_chunk, odd_chunk):
        return lax.ppermute(jnp.where(odd, odd_chunk, even_chunk), "row", x_pairs)

    own = [right[q * per:(q + 1) * per] for q in range(QUARTERS)]

    def left_of(turn):
        to = (col - turn) % cols_n
        panel = lax.dynamic_index_in_dim(panels, (to + turn) // cols_n, 0, keepdims=False)
        if turn % cols_n == 0:
            return panel
        return lax.ppermute(panel, "col", [(c, (c - turn) % cols_n) for c in range(cols_n)])

    z = {}
    x = {}
    z[1] = along_z(own[0], own[1])
    x[1] = along_x(own[0], own[0])
    lefts = [left_of(turn) for turn in range(STEPS)]
    z[2] = along_z(own[1], own[2])

    rows_all = lax.all_gather(left_rows[0, 0, 0], "col").reshape(-1)
    cols_all = lax.all_gather(right_cols[0, 0, 0], "row").reshape(-1)
    where_at = jnp.stack([row, jnp.int32(rows_n), col, jnp.int32(cols_n), jnp.int32(slots_m), rep]).astype(jnp.int32)
    even_table = jnp.array(Z_EVEN + X_EVEN + OWN, jnp.int32).reshape(-1)
    odd_table = jnp.array(Z_ODD + X_ODD + OWN, jnp.int32).reshape(-1)
    table = jnp.where(odd, odd_table, even_table)
    places = (rows_all, cols_all, slots, where_at)
    left_cat = split_left(lefts)

    def add(totals, chunks):
        return accumulate(places, None, table, left_cat, chunks, totals, kb)

    def received(stage):
        return [(z[stage], 0, stage - 1), (x[stage], 0, STAGES + stage - 1)]

    totals = add(None, [(right, q, 2 * STAGES + q) for q in range(QUARTERS)])
    x[2] = along_x(z[1], own[1])
    z[3] = along_z(own[2], own[3])
    x[3] = along_x(z[1], own[2])
    totals = add(totals, received(1))
    z[4] = along_z(own[3], x[3])
    x[4] = along_x(z[2], own[3])
    totals = add(totals, received(2))
    z[5] = along_z(x[1], x[4])
    x[5] = along_x(z[3], z[1])
    totals = add(totals, received(3))
    z[6] = along_z(x[5], x[5])
    x[6] = along_x(z[4], z[2])
    totals = add(totals, received(4))
    z[7] = along_z(x[6], x[6])
    x[7] = along_x(z[5], z[3])
    totals = add(totals, received(5))
    totals = add(totals, received(6))
    totals = add(totals, received(7))
    half = nc // 2
    other = lax.ppermute(totals[half:nc], "rep", [(0, 1), (1, 0)])
    return (totals[:half] + other)[None, None]


def solution(mesh):
    in_specs = (
        P("row", "rep", "col", None, None, None, None, None),
        P("row", "rep", "col", None, None, None),
        P("rep", "row", "col", None, None, None, None),
        P("rep", "row", "col", None, None),
        P("row", "col", None),
    )
    out_specs = P("row", "col", "rep", None, None)
    return jax.shard_map(shards, mesh=mesh, in_specs=in_specs, out_specs=out_specs, check_vma=False)
```

```python
import jax
import jax.numpy as jnp
from jax import lax
from jax.experimental import pallas as pl
from jax.experimental.pallas import tpu as pltpu
from jax.sharding import PartitionSpec as P

STEPS = 4
CB = 8
QUARTERS = 4

bf16 = jnp.bfloat16
f32 = jnp.float32

Z_CHUNKS = (
    ((2, 0), (2, 0)),
    ((2, 1), (2, 1)),
    ((2, 2), (2, 2)),
    ((2, 3), (3, 0)),
    ((3, 3), (3, 1)),
    (None, (3, 2)),
    (None, (3, 3)),
)
X_CHUNKS = (
    ((1, 3), None),
    ((1, 0), None),
    ((1, 1), (1, 0)),
    ((1, 2), (1, 1)),
    ((3, 0), (1, 2)),
    ((3, 1), (1, 3)),
    ((3, 2), (2, 3)),
)


def copy_call(kernel, scalar, operands, out_shapes, name):
    any_spec = pl.BlockSpec(memory_space=pl.ANY)
    moved = sum(8 * shape.size for shape in out_shapes)
    return pl.pallas_call(
        kernel,
        in_specs=[pl.BlockSpec(memory_space=pltpu.SMEM)] + [any_spec] * len(operands),
        out_specs=[any_spec] * len(out_shapes),
        out_shape=out_shapes,
        scratch_shapes=[pltpu.SemaphoreType.DMA((len(out_shapes),))],
        cost_estimate=pl.CostEstimate(flops=0, bytes_accessed=moved, transcendentals=0),
        name=name,
    )(scalar, *operands)


def pick(odd, per, even_part, odd_part, *others):
    (even_from, even_at), (odd_from, odd_at) = even_part, odd_part

    def kernel(odd_ref, even_ref, other_ref, *refs):
        out_ref, sems = refs[-2:]

        def copy_from(ref, at):
            copy = pltpu.make_async_copy(ref.at[pl.ds(at * per, per)], out_ref, sems.at[0])
            copy.start()
            copy.wait()

        if even_part is odd_part:
            copy_from(even_ref, even_at)
        else:
            pl.when(odd_ref[0] == 0)(lambda: copy_from(even_ref, even_at))
            pl.when(odd_ref[0] != 0)(lambda: copy_from(other_ref, odd_at))

    out_shape = jax.ShapeDtypeStruct((per,) + even_from.shape[1:], even_from.dtype)
    return copy_call(kernel, odd, [even_from, odd_from, *others], [out_shape], "pick")[0]


def pick_panels(panels, which):
    count = which.shape[0]

    def kernel(which_ref, panels_ref, *refs):
        sems = refs[-1]
        copies = [pltpu.make_async_copy(panels_ref.at[which_ref[n]], refs[n], sems.at[n]) for n in range(count)]
        for copy in copies:
            copy.start()
        for copy in copies:
            copy.wait()

    out_shape = jax.ShapeDtypeStruct(panels.shape[1:], panels.dtype)
    return copy_call(kernel, which, [panels], [out_shape] * count, "pick_panels")


def accumulate(scalars, lefts, chunks, totals, nc):
    _, kb, lpb, bs, _ = lefts[0][0].shape
    per = kb // QUARTERS
    bpr = chunks[0][0].shape[1]
    products = lpb * bpr
    odd_at = STEPS * kb * products
    first = totals is None
    sides = [(c, side) for c in range(len(chunks)) for side in range(2) if chunks[c][2][side] is not None]
    sides = [(c, side) for c, side in sides if side == 0 or chunks[c][2][0] != chunks[c][2][1]]

    def kernel(scalar_ref, *refs):
        left_refs = dict(zip(sides, refs))
        right_refs = refs[len(sides):len(sides) + len(chunks)]
        out_ref = refs[-1]
        odd = scalar_ref[odd_at]
        if first:
            out_ref[...] = jnp.zeros_like(out_ref)
        else:
            out_ref[...] = refs[-2][...]
        for c, (_, _, (even_is, odd_is)) in enumerate(chunks):
            def one(c=c, even_is=even_is, odd_is=odd_is):
                both = even_is != odd_is and even_is is not None and odd_is is not None
                base = [0 if what is None else (what[0] * kb + what[1] * per) * products for what in (even_is, odd_is)]
                base_at = jnp.where(odd == 0, base[0], base[1]) if both else base[0] if even_is else base[1]
                for k in range(per):
                    if both:
                        left = jnp.where(odd == 0, left_refs[c, 0][0, k], left_refs[c, 1][0, k])
                    else:
                        left = left_refs[c, 0 if even_is else 1][0, k]
                    left = left.reshape(lpb * bs, bs)
                    left_high = left.astype(bf16)
                    left_low = (left - left_high.astype(f32)).astype(bf16)
                    right = jnp.concatenate([right_refs[c][k, b] for b in range(bpr)], axis=1)
                    high = right.astype(bf16)
                    low = (right - high.astype(f32)).astype(bf16)
                    out = jnp.dot(
                        jnp.concatenate([left_high, left_low, left_high], axis=1),
                        jnp.concatenate([high, high, low], axis=0),
                        preferred_element_type=f32,
                    )
                    for a in range(lpb):
                        for b in range(bpr):
                            n = scalar_ref[base_at + k * products + a * bpr + b]
                            out_ref[n] += out[a * bs:(a + 1) * bs, b * bs:(b + 1) * bs]

            if even_is is None:
                pl.when(odd != 0)(one)
            elif odd_is is None:
                pl.when(odd == 0)(one)
            else:
                one()

    def left_spec(turn, quarter):
        held_at = lefts[turn][1]
        return pl.BlockSpec((1, per, lpb, bs, bs), lambda g, *_: (held_at, quarter, 0, 0, 0))

    def right_spec(at):
        return pl.BlockSpec((per, bpr, bs, bs), lambda g, *_: (at, 0, 0, 0))

    total_spec = pl.BlockSpec((nc + 1, bs, bs), lambda g, *_: (0, 0, 0))
    operands = [lefts[chunks[c][2][side][0]][0] for c, side in sides] + [c[0] for c in chunks]
    in_specs = [left_spec(*chunks[c][2][side]) for c, side in sides]
    in_specs += [right_spec(at) for _, at, _ in chunks]
    if not first:
        operands.append(totals)
        in_specs.append(total_spec)
    flops = len(chunks) * per * 2 * lpb * bs * 3 * bs * bpr * bs
    moved = 4 * (len(chunks) * per * (bpr + lpb) * bs * bs + 2 * (nc + 1) * bs * bs)
    return pl.pallas_call(
        kernel,
        grid_spec=pltpu.PrefetchScalarGridSpec(
            num_scalar_prefetch=1,
            grid=(1,),
            in_specs=in_specs,
            out_specs=total_spec,
        ),
        out_shape=jax.ShapeDtypeStruct((nc + 1, bs, bs), f32),
        input_output_aliases={} if first else {len(operands): 0},
        compiler_params=pltpu.CompilerParams(vmem_limit_bytes=32 * 1024 * 1024),
        cost_estimate=pl.CostEstimate(flops=flops, bytes_accessed=moved, transcendentals=0),
        name="accumulate",
    )(scalars, *operands)


def shards(left_values, left_rows, right_values, right_cols, result_slots):
    rows_n, cols_n = (lax.axis_size(a) for a in ("row", "col"))
    row, col, rep = (lax.axis_index(a) for a in ("row", "col", "rep"))
    panels = left_values[0, 0, 0]
    panel_rows = left_rows[0, 0, 0]
    right = right_values[0, 0, 0]
    right_places = right_cols[0, 0, 0]
    slots = result_slots[0, 0]
    kb = right.shape[0]
    nc = slots.shape[0]
    half = nc // 2
    per = kb // QUARTERS
    odd = (row % 2).astype(jnp.int32).reshape(1)

    z_pairs = [(r, (r - 2) % rows_n) for r in range(rows_n)]
    x_pairs = [(r, r ^ 1) for r in range(rows_n)]

    def along_z(chunk):
        return lax.ppermute(chunk, "row", z_pairs)

    def along_x(chunk):
        return lax.ppermute(chunk, "row", x_pairs)

    def sent(even_part, odd_part=None, *others):
        even_part = even_part if isinstance(even_part, tuple) else (even_part, 0)
        odd_part = even_part if odd_part is None else odd_part if isinstance(odd_part, tuple) else (odd_part, 0)
        return pick(odd, per, even_part, odd_part, *others)

    z = {}
    x = {}
    z[1] = along_z(sent((right, 0)))
    x[1] = along_x(sent((right, 3)))
    z[2] = along_z(sent((right, 1)))

    def to_reader(held, turn):
        return lax.ppermute(held, "col", [(c, (c - turn) % cols_n) for c in range(cols_n)])

    moving = [turn for turn in range(STEPS) if turn % cols_n]
    place = [turn // cols_n if turn % cols_n == 0 else ((col - turn) % cols_n + turn) // cols_n for turn in range(STEPS)]
    lefts = [(panels, place[turn]) for turn in range(STEPS)]
    row_turns = [panel_rows[place[turn]] for turn in range(STEPS)]
    if moving:
        picked = pick_panels(panels, jnp.stack([place[turn] for turn in moving]).astype(jnp.int32))
        for turn, panel in zip(moving, picked):
            lefts[turn] = (to_reader(panel, turn)[None], 0)
            row_turns[turn] = to_reader(row_turns[turn], turn)

    def right_of(held, turn):
        if turn % rows_n == 0:
            return held
        return lax.ppermute(held, "row", [(r, (r - turn) % rows_n) for r in range(rows_n)])

    rows_at = jnp.stack(row_turns)
    cols_at = jnp.stack([right_of(right_places, turn) for turn in range(STEPS)])
    codes = rows_at[:, :, :, None] * CB + cols_at[:, :, None, :]
    order = (jnp.arange(nc, dtype=jnp.int32) + nc - half * rep) % nc
    listed = codes[..., None] == slots
    where_to = nc - jnp.sum(jnp.where(listed, nc - order, 0), axis=-1, dtype=jnp.int32)
    scalars = jnp.concatenate([where_to.reshape(-1), odd])

    def add(totals, chunks):
        return accumulate(scalars, lefts, chunks, totals, nc)

    def received(stage):
        return [(z[stage], 0, Z_CHUNKS[stage - 1]), (x[stage], 0, X_CHUNKS[stage - 1])]

    x[2] = along_x(sent((right, 0)))
    totals = add(None, [(right, q, ((0, q), (0, q))) for q in range(QUARTERS)])
    z[3] = along_z(sent((right, 2), None, z[1], totals))
    x[3] = along_x(sent(z[1], (right, 1), x[1], totals))
    totals = add(totals, received(1))
    x[4] = along_x(sent(z[2], (right, 2), x[2], totals))
    z[4] = along_z(sent((right, 3), x[3], totals))
    totals = add(totals, received(2))
    x[5] = along_x(sent(z[3], z[1], totals))
    z[5] = along_z(sent(x[1], x[4], totals))
    totals = add(totals, received(3))
    x[6] = along_x(sent(z[4], z[2], totals))
    z[6] = along_z(x[5])
    totals = add(totals, received(4))
    x[7] = along_x(sent(z[5], z[3], totals))
    z[7] = along_z(x[6])
    totals = add(totals, received(5))
    totals = add(totals, received(6))
    totals = add(totals, received(7))
    other = lax.ppermute(totals[half:nc], "rep", [(0, 1), (1, 0)])
    return (totals[:half] + other)[None, None]


def solution(mesh):
    in_specs = (
        P("row", "rep", "col", None, None, None, None, None),
        P("row", "rep", "col", None, None, None),
        P("rep", "row", "col", None, None, None, None),
        P("rep", "row", "col", None, None),
        P("row", "col", None),
    )
    out_specs = P("row", "col", "rep", None, None)
    return jax.shard_map(shards, mesh=mesh, in_specs=in_specs, out_specs=out_specs, check_vma=False)
```

```python
import jax
import jax.numpy as jnp
from jax import lax
from jax.experimental import pallas as pl
from jax.experimental.pallas import tpu as pltpu
from jax.sharding import PartitionSpec as P

STEPS = 4
CB = 8
QUARTERS = 4

bf16 = jnp.bfloat16
f32 = jnp.float32

Z_CHUNKS = (
    ((2, 0), (2, 0)),
    ((2, 1), (2, 1)),
    ((2, 2), (2, 2)),
    ((2, 3), (3, 0)),
    ((3, 3), (3, 1)),
    (None, (3, 2)),
    (None, (3, 3)),
)
X_CHUNKS = (
    ((1, 3), None),
    ((1, 0), None),
    ((1, 1), (1, 0)),
    ((1, 2), (1, 1)),
    ((3, 0), (1, 2)),
    ((3, 1), (1, 3)),
    ((3, 2), (2, 3)),
)


def pick(odd, per, even_part, odd_part, *others):
    parts = [even_part] if even_part is odd_part else [even_part, odd_part]
    array = even_part[0]

    def kernel(odd_ref, *refs):
        out_ref = refs[-1]
        if len(parts) == 1:
            out_ref[...] = refs[0][...]
            return

        def copy_from(ref):
            out_ref[...] = ref[...]

        pl.when(odd_ref[0] == 0)(lambda: copy_from(refs[0]))
        pl.when(odd_ref[0] != 0)(lambda: copy_from(refs[1]))

    def spec(at):
        return pl.BlockSpec((per,) + array.shape[1:], lambda g, *_: (at, 0, 0, 0))

    out_shape = jax.ShapeDtypeStruct((per,) + array.shape[1:], array.dtype)
    return pl.pallas_call(
        kernel,
        grid_spec=pltpu.PrefetchScalarGridSpec(
            num_scalar_prefetch=1,
            grid=(1,),
            in_specs=[spec(at) for _, at in parts] + [pl.BlockSpec(memory_space=pl.ANY)] * len(others),
            out_specs=spec(0),
        ),
        out_shape=out_shape,
        compiler_params=pltpu.CompilerParams(vmem_limit_bytes=16 * 1024 * 1024),
        cost_estimate=pl.CostEstimate(flops=0, bytes_accessed=8 * out_shape.size, transcendentals=0),
        name="pick",
    )(odd, *[part for part, _ in parts], *others)


def pick_panel(panels, which):
    _, kb, lpb, bs, _ = panels.shape
    per = kb // QUARTERS

    def kernel(which_ref, panel_ref, out_ref):
        out_ref[...] = panel_ref[0]

    return pl.pallas_call(
        kernel,
        grid_spec=pltpu.PrefetchScalarGridSpec(
            num_scalar_prefetch=1,
            grid=(QUARTERS,),
            in_specs=[pl.BlockSpec((1, per, lpb, bs, bs), lambda g, which_ref: (which_ref[0], g, 0, 0, 0))],
            out_specs=pl.BlockSpec((per, lpb, bs, bs), lambda g, which_ref: (g, 0, 0, 0)),
        ),
        out_shape=jax.ShapeDtypeStruct(panels.shape[1:], panels.dtype),
        cost_estimate=pl.CostEstimate(flops=0, bytes_accessed=8 * kb * lpb * bs * bs, transcendentals=0),
        name="pick_panel",
    )(which.astype(jnp.int32).reshape(1), panels)


def accumulate(scalars, lefts, chunks, totals, nc):
    _, kb, lpb, bs, _ = lefts[0][0].shape
    per = kb // QUARTERS
    bpr = chunks[0][0].shape[1]
    products = lpb * bpr
    odd_at = STEPS * kb * products
    first = totals is None
    sides = [(c, side) for c in range(len(chunks)) for side in range(2) if chunks[c][2][side] is not None]
    sides = [(c, side) for c, side in sides if side == 0 or chunks[c][2][0] != chunks[c][2][1]]

    def kernel(scalar_ref, *refs):
        left_refs = dict(zip(sides, refs))
        right_refs = refs[len(sides):len(sides) + len(chunks)]
        out_ref, token_ref = refs[-2:]
        token_ref[...] = jnp.zeros_like(token_ref)
        odd = scalar_ref[odd_at]
        if first:
            out_ref[...] = jnp.zeros_like(out_ref)
        else:
            out_ref[...] = refs[-3][...]
        for c, (_, _, (even_is, odd_is)) in enumerate(chunks):
            def one(c=c, even_is=even_is, odd_is=odd_is):
                both = even_is != odd_is and even_is is not None and odd_is is not None
                base = [0 if what is None else (what[0] * kb + what[1] * per) * products for what in (even_is, odd_is)]
                base_at = jnp.where(odd == 0, base[0], base[1]) if both else base[0] if even_is else base[1]
                for k in range(per):
                    if both:
                        left = jnp.where(odd == 0, left_refs[c, 0][0, k], left_refs[c, 1][0, k])
                    else:
                        left = left_refs[c, 0 if even_is else 1][0, k]
                    left = left.reshape(lpb * bs, bs)
                    left_high = left.astype(bf16)
                    left_low = (left - left_high.astype(f32)).astype(bf16)
                    right = jnp.concatenate([right_refs[c][k, b] for b in range(bpr)], axis=1)
                    high = right.astype(bf16)
                    low = (right - high.astype(f32)).astype(bf16)
                    out = jnp.dot(
                        jnp.concatenate([left_high, left_low, left_high], axis=1),
                        jnp.concatenate([high, high, low], axis=0),
                        preferred_element_type=f32,
                    )
                    for a in range(lpb):
                        for b in range(bpr):
                            n = scalar_ref[base_at + k * products + a * bpr + b]
                            out_ref[n] += out[a * bs:(a + 1) * bs, b * bs:(b + 1) * bs]

            if even_is is None:
                pl.when(odd != 0)(one)
            elif odd_is is None:
                pl.when(odd == 0)(one)
            else:
                one()

    def left_spec(turn, quarter):
        held_at = lefts[turn][1]
        return pl.BlockSpec((1, per, lpb, bs, bs), lambda g, *_: (held_at, quarter, 0, 0, 0))

    def right_spec(at):
        return pl.BlockSpec((per, bpr, bs, bs), lambda g, *_: (at, 0, 0, 0))

    total_spec = pl.BlockSpec((nc + 1, bs, bs), lambda g, *_: (0, 0, 0))
    operands = [lefts[chunks[c][2][side][0]][0] for c, side in sides] + [c[0] for c in chunks]
    in_specs = [left_spec(*chunks[c][2][side]) for c, side in sides]
    in_specs += [right_spec(at) for _, at, _ in chunks]
    if not first:
        operands.append(totals)
        in_specs.append(total_spec)
    flops = len(chunks) * per * 2 * lpb * bs * 3 * bs * bpr * bs
    moved = 4 * (len(chunks) * per * (bpr + lpb) * bs * bs + 2 * (nc + 1) * bs * bs)
    return pl.pallas_call(
        kernel,
        grid_spec=pltpu.PrefetchScalarGridSpec(
            num_scalar_prefetch=1,
            grid=(1,),
            in_specs=in_specs,
            out_specs=[total_spec, pl.BlockSpec((8, 128), lambda g, *_: (0, 0))],
        ),
        out_shape=[jax.ShapeDtypeStruct((nc + 1, bs, bs), f32), jax.ShapeDtypeStruct((8, 128), f32)],
        input_output_aliases={} if first else {len(operands): 0},
        compiler_params=pltpu.CompilerParams(vmem_limit_bytes=32 * 1024 * 1024),
        cost_estimate=pl.CostEstimate(flops=flops, bytes_accessed=moved, transcendentals=0),
        name="accumulate",
    )(scalars, *operands)


def shards(left_values, left_rows, right_values, right_cols, result_slots):
    rows_n, cols_n = (lax.axis_size(a) for a in ("row", "col"))
    row, col, rep = (lax.axis_index(a) for a in ("row", "col", "rep"))
    panels = left_values[0, 0, 0]
    panel_rows = left_rows[0, 0, 0]
    right = right_values[0, 0, 0]
    right_places = right_cols[0, 0, 0]
    slots = result_slots[0, 0]
    kb = right.shape[0]
    nc = slots.shape[0]
    half = nc // 2
    per = kb // QUARTERS
    odd = (row % 2).astype(jnp.int32).reshape(1)

    z_pairs = [(r, (r - 2) % rows_n) for r in range(rows_n)]
    x_pairs = [(r, r ^ 1) for r in range(rows_n)]

    def along_z(chunk):
        return lax.ppermute(chunk, "row", z_pairs)

    def along_x(chunk):
        return lax.ppermute(chunk, "row", x_pairs)

    def sent(even_part, odd_part=None, *others):
        even_part = even_part if isinstance(even_part, tuple) else (even_part, 0)
        odd_part = even_part if odd_part is None else odd_part if isinstance(odd_part, tuple) else (odd_part, 0)
        return pick(odd, per, even_part, odd_part, *others)

    z = {}
    x = {}
    z[1] = along_z(sent((right, 0)))
    x[1] = along_x(sent((right, 3)))
    z[2] = along_z(sent((right, 1)))

    def to_reader(held, turn):
        return lax.ppermute(held, "col", [(c, (c - turn) % cols_n) for c in range(cols_n)])

    moving = [turn for turn in range(STEPS) if turn % cols_n]
    place = [turn // cols_n if turn % cols_n == 0 else ((col - turn) % cols_n + turn) // cols_n for turn in range(STEPS)]
    lefts = [(panels, place[turn]) for turn in range(STEPS)]
    row_turns = [panel_rows[place[turn]] for turn in range(STEPS)]
    if moving:
        for turn in moving:
            lefts[turn] = (to_reader(pick_panel(panels, place[turn]), turn)[None], 0)
            row_turns[turn] = to_reader(row_turns[turn], turn)

    def right_of(held, turn):
        if turn % rows_n == 0:
            return held
        return lax.ppermute(held, "row", [(r, (r - turn) % rows_n) for r in range(rows_n)])

    rows_at = jnp.stack(row_turns)
    cols_at = jnp.stack([right_of(right_places, turn) for turn in range(STEPS)])
    codes = rows_at[:, :, :, None] * CB + cols_at[:, :, None, :]
    order = (jnp.arange(nc, dtype=jnp.int32) + nc - half * rep) % nc
    listed = codes[..., None] == slots
    where_to = nc - jnp.sum(jnp.where(listed, nc - order, 0), axis=-1, dtype=jnp.int32)
    scalars = jnp.concatenate([where_to.reshape(-1), odd])

    def add(totals, chunks):
        return accumulate(scalars, lefts, chunks, totals, nc)

    def received(stage):
        return [(z[stage], 0, Z_CHUNKS[stage - 1]), (x[stage], 0, X_CHUNKS[stage - 1])]

    x[2] = along_x(sent((right, 0)))
    totals, done = add(None, [(right, q, ((0, q), (0, q))) for q in range(QUARTERS)])
    z[3] = along_z(sent((right, 2), None, z[1], done))
    x[3] = along_x(sent(z[1], (right, 1), x[1], done))
    totals, done = add(totals, received(1))
    x[4] = along_x(sent(z[2], (right, 2), x[2], done))
    z[4] = along_z(sent((right, 3), x[3], done))
    totals, done = add(totals, received(2))
    x[5] = along_x(sent(z[3], z[1], done))
    z[5] = along_z(sent(x[1], x[4], done))
    totals, done = add(totals, received(3))
    x[6] = along_x(sent(z[4], z[2], done))
    z[6] = along_z(x[5])
    totals, done = add(totals, received(4))
    x[7] = along_x(sent(z[5], z[3], done))
    z[7] = along_z(x[6])
    totals, done = add(totals, received(5))
    totals, done = add(totals, received(6))
    totals, done = add(totals, received(7))
    other = lax.ppermute(totals[half:nc], "rep", [(0, 1), (1, 0)])
    return (totals[:half] + other)[None, None]


def solution(mesh):
    in_specs = (
        P("row", "rep", "col", None, None, None, None, None),
        P("row", "rep", "col", None, None, None),
        P("rep", "row", "col", None, None, None, None),
        P("rep", "row", "col", None, None),
        P("row", "col", None),
    )
    out_specs = P("row", "col", "rep", None, None)
    return jax.shard_map(shards, mesh=mesh, in_specs=in_specs, out_specs=out_specs, check_vma=False)
```

```python
import jax
import jax.numpy as jnp
from jax import lax
from jax.experimental import pallas as pl
from jax.experimental.pallas import tpu as pltpu
from jax.sharding import PartitionSpec as P

STEPS = 4
CB = 8
QUARTERS = 4

bf16 = jnp.bfloat16
f32 = jnp.float32

Z_CHUNKS = {
    1: ((2, 0), (2, 0)),
    2: ((2, 1), (2, 1)),
    3: ((2, 2), (2, 2)),
    4: ((2, 3), (3, 0)),
    5: ((3, 3), (3, 1)),
    6: (None, (3, 2)),
    7: (None, (3, 3)),
}
X_CHUNKS = {
    1: ((1, 2), None),
    2: ((1, 3), None),
    3: ((1, 0), (1, 0)),
    4: ((1, 1), (1, 1)),
    5: ((3, 0), (1, 2)),
    6: ((3, 1), (1, 3)),
    7: ((3, 2), (2, 3)),
}


def pick(odd, size, even_part, odd_part, *others):
    parts = [even_part] if even_part is odd_part else [even_part, odd_part]
    array = even_part[0]

    def kernel(odd_ref, *refs):
        out_ref = refs[-1]
        if len(parts) == 1:
            out_ref[...] = refs[0][...]
            return

        def copy_from(ref):
            out_ref[...] = ref[...]

        pl.when(odd_ref[0] == 0)(lambda: copy_from(refs[0]))
        pl.when(odd_ref[0] != 0)(lambda: copy_from(refs[1]))

    def spec(at):
        return pl.BlockSpec((size,) + array.shape[1:], lambda g, *_: (at, 0, 0, 0))

    out_shape = jax.ShapeDtypeStruct((size,) + array.shape[1:], array.dtype)
    return pl.pallas_call(
        kernel,
        grid_spec=pltpu.PrefetchScalarGridSpec(
            num_scalar_prefetch=1,
            grid=(1,),
            in_specs=[spec(at) for _, at in parts] + [pl.BlockSpec(memory_space=pl.ANY)] * len(others),
            out_specs=spec(0),
        ),
        out_shape=out_shape,
        compiler_params=pltpu.CompilerParams(vmem_limit_bytes=16 * 1024 * 1024),
        cost_estimate=pl.CostEstimate(flops=0, bytes_accessed=8 * out_shape.size, transcendentals=0),
        name="pick",
    )(odd, *[part for part, _ in parts], *others)


def accumulate(scalars, lefts, chunks, totals, nc):
    _, kb, lpb, bs, _ = lefts[0].shape
    per = kb // QUARTERS
    bpr = chunks[0][0].shape[1]
    products = lpb * bpr
    odd_at = STEPS * kb * products
    first = totals is None
    sides = [(c, side) for c in range(len(chunks)) for side in range(2) if chunks[c][2][side] is not None]
    sides = [(c, side) for c, side in sides if side == 0 or chunks[c][2][0] != chunks[c][2][1]]

    def kernel(scalar_ref, *refs):
        left_refs = dict(zip(sides, refs))
        right_refs = refs[len(sides):len(sides) + len(chunks)]
        out_ref, token_ref = refs[-2:]
        token_ref[...] = jnp.zeros_like(token_ref)
        odd = scalar_ref[odd_at]
        if first:
            out_ref[...] = jnp.zeros_like(out_ref)
        else:
            out_ref[...] = refs[-3][...]
        for c, (_, _, (even_is, odd_is)) in enumerate(chunks):
            def one(c=c, even_is=even_is, odd_is=odd_is):
                both = even_is != odd_is and even_is is not None and odd_is is not None
                base = [0 if what is None else (what[0] * kb + what[1] * per) * products for what in (even_is, odd_is)]
                base_at = jnp.where(odd == 0, base[0], base[1]) if both else base[0] if even_is else base[1]
                for k in range(per):
                    if both:
                        left = jnp.where(odd == 0, left_refs[c, 0][0, k], left_refs[c, 1][0, k])
                    else:
                        left = left_refs[c, 0 if even_is else 1][0, k]
                    left = left.reshape(lpb * bs, bs)
                    left_high = left.astype(bf16)
                    left_low = (left - left_high.astype(f32)).astype(bf16)
                    right = jnp.concatenate([right_refs[c][k, b] for b in range(bpr)], axis=1)
                    high = right.astype(bf16)
                    low = (right - high.astype(f32)).astype(bf16)
                    out = jnp.dot(
                        jnp.concatenate([left_high, left_low, left_high], axis=1),
                        jnp.concatenate([high, high, low], axis=0),
                        preferred_element_type=f32,
                    )
                    for a in range(lpb):
                        for b in range(bpr):
                            n = scalar_ref[base_at + k * products + a * bpr + b]
                            out_ref[n] += out[a * bs:(a + 1) * bs, b * bs:(b + 1) * bs]

            if even_is is None:
                pl.when(odd != 0)(one)
            elif odd_is is None:
                pl.when(odd == 0)(one)
            else:
                one()

    def left_spec(turn, quarter):
        return pl.BlockSpec((1, per, lpb, bs, bs), lambda g, s: (s[odd_at + 1 + turn], quarter, 0, 0, 0))

    def right_spec(at):
        return pl.BlockSpec((per, bpr, bs, bs), lambda g, *_: (at, 0, 0, 0))

    total_spec = pl.BlockSpec((nc + 1, bs, bs), lambda g, *_: (0, 0, 0))
    operands = [lefts[chunks[c][2][side][0]] for c, side in sides] + [c[0] for c in chunks]
    in_specs = [left_spec(*chunks[c][2][side]) for c, side in sides]
    in_specs += [right_spec(at) for _, at, _ in chunks]
    if not first:
        operands.append(totals)
        in_specs.append(total_spec)
    flops = len(chunks) * per * 2 * lpb * bs * 3 * bs * bpr * bs
    moved = 4 * (len(chunks) * per * (bpr + lpb) * bs * bs + 2 * (nc + 1) * bs * bs)
    return pl.pallas_call(
        kernel,
        grid_spec=pltpu.PrefetchScalarGridSpec(
            num_scalar_prefetch=1,
            grid=(1,),
            in_specs=in_specs,
            out_specs=[total_spec, pl.BlockSpec((8, 128), lambda g, *_: (0, 0))],
        ),
        out_shape=[jax.ShapeDtypeStruct((nc + 1, bs, bs), f32), jax.ShapeDtypeStruct((8, 128), f32)],
        input_output_aliases={} if first else {len(operands): 0},
        compiler_params=pltpu.CompilerParams(vmem_limit_bytes=32 * 1024 * 1024),
        cost_estimate=pl.CostEstimate(flops=flops, bytes_accessed=moved, transcendentals=0),
        name="accumulate",
    )(scalars, *operands)


def shards(left_values, left_rows, right_values, right_cols, result_slots):
    rows_n, cols_n = (lax.axis_size(a) for a in ("row", "col"))
    row, col, rep = (lax.axis_index(a) for a in ("row", "col", "rep"))
    panels = left_values[0, 0, 0]
    panel_rows = left_rows[0, 0, 0]
    right = right_values[0, 0, 0]
    right_places = right_cols[0, 0, 0]
    slots = result_slots[0, 0]
    kb = right.shape[0]
    nc = slots.shape[0]
    half = nc // 2
    per = kb // QUARTERS
    odd = (row % 2).astype(jnp.int32).reshape(1)

    z_pairs = [(r, (r - 2) % rows_n) for r in range(rows_n)]
    x_pairs = [(r, r ^ 1) for r in range(rows_n)]

    def along_z(chunk):
        return lax.ppermute(chunk, "row", z_pairs)

    def along_x(chunk):
        return lax.ppermute(chunk, "row", x_pairs)

    def sent(even_part, odd_part=None, *others):
        even_part = even_part if isinstance(even_part, tuple) else (even_part, 0)
        odd_part = even_part if odd_part is None else odd_part if isinstance(odd_part, tuple) else (odd_part, 0)
        return pick(odd, per, even_part, odd_part, *others)

    z = {}
    x = {}
    z[1] = along_z(sent((right, 0)))
    x[1] = along_x(pick(odd, 2 * per, *[(right, QUARTERS // 2 - 1)] * 2))
    z[2] = along_z(sent((right, 1)))

    shifts = sorted({turn % cols_n for turn in range(STEPS)})
    held = {
        shift: (panels, panel_rows) if shift == 0 else lax.ppermute((panels, panel_rows), "col", [(c, (c - shift) % cols_n) for c in range(cols_n)])
        for shift in shifts
    }
    place = [(col + turn) // cols_n for turn in range(STEPS)]
    lefts = [held[turn % cols_n][0] for turn in range(STEPS)]
    rows_at = jnp.stack([held[turn % cols_n][1][place[turn]] for turn in range(STEPS)])

    def right_of(held, turn):
        if turn % rows_n == 0:
            return held
        return lax.ppermute(held, "row", [(r, (r - turn) % rows_n) for r in range(rows_n)])

    cols_at = jnp.stack([right_of(right_places, turn) for turn in range(STEPS)])
    codes = rows_at[:, :, :, None] * CB + cols_at[:, :, None, :]
    order = (jnp.arange(nc, dtype=jnp.int32) + nc - half * rep) % nc
    listed = codes[..., None] == slots
    where_to = nc - jnp.sum(jnp.where(listed, nc - order, 0), axis=-1, dtype=jnp.int32)
    scalars = jnp.concatenate([where_to.reshape(-1), odd, jnp.stack(place).astype(jnp.int32)])

    def add(totals, chunks):
        return accumulate(scalars, lefts, chunks, totals, nc)

    def received(stage):
        along_x_part = (x[1], stage - 1) if stage < 3 else (x[stage], 0)
        return [(z[stage], 0, Z_CHUNKS[stage]), (*along_x_part, X_CHUNKS[stage])]

    totals, done = add(None, [(right, q, ((0, q), (0, q))) for q in range(QUARTERS)])
    x[3] = along_x(sent(z[1], (right, 0), done))
    z[3] = along_z(sent((right, 2), None, z[1], done))
    totals, done = add(totals, received(1))
    x[4] = along_x(sent(z[2], (right, 1), done))
    z[4] = along_z(sent((right, 3), x[3], done))
    totals, done = add(totals, received(2))
    x[5] = along_x(sent(z[3], z[1], done))
    z[5] = along_z(sent((x[1], 1), x[4], done))
    totals, done = add(totals, received(3))
    x[6] = along_x(sent(z[4], z[2], done))
    z[6] = along_z(x[5])
    totals, done = add(totals, received(4))
    x[7] = along_x(sent(z[5], z[3], done))
    z[7] = along_z(x[6])
    totals, done = add(totals, received(5))
    totals, done = add(totals, received(6))
    totals, done = add(totals, received(7))
    other = lax.ppermute(totals[half:nc], "rep", [(0, 1), (1, 0)])
    return (totals[:half] + other)[None, None]


def solution(mesh):
    in_specs = (
        P("row", "rep", "col", None, None, None, None, None),
        P("row", "rep", "col", None, None, None),
        P("rep", "row", "col", None, None, None, None),
        P("rep", "row", "col", None, None),
        P("row", "col", None),
    )
    out_specs = P("row", "col", "rep", None, None)
    return jax.shard_map(shards, mesh=mesh, in_specs=in_specs, out_specs=out_specs, check_vma=False)
```

```python
import jax
import jax.numpy as jnp
from jax import lax
from jax.experimental import pallas as pl
from jax.experimental.pallas import tpu as pltpu
from jax.sharding import PartitionSpec as P

STEPS = 4
CB = 8
HALVES = 2
QUARTERS = HALVES * HALVES

bf16 = jnp.bfloat16
f32 = jnp.float32

Z_CHUNKS = {
    1: ((2, 0), (2, 0)),
    2: ((2, 1), (2, 1)),
    3: ((2, 2), (2, 2)),
    4: ((2, 3), (3, 0)),
    5: ((3, 3), (3, 1)),
    6: (None, (3, 2)),
    7: (None, (3, 3)),
}
X_CHUNKS = {
    1: ((1, 2), None),
    2: ((1, 3), None),
    3: ((1, 0), (1, 0)),
    4: ((1, 1), (1, 1)),
    5: ((3, 0), (1, 2)),
    6: ((3, 1), (1, 3)),
    7: ((3, 2), (2, 3)),
}

in_vmem = pl.BlockSpec(memory_space=pltpu.VMEM)
anywhere = pl.BlockSpec(memory_space=pl.ANY)


def whole(shape):
    return pl.BlockSpec(shape, lambda *_: (0,) * len(shape))


def lower_lanes(shape):
    return lax.broadcasted_iota(jnp.int32, shape, len(shape) - 1) < shape[-1] // 2


def swap_lanes(x):
    return pltpu.roll(x, x.shape[-1] // 2, x.ndim - 1)


def cut(right_ref, out_ref, half, at=0):
    per, bpr, bs, _ = right_ref.shape
    lower = lower_lanes((bs, bs))
    for k in range(per):
        for pair in range(bpr // 2):
            even, odd = right_ref[k, 2 * pair], right_ref[k, 2 * pair + 1]
            if half == 0:
                both = jnp.where(lower, even, swap_lanes(odd))
            else:
                both = jnp.where(lower, swap_lanes(even), odd)
            out_ref[at + k, :, pair * bs:(pair + 1) * bs] = both


def own_spec(right, k_half):
    return pl.BlockSpec((right.shape[0] // HALVES,) + right.shape[1:], lambda *_: (k_half, 0, 0, 0))


def quarter_shape(right):
    kb, bpr, bs, _ = right.shape
    return (kb // HALVES, bs, bpr * bs // HALVES)


def own_quarters(right, quarters, *others):
    per, bs, width = quarter_shape(right)

    def kernel(*refs):
        for n, quarter in enumerate(quarters):
            cut(refs[n], refs[-1], quarter // HALVES, n * per)

    out_shape = jax.ShapeDtypeStruct((len(quarters) * per, bs, width), right.dtype)
    return pl.pallas_call(
        kernel,
        grid=(1,),
        in_specs=[own_spec(right, quarter % HALVES) for quarter in quarters] + [anywhere] * len(others),
        out_specs=whole(out_shape.shape),
        out_shape=out_shape,
        compiler_params=pltpu.CompilerParams(vmem_limit_bytes=12 * 1024 * 1024),
        cost_estimate=pl.CostEstimate(flops=0, bytes_accessed=12 * out_shape.size, transcendentals=0),
        name="own_quarters",
    )(*[right] * len(quarters), *others)


def pick(odd, right, even_part, odd_part, *others):
    parts = (even_part, odd_part)
    per, bs, width = quarter_shape(right)

    def kernel(odd_ref, *refs):
        out_ref = refs[-1]

        def copy_from(n):
            array, at = parts[n]
            if array is None:
                cut(refs[n], out_ref, at // HALVES)
            else:
                out_ref[...] = refs[n][at * per:(at + 1) * per]

        pl.when(odd_ref[0] == 0)(lambda: copy_from(0))
        pl.when(odd_ref[0] != 0)(lambda: copy_from(1))

    out_shape = jax.ShapeDtypeStruct((per, bs, width), right.dtype)
    specs = [own_spec(right, at % HALVES) if array is None else in_vmem for array, at in parts]
    return pl.pallas_call(
        kernel,
        grid=(1,),
        in_specs=[pl.BlockSpec(memory_space=pltpu.SMEM)] + specs + [anywhere] * len(others),
        out_specs=whole(out_shape.shape),
        out_shape=out_shape,
        compiler_params=pltpu.CompilerParams(vmem_limit_bytes=8 * 1024 * 1024),
        cost_estimate=pl.CostEstimate(flops=0, bytes_accessed=8 * out_shape.size, transcendentals=0),
        name="pick",
    )(odd, *[right if array is None else array for array, _ in parts], *others)


def accumulate(scalars, lefts, chunks, totals, nc, finish=None):
    _, kb, lpb, bs, _ = lefts[0].shape
    per = kb // HALVES
    own = totals is None
    bpr = chunks[0][0].shape[1] if own else HALVES * chunks[0][0].shape[2] // bs
    width = bpr * bs // HALVES
    lanes = bs // HALVES
    products = lpb * bpr
    odd_at = STEPS * kb * products
    packed = nc // 4
    if own:
        touched = list(range(HALVES))
    else:
        touched = sorted({what[1] // HALVES for _, _, both in chunks for what in both if what is not None})
    sides = [(c, side) for c in range(len(chunks)) for side in range(2) if chunks[c][2][side] is not None]
    sides = [(c, side) for c, side in sides if side == 0 or chunks[c][2][0] != chunks[c][2][1]]

    def kernel(scalar_ref, *refs):
        left_refs = dict(zip(sides, refs))
        right_refs = refs[len(sides):len(sides) + len(chunks)]
        outs = refs[len(sides) + len(chunks) + (0 if own else len(touched)):]
        total_refs = dict(zip(touched, outs))
        outs = outs[len(touched):]
        outs[0][...] = jnp.zeros_like(outs[0])
        odd = scalar_ref[odd_at]
        if own:
            for ref in total_refs.values():
                ref[...] = jnp.zeros_like(ref)

        def products_of(left, right):
            left = left.reshape(lpb * bs, bs)
            left_high = left.astype(bf16)
            left_low = (left - left_high.astype(f32)).astype(bf16)
            high = right.astype(bf16)
            low = (right - high.astype(f32)).astype(bf16)
            return jnp.dot(
                jnp.concatenate([left_high, left_low, left_high], axis=1),
                jnp.concatenate([high, high, low], axis=0),
                preferred_element_type=f32,
            )

        def add_own(left_ref, right_ref):
            for k in range(kb):
                out = products_of(left_ref[0, k], jnp.concatenate([right_ref[k, b] for b in range(bpr)], axis=1))
                for a in range(lpb):
                    for b in range(bpr):
                        n = scalar_ref[k * products + a * bpr + b]
                        for half in range(HALVES):
                            at = slice(half * lanes, (half + 1) * lanes)
                            total_refs[half][n, :, at] += out[a * bs:(a + 1) * bs, b * bs:(b + 1) * bs][:, at]

        def add(c, side):
            turn, quarter = chunks[c][2][side]
            half, k_half = divmod(quarter, HALVES)
            base = (turn * kb + k_half * per) * products
            left_ref, right_ref, total_ref = left_refs[c, side], right_refs[c], total_refs[half]
            for k in range(per):
                out = products_of(left_ref[0, k], right_ref[chunks[c][1] * per + k])
                for a in range(lpb):
                    for b in range(bpr):
                        n = scalar_ref[base + k * products + a * bpr + b]
                        at = (b % HALVES) * lanes
                        total_ref[n, :, at:at + lanes] += out[a * bs:(a + 1) * bs, b * lanes:(b + 1) * lanes]

        if own:
            add_own(left_refs[0, 0], right_refs[0])
            return
        for c, (_, _, both) in enumerate(chunks):
            if both[0] == both[1]:
                add(c, 0)
                continue
            if both[0] is not None:
                pl.when(odd == 0)(lambda c=c: add(c, 0))
            if both[1] is not None:
                pl.when(odd != 0)(lambda c=c: add(c, 1))
        if finish is not None:
            lower = lower_lanes((bs, bs))
            for kept, ref in enumerate(outs[1:]):
                for p in range(packed):
                    n = 2 * packed * kept + p
                    one, two = total_refs[finish][n], total_refs[finish][n + packed]
                    ref[p] = jnp.where(lower, one + swap_lanes(one), two + swap_lanes(two))

    def left_spec(turn, quarter):
        return pl.BlockSpec((1, per, lpb, bs, bs), lambda g, s: (s[odd_at + 1 + turn], quarter % HALVES, 0, 0, 0))

    operands = [lefts[chunks[c][2][side][0]] for c, side in sides] + [c[0] for c in chunks]
    if own:
        in_specs = [pl.BlockSpec((1, kb, lpb, bs, bs), lambda g, s: (s[odd_at + 1], 0, 0, 0, 0)), whole(chunks[0][0].shape)]
    else:
        in_specs = [left_spec(*chunks[c][2][side]) for c, side in sides] + [in_vmem] * len(chunks)
    held = len(operands) + 1
    if not own:
        operands += [totals[half] for half in touched]
        in_specs += [in_vmem] * len(touched)
    outs = [jax.ShapeDtypeStruct((nc + 1, bs, bs), f32)] * len(touched) + [jax.ShapeDtypeStruct((8, 128), jnp.int32)]
    if finish is not None:
        outs += [jax.ShapeDtypeStruct((packed, bs, bs), f32)] * 2
    parts = QUARTERS if own else len(chunks)
    flops = parts * per * 2 * lpb * bs * 3 * bs * width
    moved = 4 * parts * per * (lpb * bs * bs + bs * width)
    results = pl.pallas_call(
        kernel,
        grid_spec=pltpu.PrefetchScalarGridSpec(
            num_scalar_prefetch=1,
            grid=(1,),
            in_specs=in_specs,
            out_specs=[in_vmem] * len(outs),
        ),
        out_shape=outs,
        input_output_aliases={} if own else {held + n: n for n in range(len(touched))},
        compiler_params=pltpu.CompilerParams(vmem_limit_bytes=16 * 1024 * 1024),
        cost_estimate=pl.CostEstimate(flops=flops, bytes_accessed=moved, transcendentals=0),
        name="accumulate",
    )(scalars, *operands)
    totals = [None] * HALVES if own else list(totals)
    for half, total in zip(touched, results):
        totals[half] = total
    return (totals, *results[len(touched):])


def combine(kept, other):
    packed, bs, _ = kept[0].shape
    steps = 2 if packed % 2 == 0 else 1
    per = packed // steps

    def kernel(kept_0, kept_1, other_0, other_1, out_ref):
        lower = lower_lanes((bs, bs))
        for p in range(per):
            left = kept_0[p] + other_0[p]
            right = kept_1[p] + other_1[p]
            out_ref[0, p] = jnp.where(lower, left, swap_lanes(right))
            out_ref[1, p] = jnp.where(lower, swap_lanes(left), right)

    return pl.pallas_call(
        kernel,
        grid=(steps,),
        in_specs=[pl.BlockSpec((per, bs, bs), lambda g: (g, 0, 0))] * 4,
        out_specs=pl.BlockSpec((2, per, bs, bs), lambda g: (0, g, 0, 0)),
        out_shape=jax.ShapeDtypeStruct((2, packed, bs, bs), f32),
        name="combine",
    )(*kept, *other).reshape(2 * packed, bs, bs)


def shards(left_values, left_rows, right_values, right_cols, result_slots):
    rows_n, cols_n = (lax.axis_size(a) for a in ("row", "col"))
    row, col, rep = (lax.axis_index(a) for a in ("row", "col", "rep"))
    panels = left_values[0, 0, 0]
    panel_rows = left_rows[0, 0, 0]
    right = right_values[0, 0, 0]
    right_places = right_cols[0, 0, 0]
    slots = result_slots[0, 0]
    kb = right.shape[0]
    nc = slots.shape[0]
    per = kb // HALVES
    odd = (row % 2).astype(jnp.int32).reshape(1)

    z_pairs = [(r, (r - 2) % rows_n) for r in range(rows_n)]
    x_pairs = [(r, r ^ 1) for r in range(rows_n)]

    def along_z(chunk):
        return lax.ppermute(chunk, "row", z_pairs)

    def along_x(chunk):
        return lax.ppermute(chunk, "row", x_pairs)

    def sent(even_part, odd_part, *others):
        return pick(odd, right, even_part, odd_part, *others)

    z = {}
    x = {}
    z[1] = along_z(own_quarters(right, (0,)))
    x[1] = along_x(own_quarters(right, (2, 3)))

    shifts = sorted({turn % cols_n for turn in range(STEPS)})
    held = {
        shift: (panels, panel_rows) if shift == 0 else lax.ppermute((panels, panel_rows), "col", [(c, (c - shift) % cols_n) for c in range(cols_n)])
        for shift in shifts
    }
    place = [(col + turn) // cols_n for turn in range(STEPS)]
    lefts = [held[turn % cols_n][0] for turn in range(STEPS)]
    rows_at = jnp.stack([held[turn % cols_n][1][place[turn]] for turn in range(STEPS)])

    def right_of(held, turn):
        if turn % rows_n == 0:
            return held
        return lax.ppermute(held, "row", [(r, (r - turn) % rows_n) for r in range(rows_n)])

    cols_at = jnp.stack([right_of(right_places, turn) for turn in range(STEPS)])
    codes = rows_at[:, :, :, None] * CB + cols_at[:, :, None, :]
    order = (jnp.arange(nc, dtype=jnp.int32) + nc - nc // 2 * rep) % nc
    listed = codes[..., None] == slots
    where_to = nc - jnp.sum(jnp.where(listed, nc - order, 0), axis=-1, dtype=jnp.int32)
    scalars = jnp.concatenate([where_to.reshape(-1), odd, jnp.stack(place).astype(jnp.int32)])

    def add(totals, chunks, finish=None):
        return accumulate(scalars, lefts, chunks, totals, nc, finish)

    def along_z_part(stage):
        return (z[stage], 0, Z_CHUNKS[stage])

    def along_x_part(stage):
        return (*((x[1], stage - 1) if stage < 3 else (x[stage], 0)), X_CHUNKS[stage])

    def received(stage):
        return [along_z_part(stage), along_x_part(stage)]

    totals, done = add(None, [(right, 0, ((0, 0), (0, 0)))])
    z[2] = along_z(own_quarters(right, (1,), done))
    x[3] = along_x(sent((z[1], 0), (None, 0), done))
    z[3] = along_z(own_quarters(right, (2,), z[1], done))
    totals, done = add(totals, received(1))
    x[4] = along_x(sent((z[2], 0), (None, 1), done))
    z[4] = along_z(sent((None, 3), (x[3], 0), done))
    totals, done = add(totals, received(2))
    x[5] = along_x(sent((z[3], 0), (z[1], 0), done))
    z[5] = along_z(sent((x[1], 1), (x[4], 0), done))
    totals, done = add(totals, received(3))
    x[6] = along_x(sent((z[4], 0), (z[2], 0), done))
    z[6] = along_z(x[5])
    totals, done = add(totals, received(4))
    x[7] = along_x(sent((z[5], 0), (z[3], 0), done))
    z[7] = along_z(x[6])
    totals, done = add(totals, received(5))

    def to_partner(blocks):
        return lax.ppermute(blocks, "rep", [(0, 1), (1, 0)])

    totals, done, kept_0, send_0 = add(totals, [along_x_part(6)], 0)
    other_0 = to_partner(send_0)
    totals, done, kept_1, send_1 = add(totals, [along_z_part(6), along_x_part(7), along_z_part(7)], 1)
    other_1 = to_partner(send_1)
    return combine((kept_0, kept_1), (other_0, other_1))[None, None]


def solution(mesh):
    in_specs = (
        P("row", "rep", "col", None, None, None, None, None),
        P("row", "rep", "col", None, None, None),
        P("rep", "row", "col", None, None, None, None),
        P("rep", "row", "col", None, None),
        P("row", "col", None),
    )
    out_specs = P("row", "col", "rep", None, None)
    return jax.shard_map(shards, mesh=mesh, in_specs=in_specs, out_specs=out_specs, check_vma=False)
```

```python
import jax
import jax.numpy as jnp
from jax import lax
from jax.experimental import pallas as pl
from jax.experimental.pallas import tpu as pltpu
from jax.sharding import PartitionSpec as P

STEPS = 4
CB = 8
HALVES = 2
QUARTERS = HALVES * HALVES

bf16 = jnp.bfloat16
f32 = jnp.float32

Z_CHUNKS = {
    1: ((2, 0), (2, 0)),
    2: ((2, 1), (2, 1)),
    3: ((2, 2), (2, 2)),
    4: ((2, 3), (3, 0)),
    5: ((3, 3), (3, 1)),
    6: (None, (3, 2)),
    7: (None, (3, 3)),
}
X_CHUNKS = {
    1: ((1, 2), None),
    2: ((1, 3), None),
    3: ((1, 0), (1, 0)),
    4: ((1, 1), (1, 1)),
    5: ((3, 0), (1, 2)),
    6: ((3, 1), (1, 3)),
    7: ((3, 2), (2, 3)),
}
EXTRA = 8

in_smem = pl.BlockSpec(memory_space=pltpu.SMEM)
in_vmem = pl.BlockSpec(memory_space=pltpu.VMEM)
anywhere = pl.BlockSpec(memory_space=pl.ANY)


def whole(shape):
    return pl.BlockSpec(shape, lambda *_: (0,) * len(shape))


def lower_lanes(shape):
    return lax.broadcasted_iota(jnp.int32, shape, len(shape) - 1) < shape[-1] // 2


def swap_lanes(x):
    return pltpu.roll(x, x.shape[-1] // 2, x.ndim - 1)


def cut(right_ref, out_ref, half, at=0):
    per, bpr, bs, _ = right_ref.shape
    lower = lower_lanes((bs, bs))
    for k in range(per):
        for pair in range(bpr // 2):
            even, odd = right_ref[k, 2 * pair], right_ref[k, 2 * pair + 1]
            if half == 0:
                both = jnp.where(lower, even, swap_lanes(odd))
            else:
                both = jnp.where(lower, swap_lanes(even), odd)
            out_ref[at + k * bs:at + (k + 1) * bs, pair * bs:(pair + 1) * bs] = both


def own_spec(right, k_half):
    return pl.BlockSpec((right.shape[0] // HALVES,) + right.shape[1:], lambda *_: (k_half, 0, 0, 0))


def quarter_shape(right):
    kb, bpr, bs, _ = right.shape
    return kb // HALVES * bs, bpr * bs // HALVES


def own_quarters(right, quarters, cols, *others):
    rows, width = quarter_shape(right)
    extra = [] if cols is None else [cols]

    def kernel(*refs):
        out_ref = refs[-1]
        for n, quarter in enumerate(quarters):
            cut(refs[n], out_ref, quarter // HALVES, n * rows)
        if extra:
            out_ref[len(quarters) * rows:, :] = refs[len(quarters)][...]

    out_shape = jax.ShapeDtypeStruct((len(quarters) * rows + EXTRA * len(extra), width), right.dtype)
    return pl.pallas_call(
        kernel,
        grid=(1,),
        in_specs=[own_spec(right, quarter % HALVES) for quarter in quarters] + [whole(x.shape) for x in extra] + [anywhere] * len(others),
        out_specs=whole(out_shape.shape),
        out_shape=out_shape,
        compiler_params=pltpu.CompilerParams(vmem_limit_bytes=12 * 1024 * 1024),
        cost_estimate=pl.CostEstimate(flops=0, bytes_accessed=12 * out_shape.size, transcendentals=0),
        name="own_quarters",
    )(*[right] * len(quarters), *extra, *others)


def pick(info, right, cols, even_part, odd_part, *others):
    parts = (even_part, odd_part)
    rows, width = quarter_shape(right)
    extra = [] if cols is None else [cols]

    def taken(array, at):
        return array.shape[0] if extra and at == 0 and array.shape[0] == rows + EXTRA else rows

    def kernel(info_ref, *refs):
        out_ref = refs[-1]

        def copy_from(n):
            array, at = parts[n]
            if array is None:
                cut(refs[n], out_ref, at // HALVES)
                if extra:
                    out_ref[rows:, :] = refs[2][...]
                return
            out_ref[:refs[n].shape[0]] = refs[n][...]
            if extra and refs[n].shape[0] == rows:
                out_ref[rows:, :] = jnp.zeros((EXTRA, width), right.dtype)

        pl.when(info_ref[0] == 0)(lambda: copy_from(0))
        pl.when(info_ref[0] != 0)(lambda: copy_from(1))

    def spec(array, at):
        if array is None:
            return own_spec(right, at % HALVES)
        return pl.BlockSpec((taken(array, at), width), lambda *_: (at, 0))

    out_shape = jax.ShapeDtypeStruct((rows + EXTRA * len(extra), width), right.dtype)
    return pl.pallas_call(
        kernel,
        grid=(1,),
        in_specs=[in_smem] + [spec(*part) for part in parts] + [whole(x.shape) for x in extra] + [anywhere] * len(others),
        out_specs=whole(out_shape.shape),
        out_shape=out_shape,
        compiler_params=pltpu.CompilerParams(vmem_limit_bytes=8 * 1024 * 1024),
        cost_estimate=pl.CostEstimate(flops=0, bytes_accessed=8 * out_shape.size, transcendentals=0),
        name="pick",
    )(info, *[right if array is None else array for array, _ in parts], *extra, *others)


def accumulate(info, places, lefts, chunks, totals, nc, finish=None):
    _, kb, lpb, bs, _ = lefts[0].shape
    per = kb // HALVES
    own = totals is None
    bpr = chunks[0][0].shape[1] if own else HALVES * chunks[0][0].shape[1] // bs
    width = bpr * bs // HALVES
    lanes = bs // HALVES
    products = lpb * bpr
    turns = sorted({what[0] for _, _, both in chunks for what in both if what is not None})
    packed = nc // 4
    if own:
        touched = list(range(HALVES))
    else:
        touched = sorted({what[1] // HALVES for _, _, both in chunks for what in both if what is not None})
    sides = [(c, side) for c in range(len(chunks)) for side in range(2) if chunks[c][2][side] is not None]
    sides = [(c, side) for c, side in sides if side == 0 or chunks[c][2][0] != chunks[c][2][1]]

    def kernel(info_ref, *refs):
        place_refs = dict(zip(turns, refs))
        refs = refs[len(turns):]
        left_refs = dict(zip(sides, refs))
        right_refs = refs[len(sides):len(sides) + len(chunks)]
        outs = refs[len(sides) + len(chunks) + (0 if own else len(touched)):]
        total_refs = dict(zip(touched, outs))
        outs = outs[len(touched):]
        outs[0][...] = jnp.zeros_like(outs[0])
        odd = info_ref[0]
        if own:
            for ref in total_refs.values():
                ref[...] = jnp.zeros_like(ref)

        def products_of(left, right):
            left = left.reshape(lpb * bs, bs)
            left_high = left.astype(bf16)
            left_low = (left - left_high.astype(f32)).astype(bf16)
            high = right.astype(bf16)
            low = (right - high.astype(f32)).astype(bf16)
            return jnp.dot(
                jnp.concatenate([left_high, left_low, left_high], axis=1),
                jnp.concatenate([high, high, low], axis=0),
                preferred_element_type=f32,
            )

        def add_own(left_ref, right_ref):
            for k in range(kb):
                out = products_of(left_ref[0, k], jnp.concatenate([right_ref[k, b] for b in range(bpr)], axis=1))
                for a in range(lpb):
                    for b in range(bpr):
                        n = place_refs[0][k * products + a * bpr + b]
                        for half in range(HALVES):
                            at = slice(half * lanes, (half + 1) * lanes)
                            total_refs[half][n, :, at] += out[a * bs:(a + 1) * bs, b * bs:(b + 1) * bs][:, at]

        def add(c, side):
            turn, quarter = chunks[c][2][side]
            half, k_half = divmod(quarter, HALVES)
            base = k_half * per * products
            left_ref, right_ref, total_ref = left_refs[c, side], right_refs[c], total_refs[half]
            for k in range(per):
                out = products_of(left_ref[0, k], right_ref[k * bs:(k + 1) * bs])
                for a in range(lpb):
                    for b in range(bpr):
                        n = place_refs[turn][base + k * products + a * bpr + b]
                        at = (b % HALVES) * lanes
                        total_ref[n, :, at:at + lanes] += out[a * bs:(a + 1) * bs, b * lanes:(b + 1) * lanes]

        if own:
            add_own(left_refs[0, 0], right_refs[0])
            return
        for c, (_, _, both) in enumerate(chunks):
            if both[0] == both[1]:
                add(c, 0)
                continue
            if both[0] is not None:
                pl.when(odd == 0)(lambda c=c: add(c, 0))
            if both[1] is not None:
                pl.when(odd != 0)(lambda c=c: add(c, 1))
        if finish is not None:
            lower = lower_lanes((bs, bs))
            for kept, ref in enumerate(outs[1:]):
                for p in range(packed):
                    n = 2 * packed * kept + p
                    one, two = total_refs[finish][n], total_refs[finish][n + packed]
                    ref[p] = jnp.where(lower, one + swap_lanes(one), two + swap_lanes(two))

    def left_spec(turn, quarter):
        return pl.BlockSpec((1, per, lpb, bs, bs), lambda g, info_ref, *_: (info_ref[1 + turn], quarter % HALVES, 0, 0, 0))

    operands = [lefts[chunks[c][2][side][0]] for c, side in sides] + [c[0] for c in chunks]
    if own:
        in_specs = [pl.BlockSpec((1, kb, lpb, bs, bs), lambda g, info_ref, *_: (info_ref[1], 0, 0, 0, 0)), whole(chunks[0][0].shape)]
    else:
        in_specs = [left_spec(*chunks[c][2][side]) for c, side in sides] + [pl.BlockSpec((per * bs, width), lambda g, *_, at=at: (at, 0)) for _, at, _ in chunks]
    held = len(operands) + 1 + len(turns)
    if not own:
        operands += [totals[half] for half in touched]
        in_specs += [in_vmem] * len(touched)
    outs = [jax.ShapeDtypeStruct((nc + 1, bs, bs), f32)] * len(touched) + [jax.ShapeDtypeStruct((8, 128), jnp.int32)]
    if finish is not None:
        outs += [jax.ShapeDtypeStruct((packed, bs, bs), f32)] * 2
    parts = QUARTERS if own else len(chunks)
    flops = parts * per * 2 * lpb * bs * 3 * bs * width
    moved = 4 * parts * per * (lpb * bs * bs + bs * width)
    results = pl.pallas_call(
        kernel,
        grid_spec=pltpu.PrefetchScalarGridSpec(
            num_scalar_prefetch=1 + len(turns),
            grid=(1,),
            in_specs=in_specs,
            out_specs=[in_vmem] * len(touched) + [whole(x.shape) for x in outs[len(touched):]],
        ),
        out_shape=outs,
        input_output_aliases={} if own else {held + n: n for n in range(len(touched))},
        compiler_params=pltpu.CompilerParams(vmem_limit_bytes=16 * 1024 * 1024),
        cost_estimate=pl.CostEstimate(flops=flops, bytes_accessed=moved, transcendentals=0),
        name="accumulate",
    )(info, *[places[turn] for turn in turns], *operands)
    totals = [None] * HALVES if own else list(totals)
    for half, total in zip(touched, results):
        totals[half] = total
    return (totals, *results[len(touched):])


def own_places(info, slots, rows, cols, kb, lpb):
    nc = slots.shape[0]
    bpr = cols.shape[0] // kb

    def kernel(info_ref, slots_ref, rows_ref, cols_ref, table_ref, out_ref):
        for code in range(CB * CB):
            table_ref[code] = nc
        behind = nc - nc // 2 * info_ref[1 + STEPS]
        for n in range(nc):
            table_ref[slots_ref[n]] = lax.rem(n + behind, nc)
        fill_places(info_ref[1], table_ref, rows_ref, lambda n: cols_ref[n], out_ref, kb, lpb, bpr)

    return pl.pallas_call(
        kernel,
        in_specs=[in_smem] * 4,
        out_specs=[in_smem] * 2,
        out_shape=[jax.ShapeDtypeStruct((CB * CB,), jnp.int32), jax.ShapeDtypeStruct((kb * lpb * bpr,), jnp.int32)],
        compiler_params=pltpu.CompilerParams(vmem_limit_bytes=1024 * 1024),
        name="own_places",
    )(info, slots, rows, cols)


def fill_places(panel, table_ref, rows_ref, col_of, out_ref, kb, lpb, bpr):
    def column(k, carry):
        cols = [col_of(k * bpr + b) for b in range(bpr)]
        for a in range(lpb):
            row = rows_ref[(panel * kb + k) * lpb + a] * CB
            for b in range(bpr):
                out_ref[(k * lpb + a) * bpr + b] = table_ref[row + cols[b]]
        return carry

    lax.fori_loop(0, kb, column, 0)


def panel_places(info, table, turn, rows, even_part, odd_part, kb, lpb, bpr):
    parts = (even_part, odd_part)

    def kernel(info_ref, table_ref, rows_ref, even_ref, odd_ref, out_ref, cols_ref, scalar_ref, sem):
        cols = jnp.where(info_ref[0] == 0, even_ref[...], odd_ref[...])
        cols_ref[...] = cols.astype(jnp.int32)
        copy = pltpu.make_async_copy(cols_ref, scalar_ref, sem)
        copy.start()
        copy.wait()
        fill_places(info_ref[1 + turn], table_ref, rows_ref, lambda n: scalar_ref[0, n], out_ref, kb, lpb, bpr)

    return pl.pallas_call(
        kernel,
        grid=(1,),
        in_specs=[in_smem] * 3 + [pl.BlockSpec((EXTRA, 128), lambda g, at=at: (at // EXTRA, 0)) for _, at in parts],
        out_specs=in_smem,
        out_shape=jax.ShapeDtypeStruct((kb * lpb * bpr,), jnp.int32),
        scratch_shapes=[pltpu.VMEM((EXTRA, 128), jnp.int32), pltpu.SMEM((EXTRA, 128), jnp.int32), pltpu.SemaphoreType.DMA],
        compiler_params=pltpu.CompilerParams(vmem_limit_bytes=1024 * 1024),
        name="panel_places",
    )(info, table, rows, *[array for array, _ in parts])


def combine(kept, other):
    packed, bs, _ = kept[0].shape
    steps = 2 if packed % 2 == 0 else 1
    per = packed // steps

    def kernel(kept_0, kept_1, other_0, other_1, out_ref):
        lower = lower_lanes((bs, bs))
        for p in range(per):
            left = kept_0[p] + other_0[p]
            right = kept_1[p] + other_1[p]
            out_ref[0, p] = jnp.where(lower, left, swap_lanes(right))
            out_ref[1, p] = jnp.where(lower, swap_lanes(left), right)

    return pl.pallas_call(
        kernel,
        grid=(steps,),
        in_specs=[pl.BlockSpec((per, bs, bs), lambda g: (g, 0, 0))] * 4,
        out_specs=pl.BlockSpec((2, per, bs, bs), lambda g: (0, g, 0, 0)),
        out_shape=jax.ShapeDtypeStruct((2, packed, bs, bs), f32),
        compiler_params=pltpu.CompilerParams(vmem_limit_bytes=8 * 1024 * 1024),
        name="combine",
    )(*kept, *other).reshape(2 * packed, bs, bs)


def shards(left_values, left_rows, right_values, right_cols, result_slots):
    rows_n, cols_n = (lax.axis_size(a) for a in ("row", "col"))
    row, col, rep = (lax.axis_index(a) for a in ("row", "col", "rep"))
    panels = left_values[0, 0, 0]
    panel_rows = left_rows.reshape(-1)
    right = right_values[0, 0, 0]
    right_places = right_cols.reshape(-1)
    slots = result_slots[0, 0]
    kb = right.shape[0]
    nc = slots.shape[0]
    place = [(col + turn) // cols_n for turn in range(STEPS)]
    info = jnp.stack([row % 2, *place, rep]).astype(jnp.int32)

    z_pairs = [(r, (r - 2) % rows_n) for r in range(rows_n)]
    x_pairs = [(r, r ^ 1) for r in range(rows_n)]

    def along_z(chunk):
        return lax.ppermute(chunk, "row", z_pairs)

    def along_x(chunk):
        return lax.ppermute(chunk, "row", x_pairs)

    rows, width = quarter_shape(right)
    cols_row = jnp.pad(right_places.astype(f32)[None], ((0, EXTRA - 1), (0, width - right_places.shape[0])))

    def sent(even_part, odd_part, *others, extra=False):
        return pick(info, right, cols_row if extra else None, even_part, odd_part, *others)

    z = {}
    x = {}
    upper = own_quarters(right, (2, 3), None)
    x[1] = along_x(upper)
    z[1] = along_z(own_quarters(right, (0,), cols_row, upper))

    shifts = sorted({turn % cols_n for turn in range(STEPS)})
    held = {
        shift: (panels, panel_rows) if shift == 0 else lax.ppermute((panels, panel_rows), "col", [(c, (c - shift) % cols_n) for c in range(cols_n)])
        for shift in shifts
    }
    lefts = [held[turn % cols_n][0] for turn in range(STEPS)]
    rows_at = [held[turn % cols_n][1] for turn in range(STEPS)]

    lpb, bpr = panels.shape[2], right.shape[1]
    places = {}
    table, places[0] = own_places(info, slots, panel_rows, right_places, kb, lpb)

    def read_places(turn, even_part, odd_part):
        places[turn] = panel_places(info, table, turn, rows_at[turn], even_part, odd_part, kb, lpb, bpr)

    def add(totals, chunks, finish=None):
        return accumulate(info, places, lefts, chunks, totals, nc, finish)

    def along_z_part(stage):
        return (z[stage], 0, Z_CHUNKS[stage])

    def along_x_part(stage):
        return (*((x[1], stage - 1) if stage < 3 else (x[stage], 0)), X_CHUNKS[stage])

    totals, done = accumulate(info, places, [panels] * STEPS, [(right, 0, ((0, 0), (0, 0)))], None, nc)
    second = own_quarters(right, (1,), None, done)
    z[2] = along_z(second)
    x[3] = along_x(sent((z[1], 0), (None, 0), done, extra=True))
    z[3] = along_z(own_quarters(right, (2,), None, z[1], done))
    read_places(2, (z[1], rows), (z[1], rows))
    totals, done = add(totals, [along_z_part(1), along_z_part(2)])
    x[4] = along_x(sent((z[2], 0), (None, 1), done))
    z[4] = along_z(sent((None, 3), (x[3], 0), done, extra=True))
    read_places(1, (x[3], rows), (x[3], rows))
    totals, done = add(totals, [along_x_part(1), along_x_part(2), along_x_part(3)])
    x[5] = along_x(sent((z[3], 0), (z[1], 0), done, extra=True))
    z[5] = along_z(sent((x[1], 1), (x[4], 0), done))
    totals, done = add(totals, [along_z_part(3), along_x_part(4)])
    x[6] = along_x(sent((z[4], 0), (z[2], 0), done))
    z[6] = along_z(x[5])
    read_places(3, (x[5], rows), (z[4], rows))
    totals, done = add(totals, [along_z_part(4), along_x_part(5)])
    x[7] = along_x(sent((z[5], 0), (z[3], 0), done))
    z[7] = along_z(x[6])
    totals, done = add(totals, [along_z_part(5)])

    def to_partner(blocks):
        return lax.ppermute(blocks, "rep", [(0, 1), (1, 0)])

    totals, done, kept_0, send_0 = add(totals, [along_x_part(6)], 0)
    other_0 = to_partner(send_0)
    totals, done = add(totals, [along_z_part(6), along_x_part(7)])
    totals, done, kept_1, send_1 = add(totals, [along_z_part(7)], 1)
    other_1 = to_partner(send_1)
    return combine((kept_0, kept_1), (other_0, other_1))[None, None]


def solution(mesh):
    in_specs = (
        P("row", "rep", "col", None, None, None, None, None),
        P("row", "rep", "col", None, None, None),
        P("rep", "row", "col", None, None, None, None),
        P("rep", "row", "col", None, None),
        P("row", "col", None),
    )
    out_specs = P("row", "col", "rep", None, None)
    return jax.shard_map(shards, mesh=mesh, in_specs=in_specs, out_specs=out_specs, check_vma=False)
```

```python
import jax
import jax.numpy as jnp
from jax import lax
from jax.experimental import pallas as pl
from jax.experimental.pallas import tpu as pltpu
from jax.sharding import PartitionSpec as P

STEPS = 4
CB = 8
HALVES = 2
QUARTERS = HALVES * HALVES

bf16 = jnp.bfloat16
f32 = jnp.float32

PARTS = 2
Z_CHUNKS = {
    1: ((2, 0, 0, 2), (2, 0, 0, 2)),
    2: ((2, 1, 0, 2), (2, 1, 0, 2)),
    3: ((2, 2, 0, 2), (2, 2, 0, 2)),
    4: ((2, 3, 0, 2), (3, 0, 0, 2)),
    5: ((3, 3, 0, 2), (3, 1, 0, 2)),
    6: ((3, 2, 0, 1), (3, 2, 0, 2)),
    7: (None, (3, 3, 0, 2)),
}
X_CHUNKS = {
    1: ((1, 3, 0, 2), None),
    2: ((1, 2, 0, 1), None),
    3: ((1, 0, 0, 2), (1, 0, 0, 2)),
    4: ((1, 1, 0, 2), (1, 1, 0, 2)),
    5: ((3, 0, 0, 2), (1, 2, 0, 2)),
    6: ((3, 1, 0, 2), (1, 3, 0, 2)),
    7: ((3, 2, 1, 1), (2, 3, 0, 2)),
    8: ((1, 2, 1, 1), None),
}

in_smem = pl.BlockSpec(memory_space=pltpu.SMEM)
in_vmem = pl.BlockSpec(memory_space=pltpu.VMEM)
anywhere = pl.BlockSpec(memory_space=pl.ANY)


def whole(shape):
    return pl.BlockSpec(shape, lambda *_: (0,) * len(shape))


def lower_lanes(shape):
    return lax.broadcasted_iota(jnp.int32, shape, len(shape) - 1) < shape[-1] // 2


def swap_lanes(x):
    return pltpu.roll(x, x.shape[-1] // 2, x.ndim - 1)


def cut(right_ref, out_ref, half, at=0):
    count, bpr, bs, _ = right_ref.shape
    lower = lower_lanes((bs, bs))
    for k in range(count):
        for pair in range(bpr // 2):
            even, odd = right_ref[k, 2 * pair], right_ref[k, 2 * pair + 1]
            if half == 0:
                both = jnp.where(lower, even, swap_lanes(odd))
            else:
                both = jnp.where(lower, swap_lanes(even), odd)
            out_ref[at + k * bs:at + (k + 1) * bs, pair * bs:(pair + 1) * bs] = both


def own_spec(right, quarter, first=0, parts=PARTS):
    count = right.shape[0] // (HALVES * PARTS) * parts
    at = (quarter % HALVES * PARTS + first) // parts
    return pl.BlockSpec((count,) + right.shape[1:], lambda *_: (at, 0, 0, 0))


def quarter_shape(right):
    kb, bpr, bs, _ = right.shape
    return kb // HALVES * bs, bpr * bs // HALVES


def put_extra(out_ref, cols_ref, rows):
    kb, bpr = cols_ref.shape
    out_ref[rows:rows + kb, :bpr] = cols_ref[...].astype(out_ref.dtype)


def own_quarters(right, quarters, cols, *others):
    rows, width = quarter_shape(right)
    extra = [] if cols is None else [cols]
    starts = [sum(parts for _, _, parts in quarters[:n]) * rows // PARTS for n in range(len(quarters) + 1)]

    def kernel(*refs):
        out_ref = refs[-1]
        for n, (quarter, _, _) in enumerate(quarters):
            cut(refs[n], out_ref, quarter // HALVES, starts[n])
        if extra:
            put_extra(out_ref, refs[len(quarters)], starts[-1])

    out_shape = jax.ShapeDtypeStruct((starts[-1] + right.shape[0] * len(extra), width), right.dtype)
    return pl.pallas_call(
        kernel,
        grid=(1,),
        in_specs=[own_spec(right, *part) for part in quarters] + [whole(x.shape) for x in extra] + [anywhere] * len(others),
        out_specs=whole(out_shape.shape),
        out_shape=out_shape,
        compiler_params=pltpu.CompilerParams(vmem_limit_bytes=12 * 1024 * 1024),
        cost_estimate=pl.CostEstimate(flops=0, bytes_accessed=12 * out_shape.size, transcendentals=0),
        name="own_quarters",
    )(*[right] * len(quarters), *extra, *others)


def pick(info, right, cols, even_parts, odd_parts, *others):
    sides = (even_parts, odd_parts)
    kb = right.shape[0]
    rows, width = quarter_shape(right)
    extra = [] if cols is None else [cols]

    def has_extra(part):
        return part[0] is not None and extra and part[0].shape[0] == rows + kb

    def size(part):
        return rows + kb if has_extra(part) else part[-1] * rows // PARTS

    def kernel(info_ref, *refs):
        out_ref = refs[-1]

        def copy_parts(side, refs_of):
            at = 0
            for part, ref in zip(sides[side], refs_of):
                if part[0] is None:
                    cut(ref, out_ref, part[1] // HALVES, at)
                else:
                    out_ref[at:at + size(part)] = ref[...]
                at += size(part)
            if at < out_ref.shape[0]:
                out_ref[at:] = jnp.zeros((out_ref.shape[0] - at, width), out_ref.dtype)
                if extra and sides[side][0][0] is None:
                    put_extra(out_ref, refs[len(even_parts) + len(odd_parts)], rows)

        pl.when(info_ref[0] == 0)(lambda: copy_parts(0, refs[:len(even_parts)]))
        pl.when(info_ref[0] != 0)(lambda: copy_parts(1, refs[len(even_parts):]))

    def spec(part):
        if part[0] is None:
            return own_spec(right, *part[1:])
        return pl.BlockSpec((size(part), width), lambda *_: (part[1], 0))

    parts = [*even_parts, *odd_parts]
    out_shape = jax.ShapeDtypeStruct((rows + kb * len(extra), width), right.dtype)
    return pl.pallas_call(
        kernel,
        grid=(1,),
        in_specs=[in_smem] + [spec(part) for part in parts] + [whole(x.shape) for x in extra] + [anywhere] * len(others),
        out_specs=whole(out_shape.shape),
        out_shape=out_shape,
        compiler_params=pltpu.CompilerParams(vmem_limit_bytes=8 * 1024 * 1024),
        cost_estimate=pl.CostEstimate(flops=0, bytes_accessed=8 * out_shape.size, transcendentals=0),
        name="pick",
    )(info, *[right if part[0] is None else part[0] for part in parts], *extra, *others)


def accumulate(info, places, lefts, chunks, totals, nc, finish=None):
    _, kb, lpb, bs, _ = lefts[0].shape
    part = kb // (HALVES * PARTS)
    own = totals is None
    bpr = chunks[0][0].shape[1] if own else HALVES * chunks[0][0].shape[1] // bs
    width = bpr * bs // HALVES
    lanes = bs // HALVES
    products = lpb * bpr
    turns = sorted({what[0] for _, _, both in chunks for what in both if what is not None})
    packed = nc // 4
    if own:
        touched = list(range(HALVES))
    else:
        touched = sorted({what[1] // HALVES for _, _, both in chunks for what in both if what is not None})
    sides = [(c, side) for c in range(len(chunks)) for side in range(2) if chunks[c][2][side] is not None]
    sides = [(c, side) for c, side in sides if side == 0 or chunks[c][2][0] != chunks[c][2][1]]

    def kernel(info_ref, *refs):
        place_refs = dict(zip(turns, refs))
        refs = refs[len(turns):]
        left_refs = dict(zip(sides, refs))
        right_refs = refs[len(sides):len(sides) + len(chunks)]
        outs = refs[len(sides) + len(chunks) + (0 if own else len(touched)):]
        total_refs = dict(zip(touched, outs))
        outs = outs[len(touched):]
        outs[0][...] = jnp.zeros_like(outs[0])
        odd = info_ref[0]
        if own:
            for ref in total_refs.values():
                ref[...] = jnp.zeros_like(ref)

        def products_of(left, right):
            left = left.reshape(lpb * bs, bs)
            left_high = left.astype(bf16)
            left_low = (left - left_high.astype(f32)).astype(bf16)
            high = right.astype(bf16)
            low = (right - high.astype(f32)).astype(bf16)
            return jnp.dot(
                jnp.concatenate([left_high, left_low, left_high], axis=1),
                jnp.concatenate([high, high, low], axis=0),
                preferred_element_type=f32,
            )

        def add_own(left_ref, right_ref):
            for k in range(kb):
                out = products_of(left_ref[0, k], jnp.concatenate([right_ref[k, b] for b in range(bpr)], axis=1))
                for a in range(lpb):
                    for b in range(bpr):
                        n = place_refs[0][k * products + a * bpr + b]
                        for half in range(HALVES):
                            at = slice(half * lanes, (half + 1) * lanes)
                            total_refs[half][n, :, at] += out[a * bs:(a + 1) * bs, b * bs:(b + 1) * bs][:, at]

        def add(c, side):
            turn, quarter, first, parts = chunks[c][2][side]
            half, k_half = divmod(quarter, HALVES)
            base = (k_half * PARTS + first) * part * products
            left_ref, right_ref, total_ref = left_refs[c, side], right_refs[c], total_refs[half]
            for k in range(parts * part):
                out = products_of(left_ref[0, k], right_ref[k * bs:(k + 1) * bs])
                for a in range(lpb):
                    for b in range(bpr):
                        n = place_refs[turn][base + k * products + a * bpr + b]
                        at = (b % HALVES) * lanes
                        total_ref[n, :, at:at + lanes] += out[a * bs:(a + 1) * bs, b * lanes:(b + 1) * lanes]

        if own:
            add_own(left_refs[0, 0], right_refs[0])
            return
        for c, (_, _, both) in enumerate(chunks):
            if both[0] == both[1]:
                add(c, 0)
                continue
            if both[0] is not None:
                pl.when(odd == 0)(lambda c=c: add(c, 0))
            if both[1] is not None:
                pl.when(odd != 0)(lambda c=c: add(c, 1))
        if finish is not None:
            lower = lower_lanes((bs, bs))
            for kept, ref in enumerate(outs[1:]):
                for p in range(packed):
                    n = 2 * packed * kept + p
                    one, two = total_refs[finish][n], total_refs[finish][n + packed]
                    ref[p] = jnp.where(lower, one + swap_lanes(one), two + swap_lanes(two))

    def left_spec(turn, quarter, first, parts):
        at = (quarter % HALVES * PARTS + first) // parts
        return pl.BlockSpec((1, parts * part, lpb, bs, bs), lambda g, info_ref, *_: (info_ref[1 + turn], at, 0, 0, 0))

    def right_spec(at, both):
        parts = max(what[3] for what in both if what is not None)
        return pl.BlockSpec((parts * part * bs, width), lambda *_: (at, 0))

    operands = [lefts[chunks[c][2][side][0]] for c, side in sides] + [c[0] for c in chunks]
    if own:
        in_specs = [pl.BlockSpec((1, kb, lpb, bs, bs), lambda g, info_ref, *_: (info_ref[1], 0, 0, 0, 0)), whole(chunks[0][0].shape)]
    else:
        in_specs = [left_spec(*chunks[c][2][side]) for c, side in sides] + [right_spec(at, both) for _, at, both in chunks]
    held = len(operands) + 1 + len(turns)
    if not own:
        operands += [totals[half] for half in touched]
        in_specs += [in_vmem] * len(touched)
    outs = [jax.ShapeDtypeStruct((nc + 1, bs, bs), f32)] * len(touched) + [jax.ShapeDtypeStruct((8, 128), jnp.int32)]
    if finish is not None:
        outs += [jax.ShapeDtypeStruct((packed, bs, bs), f32)] * 2
    parts = QUARTERS if own else len(chunks)
    per = kb // HALVES
    flops = parts * per * 2 * lpb * bs * 3 * bs * width
    moved = 4 * parts * per * (lpb * bs * bs + bs * width)
    results = pl.pallas_call(
        kernel,
        grid_spec=pltpu.PrefetchScalarGridSpec(
            num_scalar_prefetch=1 + len(turns),
            grid=(1,),
            in_specs=in_specs,
            out_specs=[in_vmem] * len(touched) + [whole(x.shape) for x in outs[len(touched):]],
        ),
        out_shape=outs,
        input_output_aliases={} if own else {held + n: n for n in range(len(touched))},
        compiler_params=pltpu.CompilerParams(vmem_limit_bytes=16 * 1024 * 1024),
        cost_estimate=pl.CostEstimate(flops=flops, bytes_accessed=moved, transcendentals=0),
        name="accumulate",
    )(info, *[places[turn] for turn in turns], *operands)
    totals = [None] * HALVES if own else list(totals)
    for half, total in zip(touched, results):
        totals[half] = total
    return (totals, *results[len(touched):])


def own_places(info, slots, rows, cols, kb, lpb):
    nc = slots.shape[0]
    bpr = cols.shape[0] // kb

    def kernel(info_ref, slots_ref, rows_ref, cols_ref, table_ref, out_ref):
        for code in range(CB * CB):
            table_ref[code] = nc
        behind = nc - nc // 2 * info_ref[1 + STEPS]
        for n in range(nc):
            table_ref[slots_ref[n]] = lax.rem(n + behind, nc)
        fill_places(info_ref[1], table_ref, rows_ref, lambda k, b: cols_ref[k * bpr + b], out_ref, kb, lpb, bpr)

    return pl.pallas_call(
        kernel,
        in_specs=[in_smem] * 4,
        out_specs=[in_smem] * 2,
        out_shape=[jax.ShapeDtypeStruct((CB * CB,), jnp.int32), jax.ShapeDtypeStruct((kb * lpb * bpr,), jnp.int32)],
        compiler_params=pltpu.CompilerParams(vmem_limit_bytes=1024 * 1024),
        name="own_places",
    )(info, slots, rows, cols)


def fill_places(panel, table_ref, rows_ref, col_of, out_ref, kb, lpb, bpr):
    def column(k, carry):
        cols = [col_of(k, b) for b in range(bpr)]
        for a in range(lpb):
            row = rows_ref[(panel * kb + k) * lpb + a] * CB
            for b in range(bpr):
                out_ref[(k * lpb + a) * bpr + b] = table_ref[row + cols[b]]
        return carry

    lax.fori_loop(0, kb, column, 0)


def panel_places(info, table, turn, rows, even_part, odd_part, kb, lpb, bpr):
    parts = (even_part, odd_part)

    def kernel(info_ref, table_ref, rows_ref, even_ref, odd_ref, out_ref, cols_ref, scalar_ref, sem):
        cols = jnp.where(info_ref[0] == 0, even_ref[...], odd_ref[...])
        cols_ref[...] = cols.astype(jnp.int32)
        copy = pltpu.make_async_copy(cols_ref, scalar_ref, sem)
        copy.start()
        copy.wait()
        fill_places(info_ref[1 + turn], table_ref, rows_ref, lambda k, b: scalar_ref[k, b], out_ref, kb, lpb, bpr)

    return pl.pallas_call(
        kernel,
        grid=(1,),
        in_specs=[in_smem] * 3 + [pl.BlockSpec((kb, 128), lambda g, at=at: (at // kb, 0)) for _, at in parts],
        out_specs=in_smem,
        out_shape=jax.ShapeDtypeStruct((kb * lpb * bpr,), jnp.int32),
        scratch_shapes=[pltpu.VMEM((kb, 128), jnp.int32), pltpu.SMEM((kb, 128), jnp.int32), pltpu.SemaphoreType.DMA],
        compiler_params=pltpu.CompilerParams(vmem_limit_bytes=1024 * 1024),
        name="panel_places",
    )(info, table, rows, *[array for array, _ in parts])


def combine(kept, other):
    packed, bs, _ = kept[0].shape
    steps = 2 if packed % 2 == 0 else 1
    per = packed // steps

    def kernel(kept_0, kept_1, other_0, other_1, out_ref):
        lower = lower_lanes((bs, bs))
        for p in range(per):
            left = kept_0[p] + other_0[p]
            right = kept_1[p] + other_1[p]
            out_ref[0, p] = jnp.where(lower, left, swap_lanes(right))
            out_ref[1, p] = jnp.where(lower, swap_lanes(left), right)

    return pl.pallas_call(
        kernel,
        grid=(steps,),
        in_specs=[pl.BlockSpec((per, bs, bs), lambda g: (g, 0, 0))] * 4,
        out_specs=pl.BlockSpec((2, per, bs, bs), lambda g: (0, g, 0, 0)),
        out_shape=jax.ShapeDtypeStruct((2, packed, bs, bs), f32),
        compiler_params=pltpu.CompilerParams(vmem_limit_bytes=8 * 1024 * 1024),
        name="combine",
    )(*kept, *other).reshape(2 * packed, bs, bs)


def shards(left_values, left_rows, right_values, right_cols, result_slots):
    rows_n, cols_n = (lax.axis_size(a) for a in ("row", "col"))
    row, col, rep = (lax.axis_index(a) for a in ("row", "col", "rep"))
    panels = left_values[0, 0, 0]
    panel_rows = left_rows.reshape(-1)
    right = right_values[0, 0, 0]
    right_places = right_cols.reshape(-1)
    slots = result_slots[0, 0]
    kb = right.shape[0]
    nc = slots.shape[0]
    place = [(col + turn) // cols_n for turn in range(STEPS)]
    info = jnp.stack([row % 2, *place, rep]).astype(jnp.int32)

    z_pairs = [(r, (r - 2) % rows_n) for r in range(rows_n)]
    x_pairs = [(r, r ^ 1) for r in range(rows_n)]

    def along_z(chunk):
        return lax.ppermute(chunk, "row", z_pairs)

    def along_x(chunk):
        return lax.ppermute(chunk, "row", x_pairs)

    rows, width = quarter_shape(right)
    cols = right_cols[0, 0, 0]

    def sent(even_parts, odd_parts, *others, extra=False):
        return pick(info, right, cols if extra else None, even_parts, odd_parts, *others)

    def all_of(array):
        return [(array, 0, PARTS)]

    def own_all(quarter):
        return [(None, quarter, 0, PARTS)]

    z = {}
    x = {}
    def own_part(quarter, first=0, parts=PARTS):
        return (quarter, first, parts)

    z[1] = along_z(own_quarters(right, [own_part(0)], cols))
    x[1] = along_x(own_quarters(right, [own_part(3), own_part(2, 0, 1)], None))

    shifts = sorted({turn % cols_n for turn in range(STEPS)})
    held = {
        shift: (panels, panel_rows) if shift == 0 else lax.ppermute((panels, panel_rows), "col", [(c, (c - shift) % cols_n) for c in range(cols_n)])
        for shift in shifts
    }
    lefts = [held[turn % cols_n][0] for turn in range(STEPS)]
    rows_at = [held[turn % cols_n][1] for turn in range(STEPS)]

    lpb, bpr = panels.shape[2], right.shape[1]
    places = {}
    table, places[0] = own_places(info, slots, panel_rows, right_places, kb, lpb)

    def read_places(turn, even_part, odd_part):
        places[turn] = panel_places(info, table, turn, rows_at[turn], even_part, odd_part, kb, lpb, bpr)

    def add(totals, chunks, finish=None):
        return accumulate(info, places, lefts, chunks, totals, nc, finish)

    def along_z_part(stage):
        return (z[stage], 0, Z_CHUNKS[stage])

    def along_x_part(stage):
        if stage == 2:
            return (x[1], PARTS, X_CHUNKS[stage])
        if stage == 8:
            return (x[7], 1, X_CHUNKS[stage])
        return (x[stage], 0, X_CHUNKS[stage])

    totals, done = accumulate(info, places, [panels] * STEPS, [(right, 0, ((0, 0), (0, 0)))], None, nc)
    second = own_quarters(right, [own_part(1)], None, done)
    z[2] = along_z(second)
    x[3] = along_x(sent(all_of(z[1]), own_all(0), done, extra=True))
    z[3] = along_z(own_quarters(right, [own_part(2)], None, z[1], x[1], done))
    read_places(2, (z[1], rows), (z[1], rows))
    totals, done = add(totals, [along_z_part(1), along_z_part(2)])
    x[4] = along_x(sent(all_of(z[2]), own_all(1), done))
    z[4] = along_z(sent(own_all(3), all_of(x[3]), done, extra=True))
    read_places(1, (x[3], rows), (x[3], rows))
    totals, done = add(totals, [along_x_part(1), along_x_part(2), along_x_part(3)])
    x[5] = along_x(sent(all_of(z[3]), all_of(z[1]), done, extra=True))
    z[5] = along_z(sent(all_of(x[1]), all_of(x[4]), done))
    totals, done = add(totals, [along_z_part(3), along_x_part(4)])
    x[6] = along_x(sent(all_of(z[4]), all_of(z[2]), done))
    z[6] = along_z(sent([(x[1], PARTS, 1)], all_of(x[5]), done))
    read_places(3, (x[5], rows), (z[4], rows))
    totals, done = add(totals, [along_z_part(4), along_x_part(5)])
    x[7] = along_x(sent(all_of(z[5]), [(z[3], 1, 1), (None, 2, 1, 1)], done))
    z[7] = along_z(x[6])
    totals, done = add(totals, [along_z_part(5)])

    def to_partner(blocks):
        return lax.ppermute(blocks, "rep", [(0, 1), (1, 0)])

    totals, done, kept_0, send_0 = add(totals, [along_x_part(6)], 0)
    other_0 = to_partner(send_0)
    totals, done = add(totals, [along_z_part(6), along_x_part(7), along_x_part(8)])
    totals, done, kept_1, send_1 = add(totals, [along_z_part(7)], 1)
    other_1 = to_partner(send_1)
    return combine((kept_0, kept_1), (other_0, other_1))[None, None]


def solution(mesh):
    in_specs = (
        P("row", "rep", "col", None, None, None, None, None),
        P("row", "rep", "col", None, None, None),
        P("rep", "row", "col", None, None, None, None),
        P("rep", "row", "col", None, None),
        P("row", "col", None),
    )
    out_specs = P("row", "col", "rep", None, None)
    return jax.shard_map(shards, mesh=mesh, in_specs=in_specs, out_specs=out_specs, check_vma=False)
```

```python
import jax
import jax.numpy as jnp
from jax import lax
from jax.experimental import pallas as pl
from jax.experimental.pallas import tpu as pltpu
from jax.sharding import PartitionSpec as P

STEPS = 4
CB = 8
HALVES = 2
QUARTERS = HALVES * HALVES

bf16 = jnp.bfloat16
f32 = jnp.float32

PARTS = 2
Z_CHUNKS = {
    1: ((2, 0, 0, 2), (2, 0, 0, 2)),
    2: ((2, 1, 0, 2), (2, 1, 0, 2)),
    3: ((2, 2, 0, 2), (2, 2, 0, 2)),
    4: ((2, 3, 0, 2), (3, 0, 0, 2)),
    5: ((3, 3, 0, 2), (3, 1, 0, 2)),
    6: ((3, 2, 0, 1), (3, 2, 0, 2)),
    7: (None, (3, 3, 0, 2)),
}
X_CHUNKS = {
    1: ((1, 3, 0, 2), None),
    2: ((1, 2, 0, 1), None),
    3: ((1, 0, 0, 2), (1, 0, 0, 2)),
    4: ((1, 1, 0, 2), (1, 1, 0, 2)),
    5: ((3, 0, 0, 2), (1, 2, 0, 2)),
    6: ((3, 1, 0, 2), (1, 3, 0, 2)),
    7: ((3, 2, 1, 1), (2, 3, 0, 2)),
    8: ((1, 2, 1, 1), None),
}

in_smem = pl.BlockSpec(memory_space=pltpu.SMEM)
in_vmem = pl.BlockSpec(memory_space=pltpu.VMEM)
anywhere = pl.BlockSpec(memory_space=pl.ANY)


def whole(shape):
    return pl.BlockSpec(shape, lambda *_: (0,) * len(shape))


def lower_lanes(shape):
    return lax.broadcasted_iota(jnp.int32, shape, len(shape) - 1) < shape[-1] // 2


def swap_lanes(x):
    return pltpu.roll(x, x.shape[-1] // 2, x.ndim - 1)


def move_lanes(x, groups):
    if groups % 4 == 0:
        return x
    return pltpu.roll(x, x.shape[-1] // 4 * (groups % 4), x.ndim - 1)


def by_group(parts):
    shape = parts[0].shape
    group = lax.broadcasted_iota(jnp.int32, shape, len(shape) - 1) // (shape[-1] // 4)
    out = parts[3]
    for g in (2, 1, 0):
        out = jnp.where(group == g, parts[g], out)
    return out


def sum_of(quarter):
    return max(quarter - 1, 0)


def block_rows(kb, quarter, first, parts):
    if quarter < 2:
        per = kb // (2 * PARTS)
        return (quarter * PARTS + first) * per, parts * per
    per = kb // PARTS
    return first * per, parts * per


def cut(right_ref, out_ref, quarter, at=0, start=0, count=None):
    count = right_ref.shape[0] if count is None else count
    _, bpr, bs, _ = right_ref.shape
    lower = lower_lanes((bs, bs))
    for n in range(count):
        blocks = [right_ref[start + n, b] for b in range(bpr)]
        if quarter < 2:
            for pair in range(bpr // 2):
                both = jnp.where(lower, blocks[2 * pair], swap_lanes(blocks[2 * pair + 1]))
                out_ref[at + n * bs:at + (n + 1) * bs, pair * bs:(pair + 1) * bs] = both
        else:
            row = at + n // 2 * bs
            four = by_group([move_lanes(block, b - quarter) for b, block in enumerate(blocks)])
            out_ref[row:row + bs, n % 2 * bs:(n % 2 + 1) * bs] = four


def own_spec(right, quarter, first=0, parts=PARTS):
    start, count = block_rows(right.shape[0], quarter, first, parts)
    return pl.BlockSpec((count,) + right.shape[1:], lambda *_: (start // count, 0, 0, 0))


def quarter_shape(right):
    kb, bpr, bs, _ = right.shape
    return kb // HALVES * bs, bpr * bs // HALVES


def put_extra(out_ref, cols_ref, rows):
    kb, bpr = cols_ref.shape
    out_ref[rows:rows + kb, :bpr] = cols_ref[...].astype(out_ref.dtype)


def own_quarters(right, quarters, cols, *others):
    rows, width = quarter_shape(right)
    extra = [] if cols is None else [cols]
    several = len(quarters) > 1
    starts = [sum(parts for _, _, parts in quarters[:n]) * rows // PARTS for n in range(len(quarters) + 1)]

    def kernel(*refs):
        out_ref = refs[-1]
        for n, part in enumerate(quarters):
            start, count = block_rows(right.shape[0], *part)
            cut(refs[0], out_ref, part[0], starts[n], start if several else 0, count)
        if extra:
            put_extra(out_ref, refs[1], starts[-1])

    out_shape = jax.ShapeDtypeStruct((starts[-1] + right.shape[0] * len(extra), width), right.dtype)
    return pl.pallas_call(
        kernel,
        grid=(1,),
        in_specs=[whole(right.shape) if several else own_spec(right, *quarters[0])] + [whole(x.shape) for x in extra] + [anywhere] * len(others),
        out_specs=whole(out_shape.shape),
        out_shape=out_shape,
        compiler_params=pltpu.CompilerParams(vmem_limit_bytes=12 * 1024 * 1024),
        cost_estimate=pl.CostEstimate(flops=0, bytes_accessed=12 * out_shape.size, transcendentals=0),
        name="own_quarters",
    )(right, *extra, *others)


def pick(info, right, cols, even_parts, odd_parts, *others):
    sides = (even_parts, odd_parts)
    kb = right.shape[0]
    rows, width = quarter_shape(right)
    extra = [] if cols is None else [cols]

    def has_extra(part):
        return part[0] is not None and extra and part[0].shape[0] == rows + kb

    def size(part):
        return rows + kb if has_extra(part) else part[-1] * rows // PARTS

    def kernel(info_ref, *refs):
        out_ref = refs[-1]

        def copy_parts(side, refs_of):
            at = 0
            for part, ref in zip(sides[side], refs_of):
                if part[0] is None:
                    cut(ref, out_ref, part[1], at)
                else:
                    out_ref[at:at + size(part)] = ref[...]
                at += size(part)
            if at < out_ref.shape[0]:
                out_ref[at:] = jnp.zeros((out_ref.shape[0] - at, width), out_ref.dtype)
                if extra and sides[side][0][0] is None:
                    put_extra(out_ref, refs[len(even_parts) + len(odd_parts)], rows)

        pl.when(info_ref[0] == 0)(lambda: copy_parts(0, refs[:len(even_parts)]))
        pl.when(info_ref[0] != 0)(lambda: copy_parts(1, refs[len(even_parts):]))

    def spec(part):
        if part[0] is None:
            return own_spec(right, *part[1:])
        return pl.BlockSpec((size(part), width), lambda *_: (part[1], 0))

    parts = [*even_parts, *odd_parts]
    out_shape = jax.ShapeDtypeStruct((rows + kb * len(extra), width), right.dtype)
    return pl.pallas_call(
        kernel,
        grid=(1,),
        in_specs=[in_smem] + [spec(part) for part in parts] + [whole(x.shape) for x in extra] + [anywhere] * len(others),
        out_specs=whole(out_shape.shape),
        out_shape=out_shape,
        compiler_params=pltpu.CompilerParams(vmem_limit_bytes=8 * 1024 * 1024),
        cost_estimate=pl.CostEstimate(flops=0, bytes_accessed=8 * out_shape.size, transcendentals=0),
        name="pick",
    )(info, *[right if part[0] is None else part[0] for part in parts], *extra, *others)


def accumulate(info, places, lefts, chunks, totals, nc, finish=None, cost=1):
    _, kb, lpb, bs, _ = lefts[0].shape
    own = totals is None
    bpr = chunks[0][0].shape[1] if own else HALVES * chunks[0][0].shape[1] // bs
    width = bpr * bs // HALVES
    products = lpb * bpr
    turns = sorted({what[0] for _, _, both in chunks for what in both if what is not None})
    if own:
        touched = list(range(3))
    else:
        touched = {sum_of(what[1]) for _, _, both in chunks for what in both if what is not None}
        touched = sorted(touched | set(finish or ()))
    sides = [(c, side) for c in range(len(chunks)) for side in range(2) if chunks[c][2][side] is not None]
    sides = [(c, side) for c, side in sides if side == 0 or chunks[c][2][0] != chunks[c][2][1]]

    def kernel(info_ref, *refs):
        place_refs = dict(zip(turns, refs))
        refs = refs[len(turns):]
        left_refs = dict(zip(sides, refs))
        right_refs = refs[len(sides):len(sides) + len(chunks)]
        outs = refs[len(sides) + len(chunks) + (0 if own else len(touched)):]
        total_refs = dict(zip(touched, outs))
        outs = outs[len(touched):]
        outs[0][...] = jnp.zeros_like(outs[0])
        odd = info_ref[0]
        if own:
            for ref in total_refs.values():
                ref[...] = jnp.zeros_like(ref)

        def products_of(left, right):
            left = left.reshape(lpb * bs, bs)
            left_high = left.astype(bf16)
            left_low = (left - left_high.astype(f32)).astype(bf16)
            high = right.astype(bf16)
            low = (right - high.astype(f32)).astype(bf16)
            return jnp.dot(
                jnp.concatenate([left_high, left_low, left_high], axis=1),
                jnp.concatenate([high, high, low], axis=0),
                preferred_element_type=f32,
            )

        def add_own(left_ref, right_ref):
            parts = (slice(0, bs // 2), slice(bs // 2, 3 * bs // 4), slice(3 * bs // 4, bs))
            for k in range(kb):
                out = products_of(left_ref[0, k], jnp.concatenate([right_ref[k, b] for b in range(bpr)], axis=1))
                for a in range(lpb):
                    for b in range(bpr):
                        n = place_refs[0][k * products + a * bpr + b]
                        block = out[a * bs:(a + 1) * bs, b * bs:(b + 1) * bs]
                        for ref, lanes in zip(total_refs.values(), parts):
                            ref[n, :, lanes] += block[:, lanes]

        def add(c, side):
            turn, quarter = chunks[c][2][side][:2]
            start, count = block_rows(kb, *chunks[c][2][side][1:])
            left_ref, right_ref, total_ref = left_refs[c, side], right_refs[c], total_refs[sum_of(quarter)]
            lanes = bs // 2 if quarter < 2 else bs // 4
            for k in range(count):
                if quarter < 2:
                    right = right_ref[k * bs:(k + 1) * bs]
                else:
                    right = right_ref[k // 2 * bs:(k // 2 + 1) * bs, k % 2 * bs:(k % 2 + 1) * bs]
                out = products_of(left_ref[0, k], right)
                for a in range(lpb):
                    for b in range(bpr):
                        n = place_refs[turn][(start + k) * products + a * bpr + b]
                        at = b * lanes % bs
                        total_ref[n, :, at:at + lanes] += out[a * bs:(a + 1) * bs, b * lanes:(b + 1) * lanes]

        def pack(total_ref, both_refs, quarters):
            for kept, ref in enumerate(both_refs):
                packed = ref.shape[0]
                for p in range(packed):
                    blocks = [total_ref[nc // 2 * kept + g * packed + p] for g in range(4 if quarters else 2)]
                    blocks = [block + swap_lanes(block) for block in blocks]
                    if quarters:
                        ref[p] = by_group([block + move_lanes(block, 1) for block in blocks])
                    else:
                        ref[p] = jnp.where(lower_lanes((bs, bs)), *blocks)

        if own:
            add_own(left_refs[0, 0], right_refs[0])
            return
        for c, (_, _, both) in enumerate(chunks):
            if both[0] == both[1]:
                add(c, 0)
                continue
            if both[0] is not None:
                pl.when(odd == 0)(lambda c=c: add(c, 0))
            if both[1] is not None:
                pl.when(odd != 0)(lambda c=c: add(c, 1))
        if finish is not None and finish[0] == finish[1]:
            pack(total_refs[finish[0]], outs[1:], finish[0] > 0)
        elif finish is not None:
            pl.when(odd == 0)(lambda: pack(total_refs[finish[0]], outs[1:], True))
            pl.when(odd != 0)(lambda: pack(total_refs[finish[1]], outs[1:], True))

    def left_spec(turn, *what):
        start, count = block_rows(kb, *what)
        return pl.BlockSpec((1, count, lpb, bs, bs), lambda g, info_ref, *_: (info_ref[1 + turn], start // count, 0, 0, 0))

    def right_spec(array, at, both):
        parts = max(what[3] for what in both if what is not None)
        rows = kb // HALVES * bs // PARTS * parts
        return pl.BlockSpec((rows, width), lambda *_: (at, 0))

    operands = [lefts[chunks[c][2][side][0]] for c, side in sides] + [c[0] for c in chunks]
    if own:
        in_specs = [pl.BlockSpec((1, kb, lpb, bs, bs), lambda g, info_ref, *_: (info_ref[1], 0, 0, 0, 0)), whole(chunks[0][0].shape)]
    else:
        in_specs = [left_spec(*chunks[c][2][side]) for c, side in sides] + [right_spec(*chunk) for chunk in chunks]
    held = len(operands) + 1 + len(turns)
    if not own:
        operands += [totals[n] for n in touched]
        in_specs += [in_vmem] * len(touched)
    outs = [jax.ShapeDtypeStruct((nc + 1, bs, bs), f32)] * len(touched) + [jax.ShapeDtypeStruct((8, 128), jnp.int32)]
    if finish is not None:
        outs += [jax.ShapeDtypeStruct((nc // (8 if finish[0] else 4), bs, bs), f32)] * 2
    parts = QUARTERS if own else len(chunks)
    per = kb // HALVES
    flops = parts * per * 2 * lpb * bs * 3 * bs * width
    moved = 4 * parts * per * (lpb * bs * bs + bs * width)
    results = pl.pallas_call(
        kernel,
        grid_spec=pltpu.PrefetchScalarGridSpec(
            num_scalar_prefetch=1 + len(turns),
            grid=(1,),
            in_specs=in_specs,
            out_specs=[in_vmem] * len(touched) + [whole(x.shape) for x in outs[len(touched):]],
        ),
        out_shape=outs,
        input_output_aliases={} if own else {held + n: n for n in range(len(touched))},
        compiler_params=pltpu.CompilerParams(vmem_limit_bytes=20 * 1024 * 1024),
        cost_estimate=pl.CostEstimate(flops=cost * flops, bytes_accessed=cost * moved, transcendentals=0),
        name="accumulate",
    )(info, *[places[turn] for turn in turns], *operands)
    totals = [None] * 3 if own else list(totals)
    for n, total in zip(touched, results):
        totals[n] = total
    return (totals, *results[len(touched):])


def own_places(info, slots, rows, cols, kb, lpb):
    nc = slots.shape[0]
    bpr = cols.shape[0] // kb

    def kernel(info_ref, slots_ref, rows_ref, cols_ref, table_ref, out_ref):
        for code in range(CB * CB):
            table_ref[code] = nc
        behind = nc - nc // 2 * info_ref[1 + STEPS]
        for n in range(nc):
            table_ref[slots_ref[n]] = lax.rem(n + behind, nc)
        fill_places(info_ref[1], table_ref, rows_ref, lambda k, b: cols_ref[k * bpr + b], out_ref, kb, lpb, bpr)

    return pl.pallas_call(
        kernel,
        in_specs=[in_smem] * 4,
        out_specs=[in_smem] * 2,
        out_shape=[jax.ShapeDtypeStruct((CB * CB,), jnp.int32), jax.ShapeDtypeStruct((kb * lpb * bpr,), jnp.int32)],
        compiler_params=pltpu.CompilerParams(vmem_limit_bytes=1024 * 1024),
        name="own_places",
    )(info, slots, rows, cols)


def fill_places(panel, table_ref, rows_ref, col_of, out_ref, kb, lpb, bpr):
    def column(k, carry):
        cols = [col_of(k, b) for b in range(bpr)]
        for a in range(lpb):
            row = rows_ref[(panel * kb + k) * lpb + a] * CB
            for b in range(bpr):
                out_ref[(k * lpb + a) * bpr + b] = table_ref[row + cols[b]]
        return carry

    lax.fori_loop(0, kb, column, 0)


def panel_places(info, table, turn, rows, even_part, odd_part, kb, lpb, bpr):
    parts = (even_part, odd_part)

    def kernel(info_ref, table_ref, rows_ref, even_ref, odd_ref, out_ref, cols_ref, scalar_ref, sem):
        cols = jnp.where(info_ref[0] == 0, even_ref[...], odd_ref[...])
        cols_ref[...] = cols.astype(jnp.int32)
        copy = pltpu.make_async_copy(cols_ref, scalar_ref, sem)
        copy.start()
        copy.wait()
        fill_places(info_ref[1 + turn], table_ref, rows_ref, lambda k, b: scalar_ref[k, b], out_ref, kb, lpb, bpr)

    return pl.pallas_call(
        kernel,
        grid=(1,),
        in_specs=[in_smem] * 3 + [pl.BlockSpec((kb, 128), lambda g, at=at: (at // kb, 0)) for _, at in parts],
        out_specs=in_smem,
        out_shape=jax.ShapeDtypeStruct((kb * lpb * bpr,), jnp.int32),
        scratch_shapes=[pltpu.VMEM((kb, 128), jnp.int32), pltpu.SMEM((kb, 128), jnp.int32), pltpu.SemaphoreType.DMA],
        compiler_params=pltpu.CompilerParams(vmem_limit_bytes=1024 * 1024),
        name="panel_places",
    )(info, table, rows, *[array for array, _ in parts])


def combine(info, kept, other):
    packed, bs, _ = kept[0].shape
    packed_4 = kept[1].shape[0]

    def kernel(info_ref, *refs):
        out_ref = refs[-1]
        even = info_ref[0] == 0
        lower = lower_lanes((bs, bs))
        halves = [refs[0][p] + refs[3][p] for p in range(packed)]
        early = [refs[1][p] + refs[4][p] for p in range(packed_4)]
        late = [refs[2][p] + refs[5][p] for p in range(packed_4)]
        thirds = [jnp.where(even, x, y) for x, y in zip(late, early)]
        fourths = [jnp.where(even, x, y) for x, y in zip(early, late)]
        for p in range(2 * packed):
            low = halves[p % packed]
            low = low if p < packed else swap_lanes(low)
            group = p // packed_4
            third = move_lanes(thirds[p % packed_4], 2 - group)
            fourth = move_lanes(fourths[p % packed_4], 3 - group)
            out_ref[p] = by_group([low, low, third, fourth])

    return pl.pallas_call(
        kernel,
        grid=(1,),
        in_specs=[in_smem] + [whole(x.shape) for x in (*kept, *other)],
        out_specs=whole((2 * packed, bs, bs)),
        out_shape=jax.ShapeDtypeStruct((2 * packed, bs, bs), f32),
        compiler_params=pltpu.CompilerParams(vmem_limit_bytes=8 * 1024 * 1024),
        name="combine",
    )(info, *kept, *other)


def shards(left_values, left_rows, right_values, right_cols, result_slots):
    rows_n, cols_n = (lax.axis_size(a) for a in ("row", "col"))
    row, col, rep = (lax.axis_index(a) for a in ("row", "col", "rep"))
    panels = left_values[0, 0, 0]
    panel_rows = left_rows.reshape(-1)
    right = right_values[0, 0, 0]
    right_places = right_cols.reshape(-1)
    slots = result_slots[0, 0]
    kb = right.shape[0]
    nc = slots.shape[0]
    place = [(col + turn) // cols_n for turn in range(STEPS)]
    info = jnp.stack([row % 2, *place, rep]).astype(jnp.int32)

    z_pairs = [(r, (r - 2) % rows_n) for r in range(rows_n)]
    x_pairs = [(r, r ^ 1) for r in range(rows_n)]

    def along_z(chunk):
        return lax.ppermute(chunk, "row", z_pairs)

    def along_x(chunk):
        return lax.ppermute(chunk, "row", x_pairs)

    rows, width = quarter_shape(right)
    cols = right_cols[0, 0, 0]

    def sent(even_parts, odd_parts, *others, extra=False):
        return pick(info, right, cols if extra else None, even_parts, odd_parts, *others)

    def all_of(array):
        return [(array, 0, PARTS)]

    def own_all(quarter):
        return [(None, quarter, 0, PARTS)]

    z = {}
    x = {}
    def own_part(quarter, first=0, parts=PARTS):
        return (quarter, first, parts)

    z[1] = along_z(own_quarters(right, [own_part(0)], cols))
    x[1] = along_x(own_quarters(right, [own_part(3), own_part(2, 0, 1)], None))

    shifts = sorted({turn % cols_n for turn in range(STEPS)})
    held = {
        shift: (panels, panel_rows) if shift == 0 else lax.ppermute((panels, panel_rows), "col", [(c, (c - shift) % cols_n) for c in range(cols_n)])
        for shift in shifts
    }
    lefts = [held[turn % cols_n][0] for turn in range(STEPS)]
    rows_at = [held[turn % cols_n][1] for turn in range(STEPS)]

    lpb, bpr = panels.shape[2], right.shape[1]
    places = {}
    table, places[0] = own_places(info, slots, panel_rows, right_places, kb, lpb)

    def read_places(turn, even_part, odd_part):
        places[turn] = panel_places(info, table, turn, rows_at[turn], even_part, odd_part, kb, lpb, bpr)

    def add(totals, chunks, finish=None, cost=1):
        return accumulate(info, places, lefts, chunks, totals, nc, finish, cost)

    def along_z_part(stage):
        return (z[stage], 0, Z_CHUNKS[stage])

    def along_x_part(stage):
        if stage == 2:
            return (x[1], PARTS, X_CHUNKS[stage])
        if stage == 8:
            return (x[7], 1, X_CHUNKS[stage])
        return (x[stage], 0, X_CHUNKS[stage])

    totals, done = accumulate(info, places, [panels] * STEPS, [(right, 0, ((0, 0), (0, 0)))], None, nc)
    second = own_quarters(right, [own_part(1)], None, done)
    z[2] = along_z(second)
    x[3] = along_x(sent(all_of(z[1]), own_all(0), done, extra=True))
    z[3] = along_z(own_quarters(right, [own_part(2)], None, z[1], x[1], done))
    read_places(2, (z[1], rows), (z[1], rows))
    totals, done = add(totals, [along_z_part(1), along_z_part(2)])
    x[4] = along_x(sent(all_of(z[2]), own_all(1), done))
    z[4] = along_z(sent(own_all(3), all_of(x[3]), done, extra=True))
    read_places(1, (x[3], rows), (x[3], rows))
    totals, done = add(totals, [along_x_part(1), along_x_part(2), along_x_part(3)])
    x[5] = along_x(sent(all_of(z[3]), all_of(z[1]), done, extra=True))
    z[5] = along_z(sent(all_of(x[1]), all_of(x[4]), done))
    totals, done = add(totals, [along_z_part(3), along_x_part(4)])
    x[6] = along_x(sent(all_of(z[4]), all_of(z[2]), done))
    z[6] = along_z(sent([(x[1], PARTS, 1)], all_of(x[5]), done))
    read_places(3, (x[5], rows), (z[4], rows))
    totals, done = add(totals, [along_z_part(4), along_x_part(5)])
    x[7] = along_x(sent(all_of(z[5]), [(z[3], 1, 1), (None, 2, 1, 1)], done))
    totals, done = add(totals, [along_z_part(5)])
    z[7] = along_z(sent(all_of(x[6]), all_of(x[6]), done))

    def to_partner(blocks):
        return lax.ppermute(blocks, "rep", [(0, 1), (1, 0)])

    totals, done, *both_0 = add(totals, [along_x_part(6)], (0, 0))
    other_0 = to_partner(both_0[1])
    totals, done, *both_1 = add(totals, [along_z_part(6)], (2, 1))
    other_1 = to_partner(both_1[1])
    totals, done = add(totals, [along_x_part(7), along_x_part(8)], cost=0)
    totals, done, *both_2 = add(totals, [along_z_part(7)], (1, 2), 0)
    other_2 = to_partner(both_2[1])
    return combine(info, [both_0[0], both_1[0], both_2[0]], [other_0, other_1, other_2])[None, None]


def solution(mesh):
    in_specs = (
        P("row", "rep", "col", None, None, None, None, None),
        P("row", "rep", "col", None, None, None),
        P("rep", "row", "col", None, None, None, None),
        P("rep", "row", "col", None, None),
        P("row", "col", None),
    )
    out_specs = P("row", "col", "rep", None, None)
    return jax.shard_map(shards, mesh=mesh, in_specs=in_specs, out_specs=out_specs, check_vma=False)
```

```python
import jax
import jax.numpy as jnp
from jax import lax
from jax.experimental import pallas as pl
from jax.experimental.pallas import tpu as pltpu
from jax.sharding import PartitionSpec as P

STEPS = 4
CB = 8
HALVES = 2
QUARTERS = HALVES * HALVES

bf16 = jnp.bfloat16
f32 = jnp.float32

PARTS = 2
Z_CHUNKS = {
    1: ((2, 0, 0, 2), (2, 0, 0, 2)),
    2: ((2, 1, 0, 2), (2, 1, 0, 2)),
    3: ((2, 2, 0, 2), (2, 2, 0, 2)),
    4: ((2, 3, 0, 2), (3, 0, 0, 2)),
    5: ((3, 3, 0, 2), (3, 1, 0, 2)),
    6: ((3, 2, 0, 1), (3, 2, 0, 2)),
    7: (None, (3, 3, 0, 2)),
}
X_CHUNKS = {
    1: ((1, 3, 0, 2), None),
    2: ((1, 2, 0, 1), None),
    3: ((1, 0, 0, 2), (1, 0, 0, 2)),
    4: ((1, 1, 0, 2), (1, 1, 0, 2)),
    5: ((3, 0, 0, 2), (1, 2, 0, 2)),
    6: ((3, 1, 0, 2), (1, 3, 0, 2)),
    7: ((3, 2, 1, 1), (2, 3, 0, 2)),
    8: ((1, 2, 1, 1), None),
}

in_smem = pl.BlockSpec(memory_space=pltpu.SMEM)
in_vmem = pl.BlockSpec(memory_space=pltpu.VMEM)
anywhere = pl.BlockSpec(memory_space=pl.ANY)


def whole(shape):
    return pl.BlockSpec(shape, lambda *_: (0,) * len(shape))


def lower_lanes(shape):
    return lax.broadcasted_iota(jnp.int32, shape, len(shape) - 1) < shape[-1] // 2


def swap_lanes(x):
    return pltpu.roll(x, x.shape[-1] // 2, x.ndim - 1)


def move_lanes(x, groups):
    if groups % 4 == 0:
        return x
    return pltpu.roll(x, x.shape[-1] // 4 * (groups % 4), x.ndim - 1)


def by_group(parts):
    shape = parts[0].shape
    group = lax.broadcasted_iota(jnp.int32, shape, len(shape) - 1) // (shape[-1] // 4)
    out = parts[3]
    for g in (2, 1, 0):
        out = jnp.where(group == g, parts[g], out)
    return out


def sum_of(quarter):
    return max(quarter - 1, 0)


def block_rows(kb, quarter, first, parts):
    if quarter < 2:
        per = kb // (2 * PARTS)
        return (quarter * PARTS + first) * per, parts * per
    per = kb // PARTS
    return first * per, parts * per


def cut(right_ref, out_ref, quarter, at=0, start=0, count=None):
    count = right_ref.shape[0] if count is None else count
    _, bpr, bs, _ = right_ref.shape
    lower = lower_lanes((bs, bs))
    for n in range(count):
        blocks = [right_ref[start + n, b] for b in range(bpr)]
        if quarter < 2:
            for pair in range(bpr // 2):
                both = jnp.where(lower, blocks[2 * pair], swap_lanes(blocks[2 * pair + 1]))
                out_ref[at + n * bs:at + (n + 1) * bs, pair * bs:(pair + 1) * bs] = both
        else:
            row = at + n // 2 * bs
            four = by_group([move_lanes(block, b - quarter) for b, block in enumerate(blocks)])
            out_ref[row:row + bs, n % 2 * bs:(n % 2 + 1) * bs] = four


def own_spec(right, quarter, first=0, parts=PARTS):
    start, count = block_rows(right.shape[0], quarter, first, parts)
    return pl.BlockSpec((count,) + right.shape[1:], lambda *_: (start // count, 0, 0, 0))


def quarter_shape(right):
    kb, bpr, bs, _ = right.shape
    return kb // HALVES * bs, bpr * bs // HALVES


def put_extra(out_ref, cols_ref, rows):
    bpr, kb = cols_ref.shape
    out_ref[rows:rows + bpr, :kb] = cols_ref[...].astype(out_ref.dtype)


def own_quarters(right, quarters, cols, *others):
    rows, width = quarter_shape(right)
    extra = [] if cols is None else [cols]
    several = len(quarters) > 1
    starts = [sum(parts for _, _, parts in quarters[:n]) * rows // PARTS for n in range(len(quarters) + 1)]

    def kernel(*refs):
        out_ref = refs[-1]
        for n, part in enumerate(quarters):
            start, count = block_rows(right.shape[0], *part)
            cut(refs[0], out_ref, part[0], starts[n], start if several else 0, count)
        if extra:
            put_extra(out_ref, refs[1], starts[-1])

    out_shape = jax.ShapeDtypeStruct((starts[-1] + right.shape[0] * len(extra), width), right.dtype)
    return pl.pallas_call(
        kernel,
        grid=(1,),
        in_specs=[whole(right.shape) if several else own_spec(right, *quarters[0])] + [whole(x.shape) for x in extra] + [anywhere] * len(others),
        out_specs=whole(out_shape.shape),
        out_shape=out_shape,
        compiler_params=pltpu.CompilerParams(vmem_limit_bytes=12 * 1024 * 1024),
        cost_estimate=pl.CostEstimate(flops=0, bytes_accessed=12 * out_shape.size, transcendentals=0),
        name="own_quarters",
    )(right, *extra, *others)


def pick(info, right, cols, even_parts, odd_parts, *others):
    sides = (even_parts, odd_parts)
    kb = right.shape[0]
    rows, width = quarter_shape(right)
    extra = [] if cols is None else [cols]

    def has_extra(part):
        return part[0] is not None and extra and part[0].shape[0] == rows + kb

    def size(part):
        return rows + kb if has_extra(part) else part[-1] * rows // PARTS

    def kernel(info_ref, *refs):
        out_ref = refs[-1]

        def copy_parts(side, refs_of):
            at = 0
            for part, ref in zip(sides[side], refs_of):
                if part[0] is None:
                    cut(ref, out_ref, part[1], at)
                else:
                    out_ref[at:at + size(part)] = ref[...]
                at += size(part)
            if at < out_ref.shape[0]:
                out_ref[at:] = jnp.zeros((out_ref.shape[0] - at, width), out_ref.dtype)
                if extra and sides[side][0][0] is None:
                    put_extra(out_ref, refs[len(even_parts) + len(odd_parts)], rows)

        pl.when(info_ref[0] == 0)(lambda: copy_parts(0, refs[:len(even_parts)]))
        pl.when(info_ref[0] != 0)(lambda: copy_parts(1, refs[len(even_parts):]))

    def spec(part):
        if part[0] is None:
            return own_spec(right, *part[1:])
        return pl.BlockSpec((size(part), width), lambda *_: (part[1], 0))

    parts = [*even_parts, *odd_parts]
    out_shape = jax.ShapeDtypeStruct((rows + kb * len(extra), width), right.dtype)
    return pl.pallas_call(
        kernel,
        grid=(1,),
        in_specs=[in_smem] + [spec(part) for part in parts] + [whole(x.shape) for x in extra] + [anywhere] * len(others),
        out_specs=whole(out_shape.shape),
        out_shape=out_shape,
        compiler_params=pltpu.CompilerParams(vmem_limit_bytes=8 * 1024 * 1024),
        cost_estimate=pl.CostEstimate(flops=0, bytes_accessed=8 * out_shape.size, transcendentals=0),
        name="pick",
    )(info, *[right if part[0] is None else part[0] for part in parts], *extra, *others)


def accumulate(info, places, lefts, chunks, totals, nc, finish=None, cost=1):
    _, kb, lpb, bs, _ = lefts[0].shape
    own = totals is None
    bpr = chunks[0][0].shape[1] if own else HALVES * chunks[0][0].shape[1] // bs
    width = bpr * bs // HALVES
    products = lpb * bpr
    turns = sorted({what[0] for _, _, both in chunks for what in both if what is not None})
    if own:
        touched = list(range(3))
    else:
        touched = {sum_of(what[1]) for _, _, both in chunks for what in both if what is not None}
        touched = sorted(touched | set(finish or ()))
    sides = [(c, side) for c in range(len(chunks)) for side in range(2) if chunks[c][2][side] is not None]
    sides = [(c, side) for c, side in sides if side == 0 or chunks[c][2][0] != chunks[c][2][1]]

    def kernel(info_ref, *refs):
        place_refs = dict(zip(turns, refs))
        refs = refs[len(turns):]
        left_refs = dict(zip(sides, refs))
        right_refs = refs[len(sides):len(sides) + len(chunks)]
        outs = refs[len(sides) + len(chunks) + (0 if own else len(touched)):]
        total_refs = dict(zip(touched, outs))
        outs = outs[len(touched):]
        outs[0][...] = jnp.zeros_like(outs[0])
        odd = info_ref[0]
        if own:
            for ref in total_refs.values():
                ref[...] = jnp.zeros_like(ref)

        def products_of(left, right):
            left = left.reshape(lpb * bs, bs)
            left_high = left.astype(bf16)
            left_low = (left - left_high.astype(f32)).astype(bf16)
            high = right.astype(bf16)
            low = (right - high.astype(f32)).astype(bf16)
            return jnp.dot(
                jnp.concatenate([left_high, left_low, left_high], axis=1),
                jnp.concatenate([high, high, low], axis=0),
                preferred_element_type=f32,
            )

        def add_own(left_ref, right_ref):
            parts = (slice(0, bs // 2), slice(bs // 2, 3 * bs // 4), slice(3 * bs // 4, bs))
            for k in range(kb):
                out = products_of(left_ref[0, k], jnp.concatenate([right_ref[k, b] for b in range(bpr)], axis=1))
                for a in range(lpb):
                    for b in range(bpr):
                        n = place_refs[0][k * products + a * bpr + b]
                        block = out[a * bs:(a + 1) * bs, b * bs:(b + 1) * bs]
                        for ref, lanes in zip(total_refs.values(), parts):
                            ref[n, :, lanes] += block[:, lanes]

        def add(c, side):
            turn, quarter = chunks[c][2][side][:2]
            start, count = block_rows(kb, *chunks[c][2][side][1:])
            left_ref, right_ref, total_ref = left_refs[c, side], right_refs[c], total_refs[sum_of(quarter)]
            lanes = bs // 2 if quarter < 2 else bs // 4
            for k in range(count):
                if quarter < 2:
                    right = right_ref[k * bs:(k + 1) * bs]
                else:
                    right = right_ref[k // 2 * bs:(k // 2 + 1) * bs, k % 2 * bs:(k % 2 + 1) * bs]
                out = products_of(left_ref[0, k], right)
                for a in range(lpb):
                    for b in range(bpr):
                        n = place_refs[turn][(start + k) * products + a * bpr + b]
                        at = b * lanes % bs
                        total_ref[n, :, at:at + lanes] += out[a * bs:(a + 1) * bs, b * lanes:(b + 1) * lanes]

        def pack(total_ref, both_refs, quarters):
            for kept, ref in enumerate(both_refs):
                packed = ref.shape[0]
                for p in range(packed):
                    blocks = [total_ref[nc // 2 * kept + g * packed + p] for g in range(4 if quarters else 2)]
                    blocks = [block + swap_lanes(block) for block in blocks]
                    if quarters:
                        ref[p] = by_group([block + move_lanes(block, 1) for block in blocks])
                    else:
                        ref[p] = jnp.where(lower_lanes((bs, bs)), *blocks)

        if own:
            add_own(left_refs[0, 0], right_refs[0])
            return
        for c, (_, _, both) in enumerate(chunks):
            if both[0] == both[1]:
                add(c, 0)
                continue
            if both[0] is not None:
                pl.when(odd == 0)(lambda c=c: add(c, 0))
            if both[1] is not None:
                pl.when(odd != 0)(lambda c=c: add(c, 1))
        if finish is not None and finish[0] == finish[1]:
            pack(total_refs[finish[0]], outs[1:], finish[0] > 0)
        elif finish is not None:
            pl.when(odd == 0)(lambda: pack(total_refs[finish[0]], outs[1:], True))
            pl.when(odd != 0)(lambda: pack(total_refs[finish[1]], outs[1:], True))

    def left_spec(turn, *what):
        start, count = block_rows(kb, *what)
        return pl.BlockSpec((1, count, lpb, bs, bs), lambda g, info_ref, *_: (info_ref[1 + turn], start // count, 0, 0, 0))

    def right_spec(array, at, both):
        parts = max(what[3] for what in both if what is not None)
        rows = kb // HALVES * bs // PARTS * parts
        return pl.BlockSpec((rows, width), lambda *_: (at, 0))

    operands = [lefts[chunks[c][2][side][0]] for c, side in sides] + [c[0] for c in chunks]
    if own:
        in_specs = [pl.BlockSpec((1, kb, lpb, bs, bs), lambda g, info_ref, *_: (info_ref[1], 0, 0, 0, 0)), whole(chunks[0][0].shape)]
    else:
        in_specs = [left_spec(*chunks[c][2][side]) for c, side in sides] + [right_spec(*chunk) for chunk in chunks]
    held = len(operands) + 1 + len(turns)
    if not own:
        operands += [totals[n] for n in touched]
        in_specs += [in_vmem] * len(touched)
    outs = [jax.ShapeDtypeStruct((nc + 1, bs, bs), f32)] * len(touched) + [jax.ShapeDtypeStruct((8, 128), jnp.int32)]
    if finish is not None:
        outs += [jax.ShapeDtypeStruct((nc // (8 if finish[0] else 4), bs, bs), f32)] * 2
    parts = QUARTERS if own else len(chunks)
    per = kb // HALVES
    flops = parts * per * 2 * lpb * bs * 3 * bs * width
    moved = 4 * parts * per * (lpb * bs * bs + bs * width)
    results = pl.pallas_call(
        kernel,
        grid_spec=pltpu.PrefetchScalarGridSpec(
            num_scalar_prefetch=1 + len(turns),
            grid=(1,),
            in_specs=in_specs,
            out_specs=[in_vmem] * len(touched) + [whole(x.shape) for x in outs[len(touched):]],
        ),
        out_shape=outs,
        input_output_aliases={} if own else {held + n: n for n in range(len(touched))},
        compiler_params=pltpu.CompilerParams(vmem_limit_bytes=20 * 1024 * 1024),
        cost_estimate=pl.CostEstimate(flops=cost * flops, bytes_accessed=cost * moved, transcendentals=0),
        name="accumulate",
    )(info, *[places[turn] for turn in turns], *operands)
    totals = [None] * 3 if own else list(totals)
    for n, total in zip(touched, results):
        totals[n] = total
    return (totals, *results[len(touched):])


def own_places(info, slots, rows, cols, kb, lpb):
    nc = slots.shape[0]
    bpr = cols.shape[0]

    def kernel(info_ref, slots_ref, rows_ref, cols_ref, table_ref, out_ref):
        for code in range(CB * CB):
            table_ref[code] = nc
        behind = nc - nc // 2 * info_ref[1 + STEPS]
        for n in range(nc):
            table_ref[slots_ref[n]] = lax.rem(n + behind, nc)
        fill_places(info_ref[1], table_ref, rows_ref, lambda k, b: cols_ref[b, k], out_ref, kb, lpb, bpr)

    return pl.pallas_call(
        kernel,
        in_specs=[in_smem] * 4,
        out_specs=[in_smem] * 2,
        out_shape=[jax.ShapeDtypeStruct((CB * CB,), jnp.int32), jax.ShapeDtypeStruct((kb * lpb * bpr,), jnp.int32)],
        compiler_params=pltpu.CompilerParams(vmem_limit_bytes=1024 * 1024),
        name="own_places",
    )(info, slots, rows, cols)


def fill_places(panel, table_ref, rows_ref, col_of, out_ref, kb, lpb, bpr):
    def column(k, carry):
        cols = [col_of(k, b) for b in range(bpr)]
        for a in range(lpb):
            row = rows_ref[panel, a, k] * CB
            for b in range(bpr):
                out_ref[(k * lpb + a) * bpr + b] = table_ref[row + cols[b]]
        return carry

    lax.fori_loop(0, kb, column, 0)


def panel_places(info, table, turn, rows, even_part, odd_part, kb, lpb, bpr):
    parts = (even_part, odd_part)

    def kernel(info_ref, table_ref, rows_ref, even_ref, odd_ref, out_ref, cols_ref, scalar_ref, sem):
        cols = jnp.where(info_ref[0] == 0, even_ref[...], odd_ref[...])
        cols_ref[...] = cols.astype(jnp.int32)
        copy = pltpu.make_async_copy(cols_ref, scalar_ref, sem)
        copy.start()
        copy.wait()
        fill_places(info_ref[1 + turn], table_ref, rows_ref, lambda k, b: scalar_ref[b, k], out_ref, kb, lpb, bpr)

    return pl.pallas_call(
        kernel,
        grid=(1,),
        in_specs=[in_smem] * 3 + [pl.BlockSpec((kb, 128), lambda g, at=at: (at // kb, 0)) for _, at in parts],
        out_specs=in_smem,
        out_shape=jax.ShapeDtypeStruct((kb * lpb * bpr,), jnp.int32),
        scratch_shapes=[pltpu.VMEM((kb, 128), jnp.int32), pltpu.SMEM((kb, 128), jnp.int32), pltpu.SemaphoreType.DMA],
        compiler_params=pltpu.CompilerParams(vmem_limit_bytes=1024 * 1024),
        name="panel_places",
    )(info, table, rows, *[array for array, _ in parts])


def combine(info, kept, other):
    packed, bs, _ = kept[0].shape
    packed_4 = kept[1].shape[0]

    def kernel(info_ref, *refs):
        out_ref = refs[-1]
        even = info_ref[0] == 0

        def step(first):
            for n in range(packed):
                p = first * packed + n
                low = refs[0][n] + refs[3][n]
                early = refs[1][p % packed_4] + refs[4][p % packed_4]
                late = refs[2][p % packed_4] + refs[5][p % packed_4]
                group = p // packed_4
                third = move_lanes(jnp.where(even, late, early), 2 - group)
                fourth = move_lanes(jnp.where(even, early, late), 3 - group)
                low = low if first == 0 else swap_lanes(low)
                out_ref[n] = by_group([low, low, third, fourth])

        for first in range(2):
            pl.when(pl.program_id(0) == first)(lambda first=first: step(first))

    return pl.pallas_call(
        kernel,
        grid=(2,),
        in_specs=[in_smem] + [in_vmem] * 6,
        out_specs=pl.BlockSpec((packed, bs, bs), lambda g: (g, 0, 0)),
        out_shape=jax.ShapeDtypeStruct((2 * packed, bs, bs), f32),
        compiler_params=pltpu.CompilerParams(vmem_limit_bytes=8 * 1024 * 1024),
        name="combine",
    )(info, *kept, *other)


def shards(left_values, left_rows, right_values, right_cols, result_slots):
    rows_n, cols_n = (lax.axis_size(a) for a in ("row", "col"))
    row, col, rep = (lax.axis_index(a) for a in ("row", "col", "rep"))
    panels = left_values[0, 0, 0]
    panel_rows = jnp.swapaxes(left_rows[0, 0, 0], 1, 2)
    right = right_values[0, 0, 0]
    cols = jnp.swapaxes(right_cols[0, 0, 0], 0, 1)
    slots = result_slots[0, 0]
    kb = right.shape[0]
    nc = slots.shape[0]
    place = [(col + turn) // cols_n for turn in range(STEPS)]
    info = jnp.stack([row % 2, *place, rep]).astype(jnp.int32)

    z_pairs = [(r, (r - 2) % rows_n) for r in range(rows_n)]
    x_pairs = [(r, r ^ 1) for r in range(rows_n)]

    def along_z(chunk):
        return lax.ppermute(chunk, "row", z_pairs)

    def along_x(chunk):
        return lax.ppermute(chunk, "row", x_pairs)

    rows, width = quarter_shape(right)
    def sent(even_parts, odd_parts, *others, extra=False):
        return pick(info, right, cols if extra else None, even_parts, odd_parts, *others)

    def all_of(array):
        return [(array, 0, PARTS)]

    def own_all(quarter):
        return [(None, quarter, 0, PARTS)]

    z = {}
    x = {}
    def own_part(quarter, first=0, parts=PARTS):
        return (quarter, first, parts)

    small = (info,)
    z[1] = along_z(own_quarters(right, [own_part(0)], cols, *small))
    x[1] = along_x(own_quarters(right, [own_part(3), own_part(2, 0, 1)], None, *small))

    shifts = sorted({turn % cols_n for turn in range(STEPS)})
    held = {
        shift: (panels, panel_rows) if shift == 0 else lax.ppermute((panels, panel_rows), "col", [(c, (c - shift) % cols_n) for c in range(cols_n)])
        for shift in shifts
    }
    lefts = [held[turn % cols_n][0] for turn in range(STEPS)]
    rows_at = [held[turn % cols_n][1] for turn in range(STEPS)]

    lpb, bpr = panels.shape[2], right.shape[1]
    places = {}
    table, places[0] = own_places(info, slots, panel_rows, cols, kb, lpb)

    def read_places(turn, even_part, odd_part):
        places[turn] = panel_places(info, table, turn, rows_at[turn], even_part, odd_part, kb, lpb, bpr)

    def add(totals, chunks, finish=None, cost=1):
        return accumulate(info, places, lefts, chunks, totals, nc, finish, cost)

    def along_z_part(stage):
        return (z[stage], 0, Z_CHUNKS[stage])

    def along_x_part(stage):
        if stage == 2:
            return (x[1], PARTS, X_CHUNKS[stage])
        if stage == 8:
            return (x[7], 1, X_CHUNKS[stage])
        return (x[stage], 0, X_CHUNKS[stage])

    totals, done = accumulate(info, places, [panels] * STEPS, [(right, 0, ((0, 0), (0, 0)))], None, nc)
    second = own_quarters(right, [own_part(1)], None, done)
    z[2] = along_z(second)
    x[3] = along_x(sent(all_of(z[1]), own_all(0), done, extra=True))
    z[3] = along_z(own_quarters(right, [own_part(2)], None, z[1], x[1], done))
    read_places(2, (z[1], rows), (z[1], rows))
    totals, done = add(totals, [along_z_part(1), along_z_part(2)])
    x[4] = along_x(sent(all_of(z[2]), own_all(1), done))
    z[4] = along_z(sent(own_all(3), all_of(x[3]), done, extra=True))
    read_places(1, (x[3], rows), (x[3], rows))
    totals, done = add(totals, [along_x_part(1), along_x_part(2), along_x_part(3)])
    x[5] = along_x(sent(all_of(z[3]), all_of(z[1]), done, extra=True))
    z[5] = along_z(sent(all_of(x[1]), all_of(x[4]), done))
    totals, done = add(totals, [along_z_part(3), along_x_part(4)])
    x[6] = along_x(sent(all_of(z[4]), all_of(z[2]), done))
    z[6] = along_z(sent([(x[1], PARTS, 1)], all_of(x[5]), done))
    read_places(3, (x[5], rows), (z[4], rows))
    totals, done = add(totals, [along_z_part(4), along_x_part(5)])
    x[7] = along_x(sent(all_of(z[5]), [(z[3], 1, 1), (None, 2, 1, 1)], done))
    totals, done = add(totals, [along_z_part(5)])
    z[7] = along_z(sent(all_of(x[6]), all_of(x[6]), done))

    def to_partner(blocks):
        return lax.ppermute(blocks, "rep", [(0, 1), (1, 0)])

    totals, done, *both_0 = add(totals, [along_x_part(6)], (0, 0))
    other_0 = to_partner(both_0[1])
    totals, done, *both_1 = add(totals, [along_z_part(6)], (2, 1))
    other_1 = to_partner(both_1[1])
    totals, done = add(totals, [along_x_part(7), along_x_part(8)], cost=0)
    totals, done, *both_2 = add(totals, [along_z_part(7)], (1, 2), 0)
    other_2 = to_partner(both_2[1])
    return combine(info, [both_0[0], both_1[0], both_2[0]], [other_0, other_1, other_2])[None, None]


def solution(mesh):
    in_specs = (
        P("row", "rep", "col", None, None, None, None, None),
        P("row", "rep", "col", None, None, None),
        P("rep", "row", "col", None, None, None, None),
        P("rep", "row", "col", None, None),
        P("row", "col", None),
    )
    out_specs = P("row", "col", "rep", None, None)
    return jax.shard_map(shards, mesh=mesh, in_specs=in_specs, out_specs=out_specs, check_vma=False)
```

```python
import jax
import jax.numpy as jnp
from jax import lax
from jax.experimental import pallas as pl
from jax.experimental.pallas import tpu as pltpu
from jax.sharding import PartitionSpec as P

STEPS = 4
CB = 8
HALVES = 2
QUARTERS = HALVES * HALVES

bf16 = jnp.bfloat16
f32 = jnp.float32

PARTS = 2
Z_CHUNKS = {
    1: ((2, 0, 0, 2), (2, 0, 0, 2)),
    2: ((2, 1, 0, 2), (2, 1, 0, 2)),
    3: ((2, 2, 0, 2), (2, 2, 0, 2)),
    4: ((2, 3, 0, 2), (3, 0, 0, 2)),
    5: ((3, 3, 0, 2), (3, 1, 0, 2)),
    6: ((3, 2, 0, 1), (3, 2, 0, 2)),
    7: (None, (3, 3, 0, 2)),
}
X_CHUNKS = {
    1: ((1, 3, 0, 2), None),
    2: ((1, 2, 0, 1), None),
    3: ((1, 0, 0, 2), (1, 0, 0, 2)),
    4: ((1, 1, 0, 2), (1, 1, 0, 2)),
    5: ((3, 0, 0, 2), (1, 2, 0, 2)),
    6: ((3, 1, 0, 2), (1, 3, 0, 2)),
    7: ((3, 2, 1, 1), (2, 3, 0, 2)),
    8: ((1, 2, 1, 1), None),
}

in_smem = pl.BlockSpec(memory_space=pltpu.SMEM)
in_vmem = pl.BlockSpec(memory_space=pltpu.VMEM)
anywhere = pl.BlockSpec(memory_space=pl.ANY)


def whole(shape):
    return pl.BlockSpec(shape, lambda *_: (0,) * len(shape))


def lower_lanes(shape):
    return lax.broadcasted_iota(jnp.int32, shape, len(shape) - 1) < shape[-1] // 2


def swap_lanes(x):
    return pltpu.roll(x, x.shape[-1] // 2, x.ndim - 1)


def move_lanes(x, groups):
    if groups % 4 == 0:
        return x
    return pltpu.roll(x, x.shape[-1] // 4 * (groups % 4), x.ndim - 1)


def lane_group(shape):
    return lax.broadcasted_iota(jnp.int32, shape, len(shape) - 1) // (shape[-1] // 4)


def fold_half(group, one, two):
    lower = group < 2
    return jnp.where(lower, one, two) + swap_lanes(jnp.where(lower, two, one))


def by_group(parts):
    group = lane_group(parts[0].shape)
    out = parts[3]
    for g in (2, 1, 0):
        out = jnp.where(group == g, parts[g], out)
    return out


def sum_of(quarter):
    return max(quarter - 1, 0)


def block_rows(kb, quarter, first, parts):
    if quarter < 2:
        per = kb // (2 * PARTS)
        return (quarter * PARTS + first) * per, parts * per
    per = kb // PARTS
    return first * per, parts * per


def cut(right_ref, out_ref, quarter, at=0, start=0, count=None):
    count = right_ref.shape[0] if count is None else count
    _, bpr, bs, _ = right_ref.shape
    lower = lower_lanes((bs, bs))
    for n in range(count):
        blocks = [right_ref[start + n, b] for b in range(bpr)]
        if quarter < 2:
            for pair in range(bpr // 2):
                both = jnp.where(lower, blocks[2 * pair], swap_lanes(blocks[2 * pair + 1]))
                out_ref[at + n * bs:at + (n + 1) * bs, pair * bs:(pair + 1) * bs] = both
        else:
            row = at + n // 2 * bs
            four = by_group([move_lanes(block, b - quarter) for b, block in enumerate(blocks)])
            out_ref[row:row + bs, n % 2 * bs:(n % 2 + 1) * bs] = four


def own_spec(right, quarter, first=0, parts=PARTS):
    start, count = block_rows(right.shape[0], quarter, first, parts)
    return pl.BlockSpec((count,) + right.shape[1:], lambda *_: (start // count, 0, 0, 0))


def quarter_shape(right):
    kb, bpr, bs, _ = right.shape
    return kb // HALVES * bs, bpr * bs // HALVES


def put_extra(out_ref, cols_ref, rows):
    bpr, kb = cols_ref.shape
    out_ref[rows:rows + bpr, :kb] = cols_ref[...].astype(out_ref.dtype)


def own_quarters(right, quarters, cols, *others):
    rows, width = quarter_shape(right)
    extra = [] if cols is None else [cols]
    several = len(quarters) > 1
    starts = [sum(parts for _, _, parts in quarters[:n]) * rows // PARTS for n in range(len(quarters) + 1)]

    def kernel(*refs):
        out_ref = refs[-1]
        for n, part in enumerate(quarters):
            start, count = block_rows(right.shape[0], *part)
            cut(refs[0], out_ref, part[0], starts[n], start if several else 0, count)
        if extra:
            put_extra(out_ref, refs[1], starts[-1])

    out_shape = jax.ShapeDtypeStruct((starts[-1] + right.shape[0] * len(extra), width), right.dtype)
    return pl.pallas_call(
        kernel,
        grid=(1,),
        in_specs=[whole(right.shape) if several else own_spec(right, *quarters[0])] + [whole(x.shape) for x in extra] + [anywhere] * len(others),
        out_specs=whole(out_shape.shape),
        out_shape=out_shape,
        compiler_params=pltpu.CompilerParams(vmem_limit_bytes=12 * 1024 * 1024),
        cost_estimate=pl.CostEstimate(flops=0, bytes_accessed=12 * out_shape.size, transcendentals=0),
        name="own_quarters",
    )(right, *extra, *others)


def first_quarter(right, cols, *others):
    rows, width = quarter_shape(right)
    start, count = block_rows(right.shape[0], 0, 0, PARTS)

    def kernel(right_ref, cols_ref, *refs):
        out_ref, blocks_ref, small_ref, sems = refs[-4:]
        copies = [
            pltpu.make_async_copy(cols_ref, small_ref, sems.at[count]),
            *(pltpu.make_async_copy(right_ref.at[start + n], blocks_ref.at[n], sems.at[n]) for n in range(count)),
        ]
        for copy in copies:
            copy.start()
        copies[0].wait()
        put_extra(out_ref, small_ref, rows)
        for n in range(count):
            copies[1 + n].wait()
            cut(blocks_ref, out_ref, 0, n * right.shape[2], n, 1)

    in_hbm = pl.BlockSpec(memory_space=pltpu.HBM)
    return pl.pallas_call(
        kernel,
        in_specs=[in_hbm] * 2 + [anywhere] * len(others),
        out_specs=in_vmem,
        out_shape=jax.ShapeDtypeStruct((rows + right.shape[0], width), right.dtype),
        scratch_shapes=[
            pltpu.VMEM((count,) + right.shape[1:], right.dtype),
            pltpu.VMEM(cols.shape, cols.dtype),
            pltpu.SemaphoreType.DMA((count + 1,)),
        ],
        compiler_params=pltpu.CompilerParams(vmem_limit_bytes=12 * 1024 * 1024),
        cost_estimate=pl.CostEstimate(flops=0, bytes_accessed=12 * rows * width, transcendentals=0),
        name="first_quarter",
    )(*(pltpu.with_memory_space_constraint(x, pltpu.HBM) for x in (right, cols)), *others)


def pick(info, right, cols, even_parts, odd_parts, *others):
    sides = (even_parts, odd_parts)
    kb = right.shape[0]
    rows, width = quarter_shape(right)
    extra = [] if cols is None else [cols]

    def has_extra(part):
        return part[0] is not None and extra and part[0].shape[0] == rows + kb

    def size(part):
        return rows + kb if has_extra(part) else part[-1] * rows // PARTS

    def kernel(info_ref, *refs):
        out_ref = refs[-1]

        def copy_parts(side, refs_of):
            at = 0
            for part, ref in zip(sides[side], refs_of):
                if part[0] is None:
                    cut(ref, out_ref, part[1], at)
                else:
                    out_ref[at:at + size(part)] = ref[...]
                at += size(part)
            if at < out_ref.shape[0]:
                out_ref[at:] = jnp.zeros((out_ref.shape[0] - at, width), out_ref.dtype)
                if extra and sides[side][0][0] is None:
                    put_extra(out_ref, refs[len(even_parts) + len(odd_parts)], rows)

        pl.when(info_ref[0] == 0)(lambda: copy_parts(0, refs[:len(even_parts)]))
        pl.when(info_ref[0] != 0)(lambda: copy_parts(1, refs[len(even_parts):]))

    def spec(part):
        if part[0] is None:
            return own_spec(right, *part[1:])
        return pl.BlockSpec((size(part), width), lambda *_: (part[1], 0))

    parts = [*even_parts, *odd_parts]
    out_shape = jax.ShapeDtypeStruct((rows + kb * len(extra), width), right.dtype)
    return pl.pallas_call(
        kernel,
        grid=(1,),
        in_specs=[in_smem] + [spec(part) for part in parts] + [whole(x.shape) for x in extra] + [anywhere] * len(others),
        out_specs=whole(out_shape.shape),
        out_shape=out_shape,
        compiler_params=pltpu.CompilerParams(vmem_limit_bytes=8 * 1024 * 1024),
        cost_estimate=pl.CostEstimate(flops=0, bytes_accessed=8 * out_shape.size, transcendentals=0),
        name="pick",
    )(info, *[right if part[0] is None else part[0] for part in parts], *extra, *others)


def accumulate(info, places, lefts, chunks, totals, nc, finish=None, cost=1):
    _, kb, lpb, bs, _ = lefts[0].shape
    own = totals is None
    bpr = chunks[0][0].shape[1] if own else HALVES * chunks[0][0].shape[1] // bs
    width = bpr * bs // HALVES
    products = lpb * bpr
    turns = sorted({what[0] for _, _, both in chunks for what in both if what is not None})
    if own:
        touched = list(range(3))
    else:
        touched = {sum_of(what[1]) for _, _, both in chunks for what in both if what is not None}
        touched = sorted(touched | set(finish or ()))
    sides = [(c, side) for c in range(len(chunks)) for side in range(2) if chunks[c][2][side] is not None]
    sides = [(c, side) for c, side in sides if side == 0 or chunks[c][2][0] != chunks[c][2][1]]

    def kernel(info_ref, *refs):
        place_refs = dict(zip(turns, refs))
        refs = refs[len(turns):]
        left_refs = dict(zip(sides, refs))
        right_refs = refs[len(sides):len(sides) + len(chunks)]
        outs = refs[len(sides) + len(chunks) + (0 if own else len(touched)):]
        total_refs = dict(zip(touched, outs))
        outs = outs[len(touched):]
        outs[0][...] = jnp.zeros_like(outs[0])
        odd = info_ref[0]
        if own:
            for ref in total_refs.values():
                ref[...] = jnp.zeros_like(ref)

        def products_of(left, right):
            left = left.reshape(lpb * bs, bs)
            left_high = left.astype(bf16)
            left_low = (left - left_high.astype(f32)).astype(bf16)
            high = right.astype(bf16)
            low = (right - high.astype(f32)).astype(bf16)
            return jnp.dot(
                jnp.concatenate([left_high, left_low, left_high], axis=1),
                jnp.concatenate([high, high, low], axis=0),
                preferred_element_type=f32,
            )

        def add_own(left_ref, right_ref):
            parts = (slice(0, bs // 2), slice(bs // 2, 3 * bs // 4), slice(3 * bs // 4, bs))
            for k in range(kb):
                out = products_of(left_ref[0, k], jnp.concatenate([right_ref[k, b] for b in range(bpr)], axis=1))
                for a in range(lpb):
                    for b in range(bpr):
                        n = place_refs[0][k * products + a * bpr + b]
                        block = out[a * bs:(a + 1) * bs, b * bs:(b + 1) * bs]
                        for ref, lanes in zip(total_refs.values(), parts):
                            ref[n, :, lanes] += block[:, lanes]

        def add(c, side):
            turn, quarter = chunks[c][2][side][:2]
            start, count = block_rows(kb, *chunks[c][2][side][1:])
            left_ref, right_ref, total_ref = left_refs[c, side], right_refs[c], total_refs[sum_of(quarter)]
            lanes = bs // 2 if quarter < 2 else bs // 4
            for k in range(count):
                if quarter < 2:
                    right = right_ref[k * bs:(k + 1) * bs]
                else:
                    right = right_ref[k // 2 * bs:(k // 2 + 1) * bs, k % 2 * bs:(k % 2 + 1) * bs]
                out = products_of(left_ref[0, k], right)
                for a in range(lpb):
                    for b in range(bpr):
                        n = place_refs[turn][(start + k) * products + a * bpr + b]
                        at = b * lanes % bs
                        total_ref[n, :, at:at + lanes] += out[a * bs:(a + 1) * bs, b * lanes:(b + 1) * lanes]

        def pack(total_ref, ref, quarters):
            packed = ref.shape[0]
            group = lane_group((bs, bs))
            for p in range(packed):
                blocks = [total_ref[nc // 2 + g * packed + p] for g in range(4 if quarters else 2)]
                if not quarters:
                    ref[p] = fold_half(group, *blocks)
                    continue
                one = fold_half(group, blocks[0], blocks[2])
                two = fold_half(group, blocks[1], blocks[3])
                even = group % 2 == 0
                moved = jnp.where(even, two, one)
                ref[p] = jnp.where(even, one + move_lanes(moved, 3), two + move_lanes(moved, 1))

        if own:
            add_own(left_refs[0, 0], right_refs[0])
            return
        for c, (_, _, both) in enumerate(chunks):
            if both[0] == both[1]:
                add(c, 0)
                continue
            if both[0] is not None:
                pl.when(odd == 0)(lambda c=c: add(c, 0))
            if both[1] is not None:
                pl.when(odd != 0)(lambda c=c: add(c, 1))
        if finish is not None and finish[0] == finish[1]:
            pack(total_refs[finish[0]], outs[1], finish[0] > 0)
        elif finish is not None:
            pl.when(odd == 0)(lambda: pack(total_refs[finish[0]], outs[1], True))
            pl.when(odd != 0)(lambda: pack(total_refs[finish[1]], outs[1], True))

    def left_spec(turn, *what):
        start, count = block_rows(kb, *what)
        return pl.BlockSpec((1, count, lpb, bs, bs), lambda g, info_ref, *_: (info_ref[1 + turn], start // count, 0, 0, 0))

    def right_spec(array, at, both):
        parts = max(what[3] for what in both if what is not None)
        rows = kb // HALVES * bs // PARTS * parts
        return pl.BlockSpec((rows, width), lambda *_: (at, 0))

    operands = [lefts[chunks[c][2][side][0]] for c, side in sides] + [c[0] for c in chunks]
    if own:
        in_specs = [pl.BlockSpec((1, kb, lpb, bs, bs), lambda g, info_ref, *_: (info_ref[1], 0, 0, 0, 0)), whole(chunks[0][0].shape)]
    else:
        in_specs = [left_spec(*chunks[c][2][side]) for c, side in sides] + [right_spec(*chunk) for chunk in chunks]
    held = len(operands) + 1 + len(turns)
    if not own:
        operands += [totals[n] for n in touched]
        in_specs += [in_vmem] * len(touched)
    outs = [jax.ShapeDtypeStruct((nc + 1, bs, bs), f32)] * len(touched) + [jax.ShapeDtypeStruct((8, 128), jnp.int32)]
    if finish is not None:
        outs.append(jax.ShapeDtypeStruct((nc // (8 if finish[0] else 4), bs, bs), f32))
    parts = QUARTERS if own else len(chunks)
    per = kb // HALVES
    flops = parts * per * 2 * lpb * bs * 3 * bs * width
    moved = 4 * parts * per * (lpb * bs * bs + bs * width)
    results = pl.pallas_call(
        kernel,
        grid_spec=pltpu.PrefetchScalarGridSpec(
            num_scalar_prefetch=1 + len(turns),
            grid=(1,),
            in_specs=in_specs,
            out_specs=[in_vmem] * len(touched) + [whole(x.shape) for x in outs[len(touched):]],
        ),
        out_shape=outs,
        input_output_aliases={} if own else {held + n: n for n in range(len(touched))},
        compiler_params=pltpu.CompilerParams(vmem_limit_bytes=20 * 1024 * 1024),
        cost_estimate=pl.CostEstimate(flops=cost * flops, bytes_accessed=cost * moved, transcendentals=0),
        name="accumulate",
    )(info, *[places[turn] for turn in turns], *operands)
    totals = [None] * 3 if own else list(totals)
    for n, total in zip(touched, results):
        totals[n] = total
    return (totals, *results[len(touched):])


def own_places(info, slots, rows, cols, kb, lpb):
    nc = slots.shape[0]
    bpr = cols.shape[0]

    def kernel(info_ref, slots_ref, rows_ref, cols_ref, table_ref, out_ref):
        for code in range(CB * CB):
            table_ref[code] = nc
        behind = nc - nc // 2 * info_ref[1 + STEPS]
        for n in range(nc):
            table_ref[slots_ref[n]] = lax.rem(n + behind, nc)
        fill_places(info_ref[1], table_ref, rows_ref, lambda k, b: cols_ref[b, k], out_ref, kb, lpb, bpr)

    return pl.pallas_call(
        kernel,
        in_specs=[in_smem] * 4,
        out_specs=[in_smem] * 2,
        out_shape=[jax.ShapeDtypeStruct((CB * CB,), jnp.int32), jax.ShapeDtypeStruct((kb * lpb * bpr,), jnp.int32)],
        compiler_params=pltpu.CompilerParams(vmem_limit_bytes=1024 * 1024),
        name="own_places",
    )(info, slots, rows, cols)


def fill_places(panel, table_ref, rows_ref, col_of, out_ref, kb, lpb, bpr):
    def column(k, carry):
        cols = [col_of(k, b) for b in range(bpr)]
        for a in range(lpb):
            row = rows_ref[panel, a, k] * CB
            for b in range(bpr):
                out_ref[(k * lpb + a) * bpr + b] = table_ref[row + cols[b]]
        return carry

    lax.fori_loop(0, kb, column, 0)


def panel_places(info, table, turn, rows, even_part, odd_part, kb, lpb, bpr):
    parts = (even_part, odd_part)

    def kernel(info_ref, table_ref, rows_ref, even_ref, odd_ref, out_ref, cols_ref, scalar_ref, sem):
        cols = jnp.where(info_ref[0] == 0, even_ref[...], odd_ref[...])
        cols_ref[...] = cols.astype(jnp.int32)
        copy = pltpu.make_async_copy(cols_ref, scalar_ref, sem)
        copy.start()
        copy.wait()
        fill_places(info_ref[1 + turn], table_ref, rows_ref, lambda k, b: scalar_ref[b, k], out_ref, kb, lpb, bpr)

    return pl.pallas_call(
        kernel,
        grid=(1,),
        in_specs=[in_smem] * 3 + [pl.BlockSpec((kb, 128), lambda g, at=at: (at // kb, 0)) for _, at in parts],
        out_specs=in_smem,
        out_shape=jax.ShapeDtypeStruct((kb * lpb * bpr,), jnp.int32),
        scratch_shapes=[pltpu.VMEM((kb, 128), jnp.int32), pltpu.SMEM((kb, 128), jnp.int32), pltpu.SemaphoreType.DMA],
        compiler_params=pltpu.CompilerParams(vmem_limit_bytes=1024 * 1024),
        name="panel_places",
    )(info, table, rows, *[array for array, _ in parts])


def kept_blocks(totals, nc):
    bs = totals[0].shape[-1]

    def kernel(half_ref, third_ref, fourth_ref, out_ref):
        for n in range(nc // 2):
            half = half_ref[n]
            upper = [ref[n] + swap_lanes(ref[n]) for ref in (third_ref, fourth_ref)]
            half = half + swap_lanes(half)
            out_ref[n] = by_group([half, half, *(x + move_lanes(x, 1) for x in upper)])

    return pl.pallas_call(
        kernel,
        in_specs=[in_vmem] * 3,
        out_specs=in_vmem,
        out_shape=jax.ShapeDtypeStruct((nc // 2, bs, bs), f32),
        compiler_params=pltpu.CompilerParams(vmem_limit_bytes=8 * 1024 * 1024),
        cost_estimate=pl.CostEstimate(flops=0, bytes_accessed=0, transcendentals=0),
        name="kept_blocks",
    )(*totals)


def combine(info, kept, other):
    packed, bs, _ = other[0].shape
    packed_4 = other[1].shape[0]

    def kernel(info_ref, kept_ref, half_ref, early_ref, late_ref, out_ref):
        even = info_ref[0] == 0

        def step(first):
            for n in range(packed):
                p = first * packed + n
                low = half_ref[n] if first == 0 else swap_lanes(half_ref[n])
                early, late = early_ref[p % packed_4], late_ref[p % packed_4]
                group = p // packed_4
                third = move_lanes(jnp.where(even, late, early), 2 - group)
                fourth = move_lanes(jnp.where(even, early, late), 3 - group)
                out_ref[n] = kept_ref[p] + by_group([low, low, third, fourth])

        for first in range(2):
            pl.when(pl.program_id(0) == first)(lambda first=first: step(first))

    return pl.pallas_call(
        kernel,
        grid=(2,),
        in_specs=[in_smem] + [in_vmem] * 4,
        out_specs=pl.BlockSpec((packed, bs, bs), lambda g: (g, 0, 0)),
        out_shape=jax.ShapeDtypeStruct((2 * packed, bs, bs), f32),
        compiler_params=pltpu.CompilerParams(vmem_limit_bytes=8 * 1024 * 1024),
        name="combine",
    )(info, kept, *other)


def shards(left_values, left_rows, right_values, right_cols, result_slots):
    rows_n, cols_n = (lax.axis_size(a) for a in ("row", "col"))
    row, col, rep = (lax.axis_index(a) for a in ("row", "col", "rep"))
    panels = left_values[0, 0, 0]
    panel_rows = jnp.swapaxes(left_rows[0, 0, 0], 1, 2)
    right = right_values[0, 0, 0]
    cols = jnp.swapaxes(right_cols[0, 0, 0], 0, 1)
    slots = result_slots[0, 0]
    kb = right.shape[0]
    nc = slots.shape[0]
    place = [(col + turn) // cols_n for turn in range(STEPS)]
    info = jnp.stack([row % 2, *place, rep]).astype(jnp.int32)

    z_pairs = [(r, (r - 2) % rows_n) for r in range(rows_n)]
    x_pairs = [(r, r ^ 1) for r in range(rows_n)]

    def along_z(chunk):
        return lax.ppermute(chunk, "row", z_pairs)

    def along_x(chunk):
        return lax.ppermute(chunk, "row", x_pairs)

    rows, width = quarter_shape(right)
    def sent(even_parts, odd_parts, *others, extra=False):
        return pick(info, right, cols if extra else None, even_parts, odd_parts, *others)

    def all_of(array):
        return [(array, 0, PARTS)]

    def own_all(quarter):
        return [(None, quarter, 0, PARTS)]

    z = {}
    x = {}
    def own_part(quarter, first=0, parts=PARTS):
        return (quarter, first, parts)

    small = (info,)
    z[1] = along_z(first_quarter(right, cols, *small))
    x[1] = along_x(own_quarters(right, [own_part(3), own_part(2, 0, 1)], None, *small))

    shifts = sorted({turn % cols_n for turn in range(STEPS)})
    held = {
        shift: (panels, panel_rows) if shift == 0 else lax.ppermute((panels, panel_rows), "col", [(c, (c - shift) % cols_n) for c in range(cols_n)])
        for shift in shifts
    }
    lefts = [held[turn % cols_n][0] for turn in range(STEPS)]
    rows_at = [held[turn % cols_n][1] for turn in range(STEPS)]

    lpb, bpr = panels.shape[2], right.shape[1]
    places = {}
    table, places[0] = own_places(info, slots, panel_rows, cols, kb, lpb)

    def read_places(turn, even_part, odd_part):
        places[turn] = panel_places(info, table, turn, rows_at[turn], even_part, odd_part, kb, lpb, bpr)

    def add(totals, chunks, finish=None, cost=1):
        return accumulate(info, places, lefts, chunks, totals, nc, finish, cost)

    def along_z_part(stage):
        return (z[stage], 0, Z_CHUNKS[stage])

    def along_x_part(stage):
        if stage == 2:
            return (x[1], PARTS, X_CHUNKS[stage])
        if stage == 8:
            return (x[7], 1, X_CHUNKS[stage])
        return (x[stage], 0, X_CHUNKS[stage])

    totals, done = accumulate(info, places, [panels] * STEPS, [(right, 0, ((0, 0), (0, 0)))], None, nc)
    second = own_quarters(right, [own_part(1)], None, done)
    z[2] = along_z(second)
    x[3] = along_x(sent(all_of(z[1]), own_all(0), done, extra=True))
    z[3] = along_z(own_quarters(right, [own_part(2)], None, z[1], x[1], done))
    read_places(2, (z[1], rows), (z[1], rows))
    totals, done = add(totals, [along_z_part(1), along_z_part(2)])
    x[4] = along_x(sent(all_of(z[2]), own_all(1), done))
    z[4] = along_z(sent(own_all(3), all_of(x[3]), done, extra=True))
    read_places(1, (x[3], rows), (x[3], rows))
    totals, done = add(totals, [along_x_part(1), along_x_part(2), along_x_part(3)])
    x[5] = along_x(sent(all_of(z[3]), all_of(z[1]), done, extra=True))
    z[5] = along_z(sent(all_of(x[1]), all_of(x[4]), done))
    totals, done = add(totals, [along_z_part(3), along_x_part(4)])
    x[6] = along_x(sent(all_of(z[4]), all_of(z[2]), done))
    z[6] = along_z(sent([(x[1], PARTS, 1)], all_of(x[5]), done))
    read_places(3, (x[5], rows), (z[4], rows))
    totals, done = add(totals, [along_z_part(4), along_x_part(5)])
    x[7] = along_x(sent(all_of(z[5]), [(z[3], 1, 1), (None, 2, 1, 1)], done))
    totals, done = add(totals, [along_z_part(5)])
    z[7] = along_z(sent(all_of(x[6]), all_of(x[6]), done))

    def to_partner(blocks):
        return lax.ppermute(blocks, "rep", [(0, 1), (1, 0)])

    totals, done, send_0 = add(totals, [along_x_part(6)], (0, 0))
    other_0 = to_partner(send_0)
    totals, done, send_1 = add(totals, [along_z_part(6)], (2, 1))
    other_1 = to_partner(send_1)
    totals, done = add(totals, [along_x_part(7), along_x_part(8)], cost=0)
    totals, done, send_2 = add(totals, [along_z_part(7)], (1, 2), 0)
    other_2 = to_partner(send_2)
    return combine(info, kept_blocks(totals, nc), [other_0, other_1, other_2])[None, None]


def solution(mesh):
    in_specs = (
        P("row", "rep", "col", None, None, None, None, None),
        P("row", "rep", "col", None, None, None),
        P("rep", "row", "col", None, None, None, None),
        P("rep", "row", "col", None, None),
        P("row", "col", None),
    )
    out_specs = P("row", "col", "rep", None, None)
    return jax.shard_map(shards, mesh=mesh, in_specs=in_specs, out_specs=out_specs, check_vma=False)
```

```python
import jax
import jax.numpy as jnp
from jax import lax
from jax.experimental import pallas as pl
from jax.experimental.pallas import tpu as pltpu
from jax.sharding import PartitionSpec as P

STEPS = 4
CB = 8
HALVES = 2
QUARTERS = HALVES * HALVES

bf16 = jnp.bfloat16
f32 = jnp.float32

PARTS = 2
Z_CHUNKS = {
    1: ((2, 0, 0, 2), (2, 0, 0, 2)),
    2: ((2, 1, 0, 2), (2, 1, 0, 2)),
    3: ((2, 2, 0, 2), (2, 2, 0, 2)),
    4: ((2, 3, 0, 2), (3, 0, 0, 2)),
    5: ((3, 3, 0, 2), (3, 1, 0, 2)),
    6: ((3, 2, 0, 1), (3, 2, 0, 2)),
    7: (None, (3, 3, 0, 2)),
}
X_CHUNKS = {
    1: ((1, 3, 0, 2), None),
    2: ((1, 2, 0, 1), None),
    3: ((1, 0, 0, 2), (1, 0, 0, 2)),
    4: ((1, 1, 0, 2), (1, 1, 0, 2)),
    5: ((3, 0, 0, 2), (1, 2, 0, 2)),
    6: ((3, 1, 0, 2), (1, 3, 0, 2)),
    7: ((3, 2, 1, 1), (2, 3, 0, 2)),
    8: ((1, 2, 1, 1), None),
}

in_smem = pl.BlockSpec(memory_space=pltpu.SMEM)
in_vmem = pl.BlockSpec(memory_space=pltpu.VMEM)
anywhere = pl.BlockSpec(memory_space=pl.ANY)


def whole(shape):
    return pl.BlockSpec(shape, lambda *_: (0,) * len(shape))


def lower_lanes(shape):
    return lax.broadcasted_iota(jnp.int32, shape, len(shape) - 1) < shape[-1] // 2


def swap_lanes(x):
    return pltpu.roll(x, x.shape[-1] // 2, x.ndim - 1)


def move_lanes(x, groups):
    if groups % 4 == 0:
        return x
    return pltpu.roll(x, x.shape[-1] // 4 * (groups % 4), x.ndim - 1)


def lane_group(shape):
    return lax.broadcasted_iota(jnp.int32, shape, len(shape) - 1) // (shape[-1] // 4)


def fold_half(group, one, two):
    lower = group < 2
    return jnp.where(lower, one, two) + swap_lanes(jnp.where(lower, two, one))


def by_group(parts):
    group = lane_group(parts[0].shape)
    out = parts[3]
    for g in (2, 1, 0):
        out = jnp.where(group == g, parts[g], out)
    return out


def sum_of(quarter):
    return max(quarter - 1, 0)


def block_rows(kb, quarter, first, parts):
    if quarter < 2:
        per = kb // (2 * PARTS)
        return (quarter * PARTS + first) * per, parts * per
    per = kb // PARTS
    return first * per, parts * per


def cut(right_ref, out_ref, quarter, at=0, start=0, count=None):
    count = right_ref.shape[0] if count is None else count
    _, bpr, bs, _ = right_ref.shape
    lower = lower_lanes((bs, bs))
    for n in range(count):
        blocks = [right_ref[start + n, b] for b in range(bpr)]
        if quarter < 2:
            for pair in range(bpr // 2):
                both = jnp.where(lower, blocks[2 * pair], swap_lanes(blocks[2 * pair + 1]))
                out_ref[at + n * bs:at + (n + 1) * bs, pair * bs:(pair + 1) * bs] = both
        else:
            row = at + n // 2 * bs
            four = by_group([move_lanes(block, b - quarter) for b, block in enumerate(blocks)])
            out_ref[row:row + bs, n % 2 * bs:(n % 2 + 1) * bs] = four


def own_spec(right, quarter, first=0, parts=PARTS):
    start, count = block_rows(right.shape[0], quarter, first, parts)
    return pl.BlockSpec((count,) + right.shape[1:], lambda *_: (start // count, 0, 0, 0))


def quarter_shape(right):
    kb, bpr, bs, _ = right.shape
    return kb // HALVES * bs, bpr * bs // HALVES


def put_extra(out_ref, cols_ref, rows):
    bpr, kb = cols_ref.shape
    out_ref[rows:rows + bpr, :kb] = cols_ref[...].astype(out_ref.dtype)


def own_quarters(right, quarters, cols, *others):
    rows, width = quarter_shape(right)
    extra = [] if cols is None else [cols]
    several = len(quarters) > 1
    starts = [sum(parts for _, _, parts in quarters[:n]) * rows // PARTS for n in range(len(quarters) + 1)]

    def kernel(*refs):
        out_ref = refs[-1]
        for n, part in enumerate(quarters):
            start, count = block_rows(right.shape[0], *part)
            cut(refs[0], out_ref, part[0], starts[n], start if several else 0, count)
        if extra:
            put_extra(out_ref, refs[1], starts[-1])

    out_shape = jax.ShapeDtypeStruct((starts[-1] + right.shape[0] * len(extra), width), right.dtype)
    return pl.pallas_call(
        kernel,
        grid=(1,),
        in_specs=[whole(right.shape) if several else own_spec(right, *quarters[0])] + [whole(x.shape) for x in extra] + [anywhere] * len(others),
        out_specs=whole(out_shape.shape),
        out_shape=out_shape,
        compiler_params=pltpu.CompilerParams(vmem_limit_bytes=12 * 1024 * 1024),
        cost_estimate=pl.CostEstimate(flops=0, bytes_accessed=12 * out_shape.size, transcendentals=0),
        name="own_quarters",
    )(right, *extra, *others)


def first_quarter(right, cols, *others):
    rows, width = quarter_shape(right)
    start, count = block_rows(right.shape[0], 0, 0, PARTS)

    def kernel(right_ref, cols_ref, *refs):
        out_ref, blocks_ref, small_ref, sems = refs[-4:]
        copies = [
            pltpu.make_async_copy(cols_ref, small_ref, sems.at[count]),
            *(pltpu.make_async_copy(right_ref.at[start + n], blocks_ref.at[n], sems.at[n]) for n in range(count)),
        ]
        for copy in copies:
            copy.start()
        copies[0].wait()
        put_extra(out_ref, small_ref, rows)
        for n in range(count):
            copies[1 + n].wait()
            cut(blocks_ref, out_ref, 0, n * right.shape[2], n, 1)

    in_hbm = pl.BlockSpec(memory_space=pltpu.HBM)
    return pl.pallas_call(
        kernel,
        in_specs=[in_hbm] * 2 + [anywhere] * len(others),
        out_specs=in_vmem,
        out_shape=jax.ShapeDtypeStruct((rows + right.shape[0], width), right.dtype),
        scratch_shapes=[
            pltpu.VMEM((count,) + right.shape[1:], right.dtype),
            pltpu.VMEM(cols.shape, cols.dtype),
            pltpu.SemaphoreType.DMA((count + 1,)),
        ],
        compiler_params=pltpu.CompilerParams(vmem_limit_bytes=12 * 1024 * 1024),
        cost_estimate=pl.CostEstimate(flops=0, bytes_accessed=12 * rows * width, transcendentals=0),
        name="first_quarter",
    )(*(pltpu.with_memory_space_constraint(x, pltpu.HBM) for x in (right, cols)), *others)


def pick(info, right, cols, even_parts, odd_parts, *others):
    sides = (even_parts, odd_parts)
    kb = right.shape[0]
    rows, width = quarter_shape(right)
    extra = [] if cols is None else [cols]

    def has_extra(part):
        return part[0] is not None and extra and part[0].shape[0] == rows + kb

    def size(part):
        return rows + kb if has_extra(part) else part[-1] * rows // PARTS

    def kernel(info_ref, *refs):
        out_ref = refs[-1]

        def copy_parts(side, refs_of):
            at = 0
            for part, ref in zip(sides[side], refs_of):
                if part[0] is None:
                    cut(ref, out_ref, part[1], at)
                else:
                    out_ref[at:at + size(part)] = ref[...]
                at += size(part)
            if at < out_ref.shape[0]:
                out_ref[at:] = jnp.zeros((out_ref.shape[0] - at, width), out_ref.dtype)
                if extra and sides[side][0][0] is None:
                    put_extra(out_ref, refs[len(even_parts) + len(odd_parts)], rows)

        pl.when(info_ref[0] == 0)(lambda: copy_parts(0, refs[:len(even_parts)]))
        pl.when(info_ref[0] != 0)(lambda: copy_parts(1, refs[len(even_parts):]))

    def spec(part):
        if part[0] is None:
            return own_spec(right, *part[1:])
        return pl.BlockSpec((size(part), width), lambda *_: (part[1], 0))

    parts = [*even_parts, *odd_parts]
    out_shape = jax.ShapeDtypeStruct((rows + kb * len(extra), width), right.dtype)
    return pl.pallas_call(
        kernel,
        grid=(1,),
        in_specs=[in_smem] + [spec(part) for part in parts] + [whole(x.shape) for x in extra] + [anywhere] * len(others),
        out_specs=whole(out_shape.shape),
        out_shape=out_shape,
        compiler_params=pltpu.CompilerParams(vmem_limit_bytes=8 * 1024 * 1024),
        cost_estimate=pl.CostEstimate(flops=0, bytes_accessed=8 * out_shape.size, transcendentals=0),
        name="pick",
    )(info, *[right if part[0] is None else part[0] for part in parts], *extra, *others)


def accumulate(info, places, lefts, chunks, totals, nc, finish=None, cost=1):
    _, kb, lpb, bs, _ = lefts[0].shape
    own = totals is None
    bpr = chunks[0][0].shape[1] if own else HALVES * chunks[0][0].shape[1] // bs
    width = bpr * bs // HALVES
    products = lpb * bpr
    turns = sorted({what[0] for _, _, both in chunks for what in both if what is not None})
    if own:
        touched = list(range(3))
    else:
        touched = {sum_of(what[1]) for _, _, both in chunks for what in both if what is not None}
        touched = sorted(touched | set(finish or ()))
    sides = [(c, side) for c in range(len(chunks)) for side in range(2) if chunks[c][2][side] is not None]
    sides = [(c, side) for c, side in sides if side == 0 or chunks[c][2][0] != chunks[c][2][1]]

    def kernel(info_ref, *refs):
        place_refs = dict(zip(turns, refs))
        refs = refs[len(turns):]
        left_refs = dict(zip(sides, refs))
        right_refs = refs[len(sides):len(sides) + len(chunks)]
        outs = refs[len(sides) + len(chunks) + (0 if own else len(touched)):]
        total_refs = dict(zip(touched, outs))
        outs = outs[len(touched):]
        outs[0][...] = jnp.zeros_like(outs[0])
        odd = info_ref[0]
        if own:
            for ref in total_refs.values():
                ref[...] = jnp.zeros_like(ref)

        def products_of(left, right):
            left = left.reshape(lpb * bs, bs)
            left_high = left.astype(bf16)
            left_low = (left - left_high.astype(f32)).astype(bf16)
            high = right.astype(bf16)
            low = (right - high.astype(f32)).astype(bf16)
            return jnp.dot(
                jnp.concatenate([left_high, left_low, left_high], axis=1),
                jnp.concatenate([high, high, low], axis=0),
                preferred_element_type=f32,
            )

        def add_own(left_ref, right_ref):
            parts = (slice(0, bs // 2), slice(bs // 2, 3 * bs // 4), slice(3 * bs // 4, bs))
            for k in range(kb):
                out = products_of(left_ref[0, k], jnp.concatenate([right_ref[k, b] for b in range(bpr)], axis=1))
                for a in range(lpb):
                    for b in range(bpr):
                        n = place_refs[0][k * products + a * bpr + b]
                        block = out[a * bs:(a + 1) * bs, b * bs:(b + 1) * bs]
                        for ref, lanes in zip(total_refs.values(), parts):
                            ref[n, :, lanes] += block[:, lanes]

        def add(c, side):
            turn, quarter = chunks[c][2][side][:2]
            start, count = block_rows(kb, *chunks[c][2][side][1:])
            left_ref, right_ref, total_ref = left_refs[c, side], right_refs[c], total_refs[sum_of(quarter)]
            lanes = bs // 2 if quarter < 2 else bs // 4
            for k in range(count):
                if quarter < 2:
                    right = right_ref[k * bs:(k + 1) * bs]
                else:
                    right = right_ref[k // 2 * bs:(k // 2 + 1) * bs, k % 2 * bs:(k % 2 + 1) * bs]
                out = products_of(left_ref[0, k], right)
                for a in range(lpb):
                    for b in range(bpr):
                        n = place_refs[turn][(start + k) * products + a * bpr + b]
                        at = b * lanes % bs
                        total_ref[n, :, at:at + lanes] += out[a * bs:(a + 1) * bs, b * lanes:(b + 1) * lanes]

        def pack(total_ref, ref, quarters):
            packed = ref.shape[0]
            group = lane_group((bs, bs))
            for p in range(packed):
                blocks = [total_ref[nc // 2 + g * packed + p] for g in range(4 if quarters else 2)]
                if not quarters:
                    ref[p] = fold_half(group, *blocks)
                    continue
                one = fold_half(group, blocks[0], blocks[2])
                two = fold_half(group, blocks[1], blocks[3])
                even = group % 2 == 0
                moved = jnp.where(even, two, one)
                ref[p] = jnp.where(even, one + move_lanes(moved, 3), two + move_lanes(moved, 1))

        if own:
            add_own(left_refs[0, 0], right_refs[0])
            return
        for c, (_, _, both) in enumerate(chunks):
            if both[0] == both[1]:
                add(c, 0)
                continue
            if both[0] is not None:
                pl.when(odd == 0)(lambda c=c: add(c, 0))
            if both[1] is not None:
                pl.when(odd != 0)(lambda c=c: add(c, 1))
        if finish is not None and finish[0] == finish[1]:
            pack(total_refs[finish[0]], outs[1], finish[0] > 0)
        elif finish is not None:
            pl.when(odd == 0)(lambda: pack(total_refs[finish[0]], outs[1], True))
            pl.when(odd != 0)(lambda: pack(total_refs[finish[1]], outs[1], True))

    def left_spec(turn, *what):
        start, count = block_rows(kb, *what)
        return pl.BlockSpec((1, count, lpb, bs, bs), lambda g, info_ref, *_: (info_ref[1 + turn], start // count, 0, 0, 0))

    def right_spec(array, at, both):
        parts = max(what[3] for what in both if what is not None)
        rows = kb // HALVES * bs // PARTS * parts
        return pl.BlockSpec((rows, width), lambda *_: (at, 0))

    operands = [lefts[chunks[c][2][side][0]] for c, side in sides] + [c[0] for c in chunks]
    if own:
        in_specs = [pl.BlockSpec((1, kb, lpb, bs, bs), lambda g, info_ref, *_: (info_ref[1], 0, 0, 0, 0)), whole(chunks[0][0].shape)]
    else:
        in_specs = [left_spec(*chunks[c][2][side]) for c, side in sides] + [right_spec(*chunk) for chunk in chunks]
    held = len(operands) + 1 + len(turns)
    if not own:
        operands += [totals[n] for n in touched]
        in_specs += [in_vmem] * len(touched)
    outs = [jax.ShapeDtypeStruct((nc + 1, bs, bs), f32)] * len(touched) + [jax.ShapeDtypeStruct((8, 128), jnp.int32)]
    if finish is not None:
        outs.append(jax.ShapeDtypeStruct((nc // (8 if finish[0] else 4), bs, bs), f32))
    parts = QUARTERS if own else len(chunks)
    per = kb // HALVES
    flops = parts * per * 2 * lpb * bs * 3 * bs * width
    moved = 4 * parts * per * (lpb * bs * bs + bs * width)
    results = pl.pallas_call(
        kernel,
        grid_spec=pltpu.PrefetchScalarGridSpec(
            num_scalar_prefetch=1 + len(turns),
            grid=(1,),
            in_specs=in_specs,
            out_specs=[in_vmem] * len(touched) + [whole(x.shape) for x in outs[len(touched):]],
        ),
        out_shape=outs,
        input_output_aliases={} if own else {held + n: n for n in range(len(touched))},
        compiler_params=pltpu.CompilerParams(vmem_limit_bytes=20 * 1024 * 1024),
        cost_estimate=pl.CostEstimate(flops=cost * flops, bytes_accessed=cost * moved, transcendentals=0),
        name="accumulate",
    )(info, *[places[turn] for turn in turns], *operands)
    totals = [None] * 3 if own else list(totals)
    for n, total in zip(touched, results):
        totals[n] = total
    return (totals, *results[len(touched):])


def own_places(info, slots, rows, cols, kb, lpb):
    nc = slots.shape[0]
    bpr = cols.shape[0]

    def kernel(info_ref, slots_ref, rows_ref, cols_ref, table_ref, out_ref):
        for code in range(CB * CB):
            table_ref[code] = nc
        behind = nc - nc // 2 * info_ref[1 + STEPS]
        for n in range(nc):
            table_ref[slots_ref[n]] = lax.rem(n + behind, nc)
        fill_places(info_ref[1], table_ref, rows_ref, lambda k, b: cols_ref[b, k], out_ref, kb, lpb, bpr)

    return pl.pallas_call(
        kernel,
        in_specs=[in_smem] * 4,
        out_specs=[in_smem] * 2,
        out_shape=[jax.ShapeDtypeStruct((CB * CB,), jnp.int32), jax.ShapeDtypeStruct((kb * lpb * bpr,), jnp.int32)],
        compiler_params=pltpu.CompilerParams(vmem_limit_bytes=1024 * 1024),
        name="own_places",
    )(info, slots, rows, cols)


def fill_places(panel, table_ref, rows_ref, col_of, out_ref, kb, lpb, bpr):
    def column(k, carry):
        cols = [col_of(k, b) for b in range(bpr)]
        for a in range(lpb):
            row = rows_ref[panel, a, k] * CB
            for b in range(bpr):
                out_ref[(k * lpb + a) * bpr + b] = table_ref[row + cols[b]]
        return carry

    lax.fori_loop(0, kb, column, 0)


def panel_places(info, table, turn, rows, even_part, odd_part, kb, lpb, bpr):
    parts = (even_part, odd_part)

    def kernel(info_ref, table_ref, rows_ref, even_ref, odd_ref, out_ref, cols_ref, scalar_ref, sem):
        cols = jnp.where(info_ref[0] == 0, even_ref[...], odd_ref[...])
        cols_ref[...] = cols.astype(jnp.int32)
        copy = pltpu.make_async_copy(cols_ref, scalar_ref, sem)
        copy.start()
        copy.wait()
        fill_places(info_ref[1 + turn], table_ref, rows_ref, lambda k, b: scalar_ref[b, k], out_ref, kb, lpb, bpr)

    return pl.pallas_call(
        kernel,
        grid=(1,),
        in_specs=[in_smem] * 3 + [pl.BlockSpec((kb, 128), lambda g, at=at: (at // kb, 0)) for _, at in parts],
        out_specs=in_smem,
        out_shape=jax.ShapeDtypeStruct((kb * lpb * bpr,), jnp.int32),
        scratch_shapes=[pltpu.VMEM((kb, 128), jnp.int32), pltpu.SMEM((kb, 128), jnp.int32), pltpu.SemaphoreType.DMA],
        compiler_params=pltpu.CompilerParams(vmem_limit_bytes=1024 * 1024),
        name="panel_places",
    )(info, table, rows, *[array for array, _ in parts])


def kept_blocks(totals, nc):
    bs = totals[0].shape[-1]

    def kernel(half_ref, third_ref, fourth_ref, out_ref):
        for n in range(nc // 2):
            half = half_ref[n]
            upper = [ref[n] + swap_lanes(ref[n]) for ref in (third_ref, fourth_ref)]
            half = half + swap_lanes(half)
            out_ref[n] = by_group([half, half, *(x + move_lanes(x, 1) for x in upper)])

    return pl.pallas_call(
        kernel,
        in_specs=[in_vmem] * 3,
        out_specs=in_vmem,
        out_shape=jax.ShapeDtypeStruct((nc // 2, bs, bs), f32),
        compiler_params=pltpu.CompilerParams(vmem_limit_bytes=8 * 1024 * 1024),
        cost_estimate=pl.CostEstimate(flops=0, bytes_accessed=0, transcendentals=0),
        name="kept_blocks",
    )(*totals)


def combine(info, kept, other):
    packed, bs, _ = other[0].shape
    packed_4 = other[1].shape[0]

    def kernel(info_ref, kept_ref, half_ref, early_ref, late_ref, out_ref):
        even = info_ref[0] == 0

        def step(first):
            for n in range(packed):
                p = first * packed + n
                low = half_ref[n] if first == 0 else swap_lanes(half_ref[n])
                early, late = early_ref[p % packed_4], late_ref[p % packed_4]
                group = p // packed_4
                third = move_lanes(jnp.where(even, late, early), 2 - group)
                fourth = move_lanes(jnp.where(even, early, late), 3 - group)
                out_ref[n] = kept_ref[p] + by_group([low, low, third, fourth])

        for first in range(2):
            pl.when(pl.program_id(0) == first)(lambda first=first: step(first))

    return pl.pallas_call(
        kernel,
        grid=(2,),
        in_specs=[in_smem] + [in_vmem] * 4,
        out_specs=pl.BlockSpec((packed, bs, bs), lambda g: (g, 0, 0)),
        out_shape=jax.ShapeDtypeStruct((2 * packed, bs, bs), f32),
        compiler_params=pltpu.CompilerParams(vmem_limit_bytes=8 * 1024 * 1024),
        name="combine",
    )(info, kept, *other)


def shards(left_values, left_rows, right_values, right_cols, result_slots):
    rows_n, cols_n = (lax.axis_size(a) for a in ("row", "col"))
    row, col, rep = (lax.axis_index(a) for a in ("row", "col", "rep"))
    panels = left_values[0, 0, 0]
    panel_rows = jnp.swapaxes(left_rows[0, 0, 0], 1, 2)
    right = right_values[0, 0, 0]
    cols = jnp.swapaxes(right_cols[0, 0, 0], 0, 1)
    slots = result_slots[0, 0]
    kb = right.shape[0]
    nc = slots.shape[0]
    place = [(col + turn) // cols_n for turn in range(STEPS)]
    info = jnp.stack([row % 2, *place, rep]).astype(jnp.int32)

    z_pairs = [(r, (r - 2) % rows_n) for r in range(rows_n)]
    x_pairs = [(r, r ^ 1) for r in range(rows_n)]

    def along_z(chunk):
        return lax.ppermute(chunk, "row", z_pairs)

    def along_x(chunk):
        return lax.ppermute(chunk, "row", x_pairs)

    rows, width = quarter_shape(right)
    def sent(even_parts, odd_parts, *others, extra=False):
        return pick(info, right, cols if extra else None, even_parts, odd_parts, *others)

    def all_of(array):
        return [(array, 0, PARTS)]

    def own_all(quarter):
        return [(None, quarter, 0, PARTS)]

    z = {}
    x = {}
    def own_part(quarter, first=0, parts=PARTS):
        return (quarter, first, parts)

    small = (info,)
    first = first_quarter(right, cols, *small)
    z[1] = along_z(first)
    sent_panels, _ = lax.optimization_barrier((panels, first))
    x[1] = along_x(own_quarters(right, [own_part(3), own_part(2, 0, 1)], None, *small))

    shifts = sorted({turn % cols_n for turn in range(STEPS)})
    held = {
        shift: (panels, panel_rows) if shift == 0 else lax.ppermute((sent_panels, panel_rows), "col", [(c, (c - shift) % cols_n) for c in range(cols_n)])
        for shift in shifts
    }
    lefts = [held[turn % cols_n][0] for turn in range(STEPS)]
    rows_at = [held[turn % cols_n][1] for turn in range(STEPS)]

    lpb, bpr = panels.shape[2], right.shape[1]
    places = {}
    table, places[0] = own_places(info, slots, panel_rows, cols, kb, lpb)

    def read_places(turn, even_part, odd_part):
        places[turn] = panel_places(info, table, turn, rows_at[turn], even_part, odd_part, kb, lpb, bpr)

    def add(totals, chunks, finish=None, cost=1):
        return accumulate(info, places, lefts, chunks, totals, nc, finish, cost)

    def along_z_part(stage):
        return (z[stage], 0, Z_CHUNKS[stage])

    def along_x_part(stage):
        if stage == 2:
            return (x[1], PARTS, X_CHUNKS[stage])
        if stage == 8:
            return (x[7], 1, X_CHUNKS[stage])
        return (x[stage], 0, X_CHUNKS[stage])

    totals, done = accumulate(info, places, [panels] * STEPS, [(right, 0, ((0, 0), (0, 0)))], None, nc)
    second = own_quarters(right, [own_part(1)], None, done)
    z[2] = along_z(second)
    x[3] = along_x(sent(all_of(z[1]), own_all(0), done, extra=True))
    z[3] = along_z(own_quarters(right, [own_part(2)], None, z[1], x[1], done))
    read_places(2, (z[1], rows), (z[1], rows))
    totals, done = add(totals, [along_z_part(1), along_z_part(2)])
    x[4] = along_x(sent(all_of(z[2]), own_all(1), done))
    z[4] = along_z(sent(own_all(3), all_of(x[3]), done, extra=True))
    read_places(1, (x[3], rows), (x[3], rows))
    totals, done = add(totals, [along_x_part(1), along_x_part(2), along_x_part(3)])
    x[5] = along_x(sent(all_of(z[3]), all_of(z[1]), done, extra=True))
    z[5] = along_z(sent(all_of(x[1]), all_of(x[4]), done))
    totals, done = add(totals, [along_z_part(3), along_x_part(4)])
    x[6] = along_x(sent(all_of(z[4]), all_of(z[2]), done))
    z[6] = along_z(sent([(x[1], PARTS, 1)], all_of(x[5]), done))
    read_places(3, (x[5], rows), (z[4], rows))
    totals, done = add(totals, [along_z_part(4), along_x_part(5)])
    x[7] = along_x(sent(all_of(z[5]), [(z[3], 1, 1), (None, 2, 1, 1)], done))
    totals, done = add(totals, [along_z_part(5)])
    z[7] = along_z(sent(all_of(x[6]), all_of(x[6]), done))

    def to_partner(blocks):
        return lax.ppermute(blocks, "rep", [(0, 1), (1, 0)])

    totals, done, send_0 = add(totals, [along_x_part(6)], (0, 0))
    other_0 = to_partner(send_0)
    totals, done, send_1 = add(totals, [along_z_part(6)], (2, 1))
    other_1 = to_partner(send_1)
    totals, done = add(totals, [along_x_part(7), along_x_part(8)], cost=0)
    totals, done, send_2 = add(totals, [along_z_part(7)], (1, 2), 0)
    other_2 = to_partner(send_2)
    return combine(info, kept_blocks(totals, nc), [other_0, other_1, other_2])[None, None]


def solution(mesh):
    in_specs = (
        P("row", "rep", "col", None, None, None, None, None),
        P("row", "rep", "col", None, None, None),
        P("rep", "row", "col", None, None, None, None),
        P("rep", "row", "col", None, None),
        P("row", "col", None),
    )
    out_specs = P("row", "col", "rep", None, None)
    return jax.shard_map(shards, mesh=mesh, in_specs=in_specs, out_specs=out_specs, check_vma=False)
```
